128 devices in a mesh: ctx: 16 (over y_lo, x, core), tp: 8 (over y_hi, z).
Axes of the slice: x: 4, y: 4 (y_hi: 2, y_lo: 2; y = y_hi * 2 + y_lo), z: 4, core: 2. Of those that a mesh axis runs over, the one named last changes fastest.
Arguments:
- query_rows: bfloat16 [8192, 7168], P('ctx', 'tp'), may hold values from -32 to 32
- key_rows: bfloat16 [8192, 7168], P('ctx', 'tp'), may hold values from -32 to 32
- value_rows: bfloat16 [8192, 7168], P('ctx', 'tp'), may hold values from -6 to 6
- ssm_inputs: bfloat16 [8192, 7168], P('ctx', 'tp'), may hold values from -6 to 6
- ssm_gate: bfloat16 [8192, 7168], P('ctx', 'tp'), may hold values from -20 to 20
- write_vecs: bfloat16 [8192, 64], P('ctx'), may hold values from -0.75 to 0.75
- read_vecs: bfloat16 [8192, 64], P('ctx'), may hold values from -0.75 to 0.75
- step_raw: float32 [8192, 112], P('ctx', 'tp'), may hold values from -4 to 4
- decay_log: float32 [112], P('tp'), may hold values from -12 to -3
- skip_gain: float32 [112], P('tp'), may hold values from 0.5 to 2.5
- norm_gain: float32 [7168], P('tp'), may hold values from 0.1 to 1.9
Outputs:
- attention_out: bfloat16 [8192, 7168], P('ctx', 'tp')
- mixer_out: bfloat16 [8192, 7168], P('ctx', 'tp')
The draws below stay inside these ranges and needn't reach their ends.
All inputs are finite; a program needn't handle non-finite values.
Results may differ from the reference program's by a relative error of at most 0.014.
Values may be sent and summed in bfloat16 or wider, within the bound.
No kernel may reach another device: no remote copies, remote signals or barrier semaphores. Data moves between devices by JAX's collectives and lax.ppermute only.
A program may use at most 256 MiB of HBM per device.

```python
import jax
import jax.numpy as jnp
from jax import lax

ATT_HEADS = 32
ATT_DIM = 224
SSM_HEADS = 112
SSM_DIM = 64
STATE_DIM = 64
BLOCK_LEN = 256
SEQ_LEN = 8192
ATT_WIDTH = 7168
SSM_WIDTH = 7168


def draw_pair(key):
    first_key, second_key = jax.random.split(key)
    query_base = jax.random.normal(first_key, (SEQ_LEN, ATT_WIDTH), jnp.float32)
    key_base = jax.random.normal(second_key, (SEQ_LEN, ATT_WIDTH), jnp.float32)
    return (query_base, key_base)


def draw_query_rows(key, part):
    query_base, key_base = draw_pair(key)
    result = query_base
    return result.astype(jnp.bfloat16)


def draw_key_rows(key, part):
    query_base, key_base = draw_pair(key)
    result = key_base
    return result.astype(jnp.bfloat16)


def draw_ssm_gate(key, part):
    key = jax.random.fold_in(key, 13)
    first_key = jax.random.fold_in(key, 0)
    column_scale = jnp.exp(jnp.linspace(jnp.log(0.5), jnp.log(2.0), SSM_WIDTH)).astype(jnp.float32)[None, :]
    result = jax.random.normal(first_key, (SEQ_LEN, SSM_WIDTH), jnp.float32) * column_scale
    return jnp.clip(result, -20.0, 20.0).astype(jnp.bfloat16)


def draw_step_raw(key, part):
    key = jax.random.fold_in(key, 14)
    first_key, second_key = jax.random.split(key)
    offsets = jax.random.uniform(second_key, (SEQ_LEN // BLOCK_LEN, 1), jnp.float32, -3.0, 2.5)
    shift = jnp.repeat(offsets, BLOCK_LEN, axis=0)
    result = 0.3 + 0.6 * jax.random.normal(first_key, (SEQ_LEN, SSM_HEADS), jnp.float32) + shift
    return jnp.clip(result, -4.0, 4.0)


def rates_for(key, fast_share):
    first_key, second_key, third_key = jax.random.split(key, 3)
    pick = jax.random.uniform(first_key, (SSM_HEADS,), jnp.float32)
    fast_rate = jnp.exp(jax.random.uniform(second_key, (SSM_HEADS,), jnp.float32, jnp.log(1.0 / 50.0), jnp.log(1.0 / 30.0))) / 0.9
    slow_rate = jnp.exp(jax.random.uniform(third_key, (SSM_HEADS,), jnp.float32, jnp.log(0.3), jnp.log(2.0))) / (0.9 * SEQ_LEN)
    return jnp.log(jnp.where(pick < fast_share, fast_rate, slow_rate))


def draw_decay_log(key, part):
    key = jax.random.fold_in(key, 15)
    result = rates_for(key, 0.4)
    return jnp.clip(result, -12.0, -3.0)


def levels(stream_key, dims, shards, least, largest):
    gain = 1.0
    for dim, parts in shards:
        draws = jax.random.uniform(jax.random.fold_in(jax.random.fold_in(stream_key, 6), dim), (parts,), jnp.float32, least / len(shards), largest / len(shards))
        gain = gain * jnp.repeat(jnp.exp(draws), dims[dim] // parts).reshape((-1,) + (1,) * (len(dims) - 1 - dim))
    return gain


def scatter_about(key, extent, deviation, reach, cuts=(), kind=jnp.bfloat16):
    loudness = levels(key, extent, cuts, -0.22, 0.18) if cuts else 1.0
    values = jax.random.normal(key, extent, jnp.float32) * deviation * loudness
    return jnp.minimum(jnp.maximum(values, -reach), reach).astype(kind)


def setup_inputs(seed: int = 0) -> dict:
    streams_of = jax.random.split(jax.random.key(seed), 12)
    return {
        "query_rows": draw_query_rows(jax.random.fold_in(streams_of[11], 71), 0),
        "key_rows": draw_key_rows(jax.random.fold_in(streams_of[11], 71), 0),
        "value_rows": scatter_about(streams_of[2], (SEQ_LEN, ATT_WIDTH), 1.0, 6.0, ((0, 16), (1, 8))),
        "ssm_inputs": scatter_about(streams_of[3], (SEQ_LEN, SSM_WIDTH), 1.0, 6.0, ((0, 16), (1, 8))),
        "ssm_gate": draw_ssm_gate(jax.random.fold_in(streams_of[11], 71), 0),
        "write_vecs": scatter_about(streams_of[5], (SEQ_LEN, STATE_DIM), STATE_DIM ** -0.5, 0.75, ((0, 16),)),
        "read_vecs": scatter_about(streams_of[6], (SEQ_LEN, STATE_DIM), STATE_DIM ** -0.5, 0.75, ((0, 16),)),
        "step_raw": draw_step_raw(jax.random.fold_in(streams_of[11], 71), 0),
        "decay_log": draw_decay_log(jax.random.fold_in(streams_of[11], 71), 0),
        "skip_gain": jnp.clip(0.5 + 2.0 * jax.random.uniform(streams_of[9], (SSM_HEADS,), jnp.float32) ** levels(streams_of[9], (SSM_HEADS,), ((0, 8),), -0.2, 0.2), 0.5, 2.5),
        "norm_gain": jnp.clip(1.0 + 0.18 * jax.random.normal(streams_of[10], (SSM_WIDTH,), jnp.float32), 0.1, 1.9),
    }


def attention_head(operands):
    query_head, key_head, value_head = operands
    scale = ATT_DIM ** (-0.5)
    columns = jnp.arange(SEQ_LEN, dtype=jnp.int32)[None, :]

    def one_block(index):
        first = (index * BLOCK_LEN).astype(jnp.int32)
        query_block = lax.dynamic_slice_in_dim(query_head, first, BLOCK_LEN, 0)
        scores = jnp.dot(query_block, key_head.T, preferred_element_type=jnp.float32) * scale
        rows_pos = first + jnp.arange(BLOCK_LEN, dtype=jnp.int32)[:, None]
        visible = columns <= rows_pos
        scores = jnp.where(visible, scores, -1e+30)
        top = lax.optimization_barrier(jnp.max(scores, axis=1, keepdims=True))
        probs = jnp.where(visible, jnp.exp(scores - top), 0.0)
        total = lax.optimization_barrier(jnp.sum(probs, axis=1, keepdims=True))
        mixed = jnp.dot(probs.astype(jnp.bfloat16), value_head, preferred_element_type=jnp.float32)
        return (mixed / total).astype(jnp.bfloat16)
    return lax.map(one_block, jnp.arange(SEQ_LEN // BLOCK_LEN, dtype=jnp.int32))

def block_pass(state, block):
    inputs, write_f, read_f, step, log_decay = block
    high = lax.Precision.HIGHEST
    cumul = jnp.cumsum(log_decay, axis=0)
    lower = jnp.tril(jnp.ones((BLOCK_LEN, BLOCK_LEN), dtype=bool))[:, :, None]
    spread = cumul[:, None, :] - cumul[None, :, :]
    decay = jnp.where(lower, jnp.exp(jnp.where(lower, spread, 0.0)), 0.0)
    intersection = jnp.dot(read_f, write_f.T, precision=high)
    weights = decay * intersection[:, :, None] * step[None, :, :]
    inner = jnp.einsum('tsh,shp->thp', weights, inputs, precision=high)
    carried = jnp.einsum('tn,hpn->thp', read_f, state, precision=high) * jnp.exp(cumul)[:, :, None]
    tail = jnp.exp(cumul[-1][None, :] - cumul) * step
    weighted = inputs * tail[:, :, None]
    new_state = jnp.exp(cumul[-1])[:, None, None] * state + jnp.einsum('shp,sn->hpn', weighted, write_f, precision=high)
    return (new_state, inner + carried)

def reference(query_rows, key_rows, value_rows, ssm_inputs, ssm_gate, write_vecs, read_vecs, step_raw, decay_log, skip_gain, norm_gain):

    def by_head(rows):
        return rows.reshape(SEQ_LEN, ATT_HEADS, ATT_DIM).transpose(1, 0, 2)
    heads_out = lax.map(attention_head, (by_head(query_rows), by_head(key_rows), by_head(value_rows)))
    attention_out = heads_out.reshape(ATT_HEADS, SEQ_LEN, ATT_DIM).transpose(1, 0, 2).reshape(SEQ_LEN, ATT_WIDTH)
    inputs = ssm_inputs.astype(jnp.float32).reshape(SEQ_LEN, SSM_HEADS, SSM_DIM)
    write_f = write_vecs.astype(jnp.float32)
    read_f = read_vecs.astype(jnp.float32)
    step = jax.nn.softplus(step_raw)
    log_decay = -jnp.exp(decay_log)[None, :] * step
    blocks = SEQ_LEN // BLOCK_LEN

    def split(array):
        return array.reshape((blocks, BLOCK_LEN) + array.shape[1:])
    start_state = jnp.zeros((SSM_HEADS, SSM_DIM, STATE_DIM), jnp.float32)
    final_state, outputs = lax.scan(block_pass, start_state, (split(inputs), split(write_f), split(read_f), split(step), split(log_decay)))
    outputs = outputs.reshape(SEQ_LEN, SSM_HEADS, SSM_DIM)
    mixed = outputs + skip_gain[None, :, None] * inputs
    gated = mixed.reshape(SEQ_LEN, SSM_WIDTH) * jax.nn.silu(ssm_gate.astype(jnp.float32))
    square_mean = lax.optimization_barrier(jnp.mean(gated * gated, axis=1))
    mixer_out = (gated * lax.rsqrt(square_mean + 1e-05)[:, None] * norm_gain[None, :]).astype(jnp.bfloat16)
    return (attention_out, mixer_out)
```

```python
import math

import jax
import jax.numpy as jnp
from jax import lax
from jax.experimental import pallas as pl
from jax.experimental.pallas import tpu as pltpu
from jax.sharding import PartitionSpec as P

ATT_DIM = 224
SSM_DIM = 64
STATE_DIM = 64
SSM_WIDTH = 7168
TOK = 512
HEADS = 4
CTX = 16
HALF = 256
LOG2E = math.log2(math.e)
F32 = jnp.float32
BF16 = jnp.bfloat16


def exchanged(i, r):
    y, x, c = i >> 3, (i >> 1) & 3, i & 1
    if r & 1:
        x = 3 - x
    if r & 2:
        y = 1 - y
    return y * 8 + x * 2 + c


def head_swap(value, r):
    return lax.ppermute(value, "ctx", [(i, exchanged(i, r)) for i in range(CTX)])


def class_swap(value):
    return lax.ppermute(value, "ctx", [(i, i ^ 2) for i in range(CTX)])


def core_swap(value):
    return lax.ppermute(value, "ctx", [(i, i ^ 1) for i in range(CTX)])


def head_rows(head):
    return pl.ds(pl.multiple_of(head * ATT_DIM, 16), ATT_DIM)


def pack_kernel(info, q_ref, k_ref, v_ref, *refs):
    q_out, kv_out, (qs, ks, vs) = refs[:4], refs[4:8], refs[8:]
    qs[...] = q_ref[...].T
    ks[...] = k_ref[...].T
    vs[...] = v_ref[...].T
    for r in range(4):
        rows = head_rows(info[0] ^ r)
        q_out[r][...] = qs[rows, :]
        kv_out[r][0:ATT_DIM, :] = ks[rows, :]
        kv_out[r][ATT_DIM : 2 * ATT_DIM, :] = vs[rows, :]


def unpack_kernel(info, *refs):
    pieces, out_ref, rows_ref = refs[:4], refs[4], refs[5]
    for r in range(4):
        rows_ref[head_rows(info[0] ^ r), :] = pieces[r][...]
    out_ref[...] = rows_ref[...].T


def token_block(chip, kind, core):
    return (chip >> 1) * 8 + (kind + (chip & 1) * (3 - 2 * kind)) * 2 + core


def attend_kernel(info, *refs):
    q_in, kv_in, o_out = refs[:4], refs[4:20], refs[20:24]
    qs, ks, vs, os, acc = refs[24:]
    hid, kind, core = info[0], info[1], info[2]
    scale = ATT_DIM ** (-0.5) * LOG2E

    for cl in range(2):
        for co in range(2):
            for r in range(4):
                piece = kv_in[(cl * 2 + co) * 4 + r]
                block = token_block(hid ^ r, kind ^ cl, core ^ co)
                ks[pl.ds(pl.multiple_of(block * TOK, TOK), TOK), :] = piece[0:ATT_DIM, :].T
                lanes = pl.ds(pl.multiple_of((block & 1) * TOK, TOK), TOK)
                vs[block >> 1, :, lanes] = piece[ATT_DIM : 2 * ATT_DIM, :]
    for r in range(4):
        qs[r] = q_in[r][...]

    def one_queries(r, carry):
        block = token_block(hid ^ r, kind, core)
        acc[...] = jnp.zeros_like(acc)

        def visit(keys, values, stats, masked):
            new_stats = []
            for half in range(2):
                top, total = stats[half]
                lanes = slice(half * HALF, (half + 1) * HALF)
                s = jnp.dot(keys, qs[r, :, lanes], preferred_element_type=F32)
                if masked:
                    k_pos = lax.broadcasted_iota(jnp.int32, s.shape, 0)
                    q_pos = lax.broadcasted_iota(jnp.int32, s.shape, 1) + half * HALF
                    s = jnp.where(k_pos <= q_pos, s, -1e30)
                new_top = jnp.maximum(top, jnp.max(s, axis=0, keepdims=True))
                p = jnp.exp2((s - new_top) * scale)
                shrink = jnp.exp2((top - new_top) * scale)
                total = total * shrink + jnp.sum(p, axis=0, keepdims=True)
                acc[:, lanes] = acc[:, lanes] * shrink + jnp.dot(
                    values, p.astype(BF16), preferred_element_type=F32
                )
                new_stats.append((new_top, total))
            return tuple(new_stats)

        def chip_block(j, stats):
            rows = pl.ds(pl.multiple_of(j * 2 * TOK, 2 * TOK), 2 * TOK)
            return visit(ks[rows, :], vs[j], stats, False)

        def core_block(j, stats, masked):
            rows = pl.ds(pl.multiple_of(j * TOK, TOK), TOK)
            lanes = pl.ds(pl.multiple_of((j & 1) * TOK, TOK), TOK)
            return visit(ks[rows, :], vs[j >> 1, :, lanes], stats, masked)

        first = (jnp.full((1, HALF), -1e30, F32), jnp.zeros((1, HALF), F32))
        stats = lax.fori_loop(0, block >> 1, chip_block, (first, first))
        stats = lax.fori_loop(
            0, block & 1, lambda k, now: core_block(block - 1, now, False), stats
        )
        stats = core_block(block, stats, True)
        for half in range(2):
            lanes = slice(half * HALF, (half + 1) * HALF)
            os[r, :, lanes] = (acc[:, lanes] / stats[half][1]).astype(BF16)
        return carry

    lax.fori_loop(0, 4, one_queries, 0)
    for r in range(4):
        o_out[r][...] = os[r]


def pair_of(low, columns, h):
    return jnp.where(low, columns[:, h : h + 1], columns[:, h + 1 : h + 2])


def softplus(v):
    return jnp.maximum(v, 0.0) + jnp.log1p(jnp.exp(-jnp.abs(v)))


PAYLOAD = 80


def ssm_local_kernel(
    x_ref, write_ref, read_ref, step_ref, step_t_ref, rate_ref, rate_t_ref, gain_ref, out_ref, pay_ref, cum_ref
):
    heads = step_ref.shape[1]
    high = lax.Precision.HIGHEST
    row = lax.broadcasted_iota(jnp.int32, (TOK, TOK), 0)
    col = lax.broadcasted_iota(jnp.int32, (TOK, TOK), 1)
    step = softplus(step_ref[...])
    decay = -jnp.exp(rate_ref[...]) * step * LOG2E
    cum = jnp.dot(jnp.where(col <= row, 1.0, 0.0), decay, precision=high, preferred_element_type=F32)
    step_t = softplus(step_t_ref[...])
    decay_t = -jnp.exp(rate_t_ref[...]) * step_t * LOG2E
    cum_t = jnp.dot(decay_t, jnp.where(row <= col, 1.0, 0.0), precision=high, preferred_element_type=F32)
    key_row = jnp.log2(step_t) - cum_t
    cum_ref[...] = cum
    last = cum[TOK - 1 : TOK, :]
    tail = jnp.exp2(last - cum) * step

    near = lax.dot_general(
        read_ref[...], write_ref[...], (((1,), (1,)), ((), ())), preferred_element_type=F32
    )
    near = jnp.where(col <= row, near, 0.0)
    low = lax.broadcasted_iota(jnp.int32, (1, 128), 1) < SSM_DIM
    for h in range(0, heads, 2):
        lanes = slice(h * SSM_DIM, (h + 2) * SSM_DIM)
        x_pair = x_ref[:, lanes]
        x_f = x_pair.astype(F32)
        weighted = (x_f * pair_of(low, tail, h)).astype(BF16)
        pay_ref[0:STATE_DIM, lanes] = lax.dot_general(
            write_ref[...], weighted, (((0,), (0,)), ((), ())), preferred_element_type=F32
        ).astype(BF16)
        span = pair_of(low, last, h)
        span_high = span.astype(BF16)
        span_low = (span - span_high.astype(F32)).astype(BF16)
        pay_ref[STATE_DIM : STATE_DIM + 8, lanes] = jnp.broadcast_to(span_high, (8, 128))
        pay_ref[STATE_DIM + 8 : PAYLOAD, lanes] = jnp.broadcast_to(span_low, (8, 128))
        for t in range(2):
            t_rows = slice(t * HALF, (t + 1) * HALF)
            both = []
            for k in range(2):
                total = None
                for s in range(t + 1):
                    s_rows = slice(s * HALF, (s + 1) * HALF)
                    weights = (
                        jnp.exp2(cum[t_rows, h + k : h + k + 1] + key_row[h + k : h + k + 1, s_rows])
                        * near[t_rows, s_rows]
                    )
                    part = jnp.dot(weights.astype(BF16), x_pair[s_rows, :], preferred_element_type=F32)
                    total = part if total is None else total + part
                both.append(total)
            out_ref[t_rows, lanes] = (
                jnp.where(low, both[0], both[1]) + gain_ref[:, lanes] * x_f[t_rows, :]
            )


def ssm_carry_kernel(info, pay_ref, mixed_ref, cum_ref, read_ref, gate_ref, gated_ref, square_ref):
    heads = cum_ref.shape[1]

    def lap(k, state):
        block = pay_ref[k]
        span = (block[STATE_DIM : STATE_DIM + 8, :].astype(F32) + block[STATE_DIM + 8 : PAYLOAD, :].astype(F32))[0:1, :]
        return state * jnp.exp2(span) + block[0:STATE_DIM, :].astype(F32)

    state = lax.fori_loop(0, info[3], lap, jnp.zeros((STATE_DIM, heads * SSM_DIM), F32))
    state_high = state.astype(BF16)
    state_low = (state - state_high.astype(F32)).astype(BF16)
    reach = jnp.exp2(cum_ref[...])
    low = lax.broadcasted_iota(jnp.int32, (1, 128), 1) < SSM_DIM
    squares = jnp.zeros((TOK, 128), F32)
    for h in range(0, heads, 2):
        lanes = slice(h * SSM_DIM, (h + 2) * SSM_DIM)
        carried = jnp.dot(read_ref[...], state_high[:, lanes], preferred_element_type=F32) + jnp.dot(
            read_ref[...], state_low[:, lanes], preferred_element_type=F32
        )
        mixed = mixed_ref[:, lanes] + carried * pair_of(low, reach, h)
        gate = gate_ref[:, lanes].astype(F32)
        gated = mixed * (gate / (1.0 + jnp.exp(-gate)))
        gated_ref[:, lanes] = gated
        squares = squares + gated * gated
    square_ref[...] = jnp.sum(squares, axis=1, keepdims=True)


def vmem(count):
    return [pl.BlockSpec(memory_space=pltpu.VMEM)] * count


SMEM = pl.BlockSpec(memory_space=pltpu.SMEM)


def params(mib):
    return pltpu.CompilerParams(vmem_limit_bytes=mib * 1024 * 1024)


def shape(dims, kind):
    return jax.ShapeDtypeStruct(dims, kind)


def attention_part(info, query_rows, key_rows, value_rows):
    width = HEADS * ATT_DIM
    packed = pl.pallas_call(
        pack_kernel,
        out_shape=[shape((ATT_DIM, TOK), BF16)] * 4 + [shape((2 * ATT_DIM, TOK), BF16)] * 4,
        in_specs=[SMEM] + vmem(3),
        out_specs=vmem(8),
        scratch_shapes=[pltpu.VMEM((width, TOK), BF16)] * 3,
        compiler_params=params(40),
    )(info, query_rows, key_rows, value_rows)
    q_own, kv_own = packed[:4], packed[4:]
    kv_here = [kv_own[0]] + [head_swap(kv_own[r], r) for r in range(1, 4)]
    q_here = [q_own[0]] + [head_swap(q_own[r], r) for r in range(1, 4)]
    kv_there = [class_swap(piece) for piece in kv_here]
    kv_here_core = [core_swap(piece) for piece in kv_here]
    kv_there_core = [core_swap(piece) for piece in kv_there]
    results = pl.pallas_call(
        attend_kernel,
        out_shape=[shape((ATT_DIM, TOK), BF16)] * 4,
        in_specs=[SMEM] + vmem(20),
        out_specs=vmem(4),
        scratch_shapes=[
            pltpu.VMEM((4, ATT_DIM, TOK), BF16),
            pltpu.VMEM((CTX * TOK, ATT_DIM), BF16),
            pltpu.VMEM((CTX // 2, ATT_DIM, 2 * TOK), BF16),
            pltpu.VMEM((4, ATT_DIM, TOK), BF16),
            pltpu.VMEM((ATT_DIM, TOK), F32),
        ],
        compiler_params=params(56),
    )(info, *q_here, *kv_here, *kv_here_core, *kv_there, *kv_there_core)
    back = [results[0]] + [head_swap(results[r], r) for r in range(1, 4)]
    return pl.pallas_call(
        unpack_kernel,
        out_shape=shape((TOK, width), BF16),
        in_specs=[SMEM] + vmem(4),
        out_specs=vmem(1)[0],
        scratch_shapes=[pltpu.VMEM((width, TOK), BF16)],
        compiler_params=params(40),
    )(info, *back)


def mixer_part(
    info, ssm_inputs, ssm_gate, write_vecs, read_vecs, step_raw, decay_log, skip_gain, norm_gain
):
    tokens, width = ssm_inputs.shape
    heads = decay_log.shape[0]
    gain = jnp.repeat(skip_gain, SSM_DIM)[None, :]
    mixed, payload, cum = pl.pallas_call(
        ssm_local_kernel,
        out_shape=[
            shape((tokens, width), F32),
            shape((PAYLOAD, width), BF16),
            shape((tokens, heads), F32),
        ],
        in_specs=vmem(8),
        out_specs=vmem(3),
        compiler_params=params(40),
    )(ssm_inputs, write_vecs, read_vecs, step_raw, step_raw.T, decay_log[None, :], decay_log[:, None], gain)
    everything = lax.all_gather(payload, "ctx")
    gated, squares = pl.pallas_call(
        ssm_carry_kernel,
        out_shape=[shape((tokens, width), F32), shape((tokens, 1), F32)],
        in_specs=[SMEM] + vmem(5),
        out_specs=vmem(2),
        compiler_params=params(40),
    )(info, everything, mixed, cum, read_vecs, ssm_gate)
    squares = squares.reshape(tokens // 128, 128)
    count = lax.axis_size("tp")
    total = squares
    for d in range(1, count):
        total = total + lax.ppermute(squares, "tp", [(i, i ^ d) for i in range(count)])
    factor = lax.rsqrt(total.reshape(tokens) / SSM_WIDTH + 1e-05)
    return (gated * factor[:, None] * norm_gain[None, :]).astype(BF16)


def on_device(
    query_rows,
    key_rows,
    value_rows,
    ssm_inputs,
    ssm_gate,
    write_vecs,
    read_vecs,
    step_raw,
    decay_log,
    skip_gain,
    norm_gain,
):
    me = lax.axis_index("ctx")
    y, x, core = me >> 3, (me >> 1) & 3, me & 1
    info = jnp.stack([y * 2 + (x >> 1), (x ^ (x >> 1)) & 1, core, me]).astype(jnp.int32)
    mixer_out = mixer_part(
        info, ssm_inputs, ssm_gate, write_vecs, read_vecs, step_raw, decay_log, skip_gain, norm_gain
    )
    attention_out = attention_part(info, query_rows, key_rows, value_rows)
    return (attention_out, mixer_out)


def solution(mesh):
    placed = (
        P("ctx", "tp"),
        P("ctx", "tp"),
        P("ctx", "tp"),
        P("ctx", "tp"),
        P("ctx", "tp"),
        P("ctx", None),
        P("ctx", None),
        P("ctx", "tp"),
        P("tp"),
        P("tp"),
        P("tp"),
    )
    return jax.shard_map(
        on_device,
        mesh=mesh,
        in_specs=placed,
        out_specs=(P("ctx", "tp"), P("ctx", "tp")),
        check_vma=False,
    )
```

```python
import functools
import math

import jax
import jax.numpy as jnp
from jax import lax
from jax.experimental import pallas as pl
from jax.experimental.pallas import tpu as pltpu
from jax.sharding import PartitionSpec as P

ATT_DIM = 224
SSM_DIM = 64
STATE_DIM = 64
SSM_WIDTH = 7168
TOK = 512
HEADS = 4
CTX = 16
HALF = 256
LOG2E = math.log2(math.e)
F32 = jnp.float32
BF16 = jnp.bfloat16


def exchanged(i, r):
    y, x, c = i >> 3, (i >> 1) & 3, i & 1
    if r & 1:
        x = 3 - x
    if r & 2:
        y = 1 - y
    return y * 8 + x * 2 + c


def head_swap(value, r):
    return lax.ppermute(value, "ctx", [(i, exchanged(i, r)) for i in range(CTX)])


def class_swap(value):
    return lax.ppermute(value, "ctx", [(i, i ^ 2) for i in range(CTX)])


def core_swap(value):
    return lax.ppermute(value, "ctx", [(i, i ^ 1) for i in range(CTX)])


def block_swap(value, step):
    return lax.ppermute(value, "ctx", [(i, i ^ step) for i in range(CTX)])


def head_rows(head):
    return pl.ds(pl.multiple_of(head * ATT_DIM, 16), ATT_DIM)


Q_ROWS = slice(0, ATT_DIM)
K_ROWS = slice(ATT_DIM, 2 * ATT_DIM)
V_ROWS = slice(2 * ATT_DIM, 3 * ATT_DIM)


def pack_kernel(info, q_in, k_in, v_in, q_own, kv_own, all_1, all_2, all_3, raw, rows_ref, sems):
    copies = [pltpu.make_async_copy(src, raw.at[i], sems.at[i]) for i, src in enumerate((q_in, k_in, v_in))]
    for copy in copies:
        copy.start()
    for i, (out, first) in enumerate(((q_own, 0), (kv_own, 0), (kv_own, ATT_DIM))):
        copies[i].wait()
        rows_ref[i] = raw[i].T
        out[first : first + ATT_DIM, :] = rows_ref[i, head_rows(info[0]), :]
        for r, away in ((1, all_1), (2, all_2), (3, all_3)):
            away[i * ATT_DIM : (i + 1) * ATT_DIM, :] = rows_ref[i, head_rows(info[0] ^ r), :]


def unpack_kernel(info, *refs):
    pieces, out_ref, rows_ref = refs[:4], refs[4], refs[5]
    for r in range(4):
        rows_ref[head_rows(info[0] ^ r), :] = pieces[r][...]
    out_ref[...] = rows_ref[...].T


def attend_kernel(own, info, *refs):
    hid, kind, core = info[0], info[1], info[2]
    scale = ATT_DIM ** (-0.5) * LOG2E

    if own:
        queries, pieces, refs = refs[:4], refs[4:12], refs[12:]
        acc, stats_out, qs, mark, ks, vs = refs
        for r in range(4):
            qs[r] = queries[r][Q_ROWS, :]
        for i, piece in enumerate(pieces):
            k_first = ATT_DIM if i & 3 else 0
            v_first = k_first + ATT_DIM
            start = pl.multiple_of((core ^ (i >> 2)) * TOK, TOK)
            ks[hid ^ (i & 3), pl.ds(start, TOK), :] = piece[k_first:v_first, :].T
            vs[hid ^ (i & 3), :, pl.ds(start, TOK)] = piece[v_first : v_first + ATT_DIM, :]
    else:
        pieces, refs = refs[:8], refs[8:]
        _, queries, acc_in, stats_in, *o_out, mark, qs, ks, vs, raw, acc, os, sems = refs
        loads = [
            pltpu.make_async_copy(queries, qs, sems.at[16]),
            pltpu.make_async_copy(acc_in, acc, sems.at[17]),
        ]
        key_loads, value_loads = [], []
        for i, piece in enumerate(pieces):
            start = pl.multiple_of((core ^ (i >> 2)) * TOK, TOK)
            key_loads.append(pltpu.make_async_copy(piece.at[0:ATT_DIM, :], raw.at[i], sems.at[i]))
            value_loads.append(
                pltpu.make_async_copy(
                    piece.at[ATT_DIM : 2 * ATT_DIM, :],
                    vs.at[hid ^ (i & 3), :, pl.ds(start, TOK)],
                    sems.at[8 + i],
                )
            )
        for load in key_loads + loads + value_loads:
            load.start()
        for i, load in enumerate(key_loads):
            load.wait()
            start = pl.multiple_of((core ^ (i >> 2)) * TOK, TOK)
            ks[hid ^ (i & 3), pl.ds(start, TOK), :] = raw[i].T
        for load in loads + value_loads:
            load.wait()
    mark[...] = jnp.zeros_like(mark)

    def one_queries(r, carry):
        chip = hid ^ r

        def visit(keys, values, stats, masked):
            lanes = [slice(half * HALF, (half + 1) * HALF) for half in range(2)]
            scores = [
                jnp.dot(keys, qs[r, :, lanes[half]], preferred_element_type=F32) for half in range(2)
            ]
            new_stats, low, shrinks = [], [], []
            for half in range(2):
                (top, total), s = stats[half], scores[half]
                if masked:
                    k_pos = lax.broadcasted_iota(jnp.int32, s.shape, 0)
                    q_pos = lax.broadcasted_iota(jnp.int32, s.shape, 1) + half * HALF
                    s = jnp.where(k_pos <= q_pos, s, -1e30)
                new_top = jnp.maximum(top, jnp.max(s, axis=0, keepdims=True))
                p = jnp.exp2((s - new_top) * scale)
                shrink = jnp.exp2((top - new_top) * scale)
                total = total * shrink + jnp.sum(p, axis=0, keepdims=True)
                new_stats.append((new_top, total))
                low.append(p.astype(BF16))
                shrinks.append(shrink)
            for half in range(2):
                acc[r, :, lanes[half]] = acc[r, :, lanes[half]] * shrinks[half] + jnp.dot(
                    values, low[half], preferred_element_type=F32
                )
            return tuple(new_stats)

        def chip_block(j, stats):
            return visit(ks[j], vs[j], stats, False)

        def core_block(start, stats, masked):
            start = pl.multiple_of(start, TOK)
            return visit(
                ks[chip, pl.ds(start, TOK), :], vs[chip, :, pl.ds(start, TOK)], stats, masked
            )

        if own:
            acc[r] = jnp.zeros((ATT_DIM, TOK), F32)
            first = (jnp.full((1, HALF), -1e30, F32), jnp.zeros((1, HALF), F32))
            stats = lax.fori_loop(0, chip, chip_block, (first, first))
            stats = lax.fori_loop(0, core, lambda k, now: core_block(0, now, False), stats)
            stats = core_block(core * TOK, stats, True)
            for half in range(2):
                lanes = slice(half * HALF, (half + 1) * HALF)
                stats_out[r, 0:8, lanes] = jnp.broadcast_to(stats[half][0], (8, HALF))
                stats_out[r, 8:16, lanes] = jnp.broadcast_to(stats[half][1], (8, HALF))
        else:
            stats = tuple(
                (
                    stats_in[r, 0:1, half * HALF : (half + 1) * HALF],
                    stats_in[r, 8:9, half * HALF : (half + 1) * HALF],
                )
                for half in range(2)
            )
            count = jnp.where(kind == 0, ((chip + 1) >> 1) * 2, (chip >> 1) * 2 + 1)
            stats = lax.fori_loop(0, count, chip_block, stats)
            for half in range(2):
                lanes = slice(half * HALF, (half + 1) * HALF)
                os[r, :, lanes] = (acc[r, :, lanes] / stats[half][1]).astype(BF16)
        return carry

    lax.fori_loop(0, 4, one_queries, 0)
    if not own:
        for r in range(4):
            o_out[r][...] = os[r]


def pair_of(low, columns, h):
    return jnp.where(low, columns[:, h : h + 1], columns[:, h + 1 : h + 2])


def softplus(v):
    return jnp.maximum(v, 0.0) + jnp.log1p(jnp.exp(-jnp.abs(v)))


SPAN = slice(STATE_DIM, STATE_DIM + 8)
SPAN_LOW = slice(STATE_DIM + 8, STATE_DIM + 16)
HELD, SENT = STATE_DIM + 8, STATE_DIM + 16


def send_state(pay_ref, lanes, state, span):
    span_high = span.astype(BF16)
    pay_ref[0:STATE_DIM, lanes] = state.astype(BF16)
    pay_ref[STATE_DIM:SENT, lanes] = jnp.concatenate(
        [span_high.astype(F32), span - span_high.astype(F32)], axis=0
    ).astype(BF16)


def ssm_local_kernel(
    x_ref, write_t_ref, read_t_ref, step_t_ref, rate_ref, gain_ref, out_ref, total_ref, pay_ref, cum_ref
):
    heads = step_t_ref.shape[0]
    high = lax.Precision.HIGHEST
    row = lax.broadcasted_iota(jnp.int32, (TOK, TOK), 0)
    col = lax.broadcasted_iota(jnp.int32, (TOK, TOK), 1)
    rate = jnp.broadcast_to(-jnp.exp(rate_ref[...]) * LOG2E, (8, heads)).T[:, 0:1]
    step_t = softplus(step_t_ref[...])
    cum_t = jnp.dot(
        rate * step_t, jnp.where(row <= col, 1.0, 0.0), precision=high, preferred_element_type=F32
    )
    key_row = jnp.log2(step_t) - cum_t
    cum = cum_t.T
    step = step_t.T
    cum_ref[...] = cum
    last = cum[TOK - 1 : TOK, :]
    tail = jnp.exp2(last - cum) * step
    gain = gain_ref[...]

    near = lax.dot_general(
        read_t_ref[...], write_t_ref[...], (((0,), (0,)), ((), ())), preferred_element_type=F32
    )
    near = jnp.where(col <= row, near, 0.0)
    low = lax.broadcasted_iota(jnp.int32, (1, 128), 1) < SSM_DIM
    for h in range(0, heads, 2):
        lanes = slice(h * SSM_DIM, (h + 2) * SSM_DIM)
        x_pair = x_ref[:, lanes]
        x_f = x_pair.astype(F32)
        weighted = (x_f * pair_of(low, tail, h)).astype(BF16)
        state = jnp.dot(write_t_ref[...], weighted, preferred_element_type=F32)
        span = jnp.broadcast_to(pair_of(low, last, h), (8, 128))
        total_ref[0:STATE_DIM, lanes] = state
        total_ref[SPAN, lanes] = span
        send_state(pay_ref, lanes, state, span)
        for t in range(2):
            t_rows = slice(t * HALF, (t + 1) * HALF)
            both = []
            for k in range(2):
                total = None
                for s in range(t + 1):
                    s_rows = slice(s * HALF, (s + 1) * HALF)
                    weights = (
                        jnp.exp2(cum[t_rows, h + k : h + k + 1] + key_row[h + k : h + k + 1, s_rows])
                        * near[t_rows, s_rows]
                    )
                    part = jnp.dot(weights.astype(BF16), x_pair[s_rows, :], preferred_element_type=F32)
                    total = part if total is None else total + part
                both.append(total)
            out_ref[t_rows, lanes] = (
                jnp.where(low, both[0], both[1]) + pair_of(low, gain, h) * x_f[t_rows, :]
            )


def ssm_merge_kernel(level, info, got_ref, total_ref, before_ref, total_out, before_out, pay_ref):
    later = ((info[3] >> level) & 1).astype(F32)
    got = got_ref[0:STATE_DIM, :].astype(F32)
    got_span = got_ref[STATE_DIM:SENT, :].astype(F32)
    got_span = got_span[0:8, :] + got_span[8:16, :]
    total, total_span = total_ref[0:STATE_DIM, :], total_ref[SPAN, :]
    before, before_span = before_ref[0:STATE_DIM, :], before_ref[SPAN, :]
    before_out[0:STATE_DIM, :] = before + later * (got * jnp.exp2(before_span[0:1, :]))
    before_out[SPAN, :] = before_span + later * got_span
    after_got = got * jnp.exp2(total_span[0:1, :]) + total
    after_total = total * jnp.exp2(got_span[0:1, :]) + got
    total = later * after_got + (1.0 - later) * after_total
    span = total_span + got_span
    total_out[0:STATE_DIM, :] = total
    total_out[SPAN, :] = span
    send_state(pay_ref, slice(None), total, span)


def ssm_carry_kernel(state_ref, mixed_ref, cum_ref, read_t_ref, gate_ref, gated_ref, square_ref):
    heads = cum_ref.shape[1]
    state = state_ref[0:STATE_DIM, :]
    state_high = state.astype(BF16)
    state_low = (state - state_high.astype(F32)).astype(BF16)
    reach = jnp.exp2(cum_ref[...])
    read = read_t_ref[...].T
    low = lax.broadcasted_iota(jnp.int32, (1, 128), 1) < SSM_DIM
    squares = jnp.zeros((TOK, 128), F32)
    for h in range(0, heads, 2):
        lanes = slice(h * SSM_DIM, (h + 2) * SSM_DIM)
        carried = jnp.dot(read, state_high[:, lanes], preferred_element_type=F32)
        carried = carried + jnp.dot(read, state_low[:, lanes], preferred_element_type=F32)
        mixed = mixed_ref[:, lanes] + carried * pair_of(low, reach, h)
        gate = gate_ref[:, lanes].astype(F32)
        gated = mixed * (gate / (1.0 + jnp.exp(-gate)))
        gated_ref[:, lanes] = gated
        squares = squares + gated * gated
    square_ref[...] = jnp.broadcast_to(jnp.sum(squares.T, axis=0, keepdims=True), square_ref.shape)


def vmem(count):
    return [pl.BlockSpec(memory_space=pltpu.VMEM)] * count


SMEM = pl.BlockSpec(memory_space=pltpu.SMEM)
ANY = pl.BlockSpec(memory_space=pl.ANY)


SMALL = pl.CostEstimate(flops=1000, bytes_accessed=1000, transcendentals=0)


def params(mib):
    return pltpu.CompilerParams(vmem_limit_bytes=mib * 1024 * 1024)


def shape(dims, kind):
    return jax.ShapeDtypeStruct(dims, kind)


def pack(info, query_rows, key_rows, value_rows):
    width = HEADS * ATT_DIM
    rows = [ATT_DIM, 2 * ATT_DIM] + [3 * ATT_DIM] * 3
    return pl.pallas_call(
        pack_kernel,
        out_shape=[shape((count, TOK), BF16) for count in rows],
        in_specs=[SMEM] + [ANY] * 3,
        out_specs=vmem(len(rows)),
        scratch_shapes=[
            pltpu.VMEM((3, TOK, width), BF16),
            pltpu.VMEM((3, width, TOK), BF16),
            pltpu.SemaphoreType.DMA((3,)),
        ],
        compiler_params=params(60),
    )(info, query_rows, key_rows, value_rows)


def attend(own, info, *operands):
    queries = pltpu.VMEM((4, ATT_DIM, TOK), BF16)
    scratch = [pltpu.VMEM((4, 2 * TOK, ATT_DIM), BF16), pltpu.VMEM((4, ATT_DIM, 2 * TOK), BF16)]
    if own:
        out = [shape((4, ATT_DIM, TOK), F32), shape((4, 16, TOK), F32), shape((4, ATT_DIM, TOK), BF16)]
        specs = vmem(len(operands))
    else:
        out = [shape((ATT_DIM, TOK), BF16)] * 4
        scratch = [queries] + scratch + [
            pltpu.VMEM((8, ATT_DIM, TOK), BF16),
            pltpu.VMEM((4, ATT_DIM, TOK), F32),
            queries,
            pltpu.SemaphoreType.DMA((18,)),
        ]
        specs = [ANY] * (len(operands) - 1) + vmem(1)
    out = out + [shape((8, 128), F32)]
    return pl.pallas_call(
        functools.partial(attend_kernel, own),
        out_shape=out,
        in_specs=[SMEM] + specs,
        out_specs=vmem(len(out)),
        scratch_shapes=scratch,
        compiler_params=params(24),
        cost_estimate=SMALL,
    )(info, *operands)


def unpack(info, pieces):
    width = HEADS * ATT_DIM
    return pl.pallas_call(
        unpack_kernel,
        out_shape=shape((TOK, width), BF16),
        in_specs=[SMEM] + vmem(4),
        out_specs=vmem(1)[0],
        scratch_shapes=[pltpu.VMEM((width, TOK), BF16)],
        compiler_params=params(40),
    )(info, *pieces)


def ssm_local(ssm_inputs, write_t, read_t, step_t, rate, gain):
    tokens, width = ssm_inputs.shape
    heads = step_t.shape[0]
    return pl.pallas_call(
        ssm_local_kernel,
        out_shape=[
            shape((tokens, width), F32),
            shape((HELD, width), F32),
            shape((SENT, width), BF16),
            shape((tokens, heads), F32),
        ],
        in_specs=vmem(6),
        out_specs=vmem(4),
        compiler_params=params(40),
        cost_estimate=SMALL,
    )(ssm_inputs, write_t, read_t, step_t, rate, gain)


def ssm_merge(level, info, got, total, before):
    held, sent = shape(total.shape, F32), shape(got.shape, BF16)
    return pl.pallas_call(
        functools.partial(ssm_merge_kernel, level),
        out_shape=[held, held, sent],
        in_specs=[SMEM] + vmem(3),
        out_specs=vmem(3),
        compiler_params=params(40),
        cost_estimate=SMALL,
    )(info, got, total, before)


def ssm_carry(state, mixed, cum, read_t, gate):
    tokens, width = mixed.shape
    return pl.pallas_call(
        ssm_carry_kernel,
        out_shape=[shape((tokens, width), F32), shape((8, tokens), F32)],
        in_specs=vmem(5),
        out_specs=vmem(2),
        compiler_params=params(40),
        cost_estimate=SMALL,
    )(state, mixed, cum, read_t, gate)


def on_device(
    query_rows,
    key_rows,
    value_rows,
    ssm_inputs,
    ssm_gate,
    write_vecs,
    read_vecs,
    step_raw,
    decay_log,
    skip_gain,
    norm_gain,
):
    me = lax.axis_index("ctx")
    y, x, core = me >> 3, (me >> 1) & 3, me & 1
    info = jnp.stack([y * 2 + (x >> 1), (x ^ (x >> 1)) & 1, core, me]).astype(jnp.int32)
    tie = lax.optimization_barrier

    q_own, kv_own, *away = pack(info, query_rows, key_rows, value_rows)
    here, near, from_core = [None] * 4, [None] * 4, [None] * 4
    here[0] = kv_own
    here[1], here[2] = head_swap(away[0], 1), head_swap(away[1], 2)
    near[0] = class_swap(kv_own)
    from_core[0] = core_swap(kv_own)

    from_core[0], ssm_inputs = tie((from_core[0], ssm_inputs))
    read_t = read_vecs.T
    mixed, total, sent, cum = ssm_local(
        ssm_inputs, write_vecs.T, read_t, step_raw.T, decay_log[None, :], skip_gain[None, :]
    )
    before = jnp.zeros_like(total)
    total, before, sent = ssm_merge(0, info, core_swap(sent), total, before)
    total, before, sent = ssm_merge(1, info, class_swap(sent), total, before)

    here[1], here[2], near[0], away[2], sent = tie((here[1], here[2], near[0], away[2], sent))
    got = block_swap(sent, 4)
    here[3] = head_swap(away[2], 3)
    for r in (1, 2):
        near[r] = class_swap(here[r][ATT_DIM:])
    from_core[1] = core_swap(here[1])
    from_core[1], piece = tie((from_core[1], here[2]))
    from_core[2] = core_swap(piece)

    here[3], near[1], near[2], got = tie((here[3], near[1], near[2], got))
    near[3] = class_swap(here[3][ATT_DIM:])
    from_core[3] = core_swap(here[3])
    total, before, sent = ssm_merge(2, info, got, total, before)
    got = block_swap(sent, 8)
    partial, stats, queries, mark = attend(True, info, q_own, *here[1:], *here, *from_core)

    near[3], got, mark = tie((near[3], got, mark))
    near_core = [core_swap(piece) for piece in near]
    total, before, sent = ssm_merge(3, info, got, total, before)
    gated, squares = ssm_carry(before, mixed, cum, read_t, ssm_gate)
    squares = lax.all_gather(squares, "tp")
    *results, _ = attend(False, info, *near, *near_core, mark, queries, partial, stats)
    back = [results[0]] + [head_swap(results[r], r) for r in range(1, 4)]
    back[1], squares = tie((back[1], squares))
    factor = lax.rsqrt(jnp.sum(squares[:, 0], axis=0) / SSM_WIDTH + 1e-05)
    mixer_out = (gated * factor[:, None] * norm_gain[None, :]).astype(BF16)
    return (unpack(info, back), mixer_out)


def solution(mesh):
    placed = (
        P("ctx", "tp"),
        P("ctx", "tp"),
        P("ctx", "tp"),
        P("ctx", "tp"),
        P("ctx", "tp"),
        P("ctx", None),
        P("ctx", None),
        P("ctx", "tp"),
        P("tp"),
        P("tp"),
        P("tp"),
    )
    return jax.shard_map(
        on_device,
        mesh=mesh,
        in_specs=placed,
        out_specs=(P("ctx", "tp"), P("ctx", "tp")),
        check_vma=False,
    )
```

```python
import functools
import math

import jax
import jax.numpy as jnp
from jax import lax
from jax.experimental import pallas as pl
from jax.experimental.pallas import tpu as pltpu
from jax.sharding import PartitionSpec as P

ATT_DIM = 224
SSM_DIM = 64
STATE_DIM = 64
SSM_WIDTH = 7168
TOK = 512
HEADS = 4
CTX = 16
HALF = 256
LOG2E = math.log2(math.e)
F32 = jnp.float32
BF16 = jnp.bfloat16


def exchanged(i, r):
    y, x, c = i >> 3, (i >> 1) & 3, i & 1
    if r & 1:
        x = 3 - x
    if r & 2:
        y = 1 - y
    return y * 8 + x * 2 + c


def head_swap(value, r):
    return lax.ppermute(value, "ctx", [(i, exchanged(i, r)) for i in range(CTX)])


def class_swap(value):
    return lax.ppermute(value, "ctx", [(i, i ^ 2) for i in range(CTX)])


def core_swap(value):
    return lax.ppermute(value, "ctx", [(i, i ^ 1) for i in range(CTX)])


def block_swap(value, step):
    return lax.ppermute(value, "ctx", [(i, i ^ step) for i in range(CTX)])


def head_rows(head):
    return pl.ds(pl.multiple_of(head * ATT_DIM, 16), ATT_DIM)


Q_ROWS = slice(0, ATT_DIM)
K_ROWS = slice(ATT_DIM, 2 * ATT_DIM)
V_ROWS = slice(2 * ATT_DIM, 3 * ATT_DIM)


def pack_kernel(info, q_in, k_in, v_in, q_own, q_1, q_2, kv_own, kv_1, kv_2, all_3, raw, rows_ref, sems):
    copies = [pltpu.make_async_copy(src, raw.at[i], sems.at[i]) for i, src in enumerate((k_in, v_in, q_in))]
    for copy in copies:
        copy.start()
    for i, (own, one, two, first) in enumerate(((kv_own, kv_1, kv_2, 0), (kv_own, kv_1, kv_2, ATT_DIM), (q_own, q_1, q_2, 0))):
        copies[i].wait()
        rows_ref[i] = raw[i].T
        for r, out in enumerate((own, one, two)):
            out[first : first + ATT_DIM, :] = rows_ref[i, head_rows(info[0] ^ r), :]
        all_3[(K_ROWS, V_ROWS, Q_ROWS)[i], :] = rows_ref[i, head_rows(info[0] ^ 3), :]


def unpack_kernel(info, _, *refs):
    pieces, out_ref, rows_ref = refs[:4], refs[4], refs[5]
    for r in range(4):
        rows_ref[head_rows(info[0] ^ r), :] = pieces[r][...]
    out_ref[...] = rows_ref[...].T


def attend_kernel(own, info, *refs):
    hid, kind, core = info[0], info[1], info[2]
    scale = ATT_DIM ** (-0.5) * LOG2E

    if own:
        queries, pieces, refs = refs[:4], refs[4:12], refs[12:]
        acc, stats_out, qs, mark, ks, vs = refs
        for r in range(4):
            qs[r] = queries[r][Q_ROWS, :]
    else:
        pieces, refs = refs[:8], refs[8:]
        _, qs, acc_in, stats_in, *o_out, mark, ks, vs, acc, os = refs
    for i, piece in enumerate(pieces):
        k_first = ATT_DIM if own and i & 3 == 3 else 0
        v_first = k_first + ATT_DIM
        start = pl.multiple_of((core ^ (i >> 2)) * TOK, TOK)
        ks[hid ^ (i & 3), pl.ds(start, TOK), :] = piece[k_first:v_first, :].T
        vs[hid ^ (i & 3), :, pl.ds(start, TOK)] = piece[v_first : v_first + ATT_DIM, :]
    mark[...] = jnp.zeros_like(mark)

    def one_queries(r, carry):
        chip = hid ^ r

        def visit(keys, values, stats, masked):
            lanes = [slice(half * HALF, (half + 1) * HALF) for half in range(2)]
            scores = [
                jnp.dot(keys, qs[r, :, lanes[half]], preferred_element_type=F32) for half in range(2)
            ]
            new_stats, low, shrinks = [], [], []
            for half in range(2):
                (top, total), s = stats[half], scores[half]
                if masked:
                    k_pos = lax.broadcasted_iota(jnp.int32, s.shape, 0)
                    q_pos = lax.broadcasted_iota(jnp.int32, s.shape, 1) + half * HALF
                    s = jnp.where(k_pos <= q_pos, s, -1e30)
                new_top = jnp.maximum(top, jnp.max(s, axis=0, keepdims=True))
                p = jnp.exp2((s - new_top) * scale)
                shrink = jnp.exp2((top - new_top) * scale)
                total = total * shrink + jnp.sum(p, axis=0, keepdims=True)
                new_stats.append((new_top, total))
                low.append(p.astype(BF16))
                shrinks.append(shrink)
            for half in range(2):
                acc[r, :, lanes[half]] = acc[r, :, lanes[half]] * shrinks[half] + jnp.dot(
                    values, low[half], preferred_element_type=F32
                )
            return tuple(new_stats)

        def chip_block(j, stats):
            return visit(ks[j], vs[j], stats, False)

        def core_block(start, stats, masked):
            start = pl.multiple_of(start, TOK)
            return visit(
                ks[chip, pl.ds(start, TOK), :], vs[chip, :, pl.ds(start, TOK)], stats, masked
            )

        if own:
            acc[r] = jnp.zeros((ATT_DIM, TOK), F32)
            first = (jnp.full((1, HALF), -1e30, F32), jnp.zeros((1, HALF), F32))
            stats = lax.fori_loop(0, chip, chip_block, (first, first))
            stats = lax.fori_loop(0, core, lambda k, now: core_block(0, now, False), stats)
            stats = core_block(core * TOK, stats, True)
            for half in range(2):
                lanes = slice(half * HALF, (half + 1) * HALF)
                stats_out[r, 0:8, lanes] = jnp.broadcast_to(stats[half][0], (8, HALF))
                stats_out[r, 8:16, lanes] = jnp.broadcast_to(stats[half][1], (8, HALF))
        else:
            acc[r] = acc_in[r]
            stats = tuple(
                (
                    stats_in[r, 0:1, half * HALF : (half + 1) * HALF],
                    stats_in[r, 8:9, half * HALF : (half + 1) * HALF],
                )
                for half in range(2)
            )
            count = jnp.where(kind == 0, ((chip + 1) >> 1) * 2, (chip >> 1) * 2 + 1)
            stats = lax.fori_loop(0, count, chip_block, stats)
            for half in range(2):
                lanes = slice(half * HALF, (half + 1) * HALF)
                os[r, :, lanes] = (acc[r, :, lanes] / stats[half][1]).astype(BF16)
        return carry

    lax.fori_loop(0, 4, one_queries, 0)
    if not own:
        for r in range(4):
            o_out[r][...] = os[r]


def pair_of(low, columns, h):
    return jnp.where(low, columns[:, h : h + 1], columns[:, h + 1 : h + 2])


def softplus(v):
    return jnp.maximum(v, 0.0) + jnp.log1p(jnp.exp(-jnp.abs(v)))


SPAN = slice(STATE_DIM, STATE_DIM + 8)
SPAN_LOW = slice(STATE_DIM + 8, STATE_DIM + 16)
HELD, SENT = STATE_DIM + 8, STATE_DIM + 16


def send_state(pay_ref, lanes, state, span):
    span_high = span.astype(BF16)
    pay_ref[0:STATE_DIM, lanes] = state.astype(BF16)
    pay_ref[STATE_DIM:SENT, lanes] = jnp.concatenate(
        [span_high.astype(F32), span - span_high.astype(F32)], axis=0
    ).astype(BF16)


def ssm_local_kernel(
    x_ref, write_t_ref, read_t_ref, step_t_ref, rate_ref, gain_ref, out_ref, total_ref, pay_ref, cum_ref
):
    heads = step_t_ref.shape[0]
    high = lax.Precision.HIGHEST
    row = lax.broadcasted_iota(jnp.int32, (TOK, TOK), 0)
    col = lax.broadcasted_iota(jnp.int32, (TOK, TOK), 1)
    rate = jnp.broadcast_to(-jnp.exp(rate_ref[...]) * LOG2E, (8, heads)).T[:, 0:1]
    step_t = softplus(step_t_ref[...])
    cum_t = jnp.dot(
        rate * step_t, jnp.where(row <= col, 1.0, 0.0), precision=high, preferred_element_type=F32
    )
    key_row = jnp.log2(step_t) - cum_t
    cum = cum_t.T
    step = step_t.T
    cum_ref[...] = cum
    last = cum[TOK - 1 : TOK, :]
    tail = jnp.exp2(last - cum) * step
    gain = gain_ref[...]

    near = lax.dot_general(
        read_t_ref[...], write_t_ref[...], (((0,), (0,)), ((), ())), preferred_element_type=F32
    )
    near = jnp.where(col <= row, near, 0.0)
    low = lax.broadcasted_iota(jnp.int32, (1, 128), 1) < SSM_DIM
    for h in range(0, heads, 2):
        lanes = slice(h * SSM_DIM, (h + 2) * SSM_DIM)
        x_pair = x_ref[:, lanes]
        x_f = x_pair.astype(F32)
        weighted = (x_f * pair_of(low, tail, h)).astype(BF16)
        state = jnp.dot(write_t_ref[...], weighted, preferred_element_type=F32)
        span = jnp.broadcast_to(pair_of(low, last, h), (8, 128))
        total_ref[0:STATE_DIM, lanes] = state
        total_ref[SPAN, lanes] = span
        send_state(pay_ref, lanes, state, span)
        for t in range(2):
            t_rows = slice(t * HALF, (t + 1) * HALF)
            both = []
            for k in range(2):
                total = None
                for s in range(t + 1):
                    s_rows = slice(s * HALF, (s + 1) * HALF)
                    weights = (
                        jnp.exp2(cum[t_rows, h + k : h + k + 1] + key_row[h + k : h + k + 1, s_rows])
                        * near[t_rows, s_rows]
                    )
                    part = jnp.dot(weights.astype(BF16), x_pair[s_rows, :], preferred_element_type=F32)
                    total = part if total is None else total + part
                both.append(total)
            out_ref[t_rows, lanes] = (
                jnp.where(low, both[0], both[1]) + pair_of(low, gain, h) * x_f[t_rows, :]
            )


def ssm_merge_kernel(level, info, got_ref, total_ref, before_ref, total_out, before_out, pay_ref):
    later = ((info[3] >> level) & 1).astype(F32)
    got = got_ref[0:STATE_DIM, :].astype(F32)
    got_span = got_ref[STATE_DIM:SENT, :].astype(F32)
    got_span = got_span[0:8, :] + got_span[8:16, :]
    total, total_span = total_ref[0:STATE_DIM, :], total_ref[SPAN, :]
    before, before_span = before_ref[0:STATE_DIM, :], before_ref[SPAN, :]
    before_out[0:STATE_DIM, :] = before + later * (got * jnp.exp2(before_span[0:1, :]))
    before_out[SPAN, :] = before_span + later * got_span
    after_got = got * jnp.exp2(total_span[0:1, :]) + total
    after_total = total * jnp.exp2(got_span[0:1, :]) + got
    total = later * after_got + (1.0 - later) * after_total
    span = total_span + got_span
    total_out[0:STATE_DIM, :] = total
    total_out[SPAN, :] = span
    send_state(pay_ref, slice(None), total, span)


def ssm_carry_kernel(state_ref, mixed_ref, cum_ref, read_t_ref, gate_ref, gated_ref, square_ref):
    heads = cum_ref.shape[1]
    state = state_ref[0:STATE_DIM, :]
    state_high = state.astype(BF16)
    state_low = (state - state_high.astype(F32)).astype(BF16)
    reach = jnp.exp2(cum_ref[...])
    read = read_t_ref[...].T
    low = lax.broadcasted_iota(jnp.int32, (1, 128), 1) < SSM_DIM
    squares = jnp.zeros((TOK, 128), F32)
    for h in range(0, heads, 2):
        lanes = slice(h * SSM_DIM, (h + 2) * SSM_DIM)
        carried = jnp.dot(read, state_high[:, lanes], preferred_element_type=F32)
        carried = carried + jnp.dot(read, state_low[:, lanes], preferred_element_type=F32)
        mixed = mixed_ref[:, lanes] + carried * pair_of(low, reach, h)
        gate = gate_ref[:, lanes].astype(F32)
        gated = mixed * (gate / (1.0 + jnp.exp(-gate)))
        gated_ref[:, lanes] = gated
        squares = squares + gated * gated
    square_ref[...] = jnp.broadcast_to(jnp.sum(squares.T, axis=0, keepdims=True), square_ref.shape)


def vmem(count):
    return [pl.BlockSpec(memory_space=pltpu.VMEM)] * count


SMEM = pl.BlockSpec(memory_space=pltpu.SMEM)
ANY = pl.BlockSpec(memory_space=pl.ANY)


SMALL = pl.CostEstimate(flops=1000, bytes_accessed=1000, transcendentals=0)
LARGE = pl.CostEstimate(flops=4 * 10**10, bytes_accessed=6 * 2**20, transcendentals=10**6)


def params(mib):
    return pltpu.CompilerParams(vmem_limit_bytes=mib * 1024 * 1024)


def shape(dims, kind):
    return jax.ShapeDtypeStruct(dims, kind)


def pack(info, query_rows, key_rows, value_rows):
    width = HEADS * ATT_DIM
    rows = [ATT_DIM] * 3 + [2 * ATT_DIM] * 3 + [3 * ATT_DIM]
    return pl.pallas_call(
        pack_kernel,
        out_shape=[shape((count, TOK), BF16) for count in rows],
        in_specs=[SMEM] + [ANY] * 3,
        out_specs=vmem(len(rows)),
        scratch_shapes=[
            pltpu.VMEM((3, TOK, width), BF16),
            pltpu.VMEM((3, width, TOK), BF16),
            pltpu.SemaphoreType.DMA((3,)),
        ],
        compiler_params=params(60),
    )(info, query_rows, key_rows, value_rows)


def attend(own, info, *operands):
    scratch = [pltpu.VMEM((4, 2 * TOK, ATT_DIM), BF16), pltpu.VMEM((4, ATT_DIM, 2 * TOK), BF16)]
    if own:
        out = [shape((4, ATT_DIM, TOK), F32), shape((4, 16, TOK), F32), shape((4, ATT_DIM, TOK), BF16)]
    else:
        out = [shape((ATT_DIM, TOK), BF16)] * 4
        scratch += [pltpu.VMEM((4, ATT_DIM, TOK), F32), pltpu.VMEM((4, ATT_DIM, TOK), BF16)]
    out = out + [shape((8, 128), F32)]
    return pl.pallas_call(
        functools.partial(attend_kernel, own),
        out_shape=out,
        in_specs=[SMEM] + vmem(len(operands)),
        out_specs=vmem(len(out)),
        scratch_shapes=scratch,
        compiler_params=params(24),
        cost_estimate=SMALL,
    )(info, *operands)


def unpack(info, mark, pieces):
    width = HEADS * ATT_DIM
    return pl.pallas_call(
        unpack_kernel,
        out_shape=shape((TOK, width), BF16),
        in_specs=[SMEM, ANY] + vmem(4),
        out_specs=vmem(1)[0],
        scratch_shapes=[pltpu.VMEM((width, TOK), BF16)],
        compiler_params=params(40),
    )(info, mark, *pieces)


def ssm_local(ssm_inputs, write_t, read_t, step_t, rate, gain):
    tokens, width = ssm_inputs.shape
    heads = step_t.shape[0]
    return pl.pallas_call(
        ssm_local_kernel,
        out_shape=[
            shape((tokens, width), F32),
            shape((HELD, width), F32),
            shape((SENT, width), BF16),
            shape((tokens, heads), F32),
        ],
        in_specs=vmem(6),
        out_specs=vmem(4),
        compiler_params=params(40),
        cost_estimate=SMALL,
    )(ssm_inputs, write_t, read_t, step_t, rate, gain)


def ssm_merge(level, info, got, total, before):
    held, sent = shape(total.shape, F32), shape(got.shape, BF16)
    return pl.pallas_call(
        functools.partial(ssm_merge_kernel, level),
        out_shape=[held, held, sent],
        in_specs=[SMEM] + vmem(3),
        out_specs=vmem(3),
        compiler_params=params(40),
        cost_estimate=LARGE if level == 3 else SMALL,
    )(info, got, total, before)


def ssm_carry(count, state, mixed, cum, read_t, gate):
    tokens, width = mixed.shape
    return pl.pallas_call(
        ssm_carry_kernel,
        out_shape=[shape((tokens, width), F32), shape((8 * count, tokens), F32)],
        in_specs=vmem(5),
        out_specs=vmem(2),
        compiler_params=params(40),
        cost_estimate=LARGE,
    )(state, mixed, cum, read_t, gate)


def on_device(
    query_rows,
    key_rows,
    value_rows,
    ssm_inputs,
    ssm_gate,
    write_vecs,
    read_vecs,
    step_raw,
    decay_log,
    skip_gain,
    norm_gain,
):
    me = lax.axis_index("ctx")
    y, x, core = me >> 3, (me >> 1) & 3, me & 1
    info = jnp.stack([y * 2 + (x >> 1), (x ^ (x >> 1)) & 1, core, me]).astype(jnp.int32)
    tie = lax.optimization_barrier

    q_own, q_1, q_2, kv_own, kv_1, kv_2, all_3 = pack(info, query_rows, key_rows, value_rows)
    here, near, from_core = [kv_own] + [None] * 3, [None] * 4, [None] * 4
    here[1], here[2] = head_swap(kv_1, 1), head_swap(kv_2, 2)
    near[0] = class_swap(kv_own)
    from_core[0] = core_swap(kv_own)

    from_core[0], ssm_inputs = tie((from_core[0], ssm_inputs))
    read_t = read_vecs.T
    mixed, total, sent, cum = ssm_local(
        ssm_inputs, write_vecs.T, read_t, step_raw.T, decay_log[None, :], skip_gain[None, :]
    )
    before = jnp.zeros_like(total)
    total, before, sent = ssm_merge(0, info, core_swap(sent), total, before)
    got = class_swap(sent)

    here[1], here[2], near[0], all_3, got = tie((here[1], here[2], near[0], all_3, got))
    near[1], near[2] = class_swap(here[1]), class_swap(here[2])
    here[3] = head_swap(all_3, 3)
    total, before, sent = ssm_merge(1, info, got, total, before)
    q_1, q_2, sent = tie((q_1, q_2, sent))
    q_1, q_2 = head_swap(q_1, 1), head_swap(q_2, 2)

    here[3], near[1], near[2], q_1, q_2, sent = tie((here[3], near[1], near[2], q_1, q_2, sent))
    near[3] = class_swap(here[3][ATT_DIM:])
    for r in range(1, 4):
        from_core[r] = core_swap(here[r])
    got = block_swap(sent, 4)
    partial, stats, queries, mark = attend(True, info, q_own, q_1, q_2, here[3], *here, *from_core)

    near[3], got, mark = tie((near[3], got, mark))
    near_core = [core_swap(piece) for piece in near]
    total, before, sent = ssm_merge(2, info, got, total, before)
    got = block_swap(sent, 8)
    *results, mark = attend(False, info, *near, *near_core, mark, queries, partial, stats)
    back = [results[0]] + [head_swap(results[r], r) for r in range(1, 4)]
    got, mark = tie((got, mark))
    total, before, sent = ssm_merge(3, info, got, total, before)
    count = lax.axis_size("tp")
    gated, squares = ssm_carry(count, before, mixed, cum, read_t, ssm_gate)
    squares = lax.all_to_all(squares, "tp", 0, 0, tiled=True).reshape(count, 8, TOK)
    *back, squares = tie((*back, squares))
    factor = lax.rsqrt(jnp.sum(squares[:, 0], axis=0) / SSM_WIDTH + 1e-05)
    mixer_out = (gated * factor[:, None] * norm_gain[None, :]).astype(BF16)
    return (unpack(info, mark, back), mixer_out)


def solution(mesh):
    placed = (
        P("ctx", "tp"),
        P("ctx", "tp"),
        P("ctx", "tp"),
        P("ctx", "tp"),
        P("ctx", "tp"),
        P("ctx", None),
        P("ctx", None),
        P("ctx", "tp"),
        P("tp"),
        P("tp"),
        P("tp"),
    )
    return jax.shard_map(
        on_device,
        mesh=mesh,
        in_specs=placed,
        out_specs=(P("ctx", "tp"), P("ctx", "tp")),
        check_vma=False,
    )
```

```python
import functools
import math

import jax
import jax.numpy as jnp
from jax import lax
from jax.experimental import pallas as pl
from jax.experimental.pallas import tpu as pltpu
from jax.sharding import PartitionSpec as P

ATT_DIM = 224
SSM_DIM = 64
STATE_DIM = 64
SSM_WIDTH = 7168
TOK = 512
HEADS = 4
CTX = 16
HALF = 256
LOG2E = math.log2(math.e)
F32 = jnp.float32
BF16 = jnp.bfloat16


def exchanged(i, r):
    y, x, c = i >> 3, (i >> 1) & 3, i & 1
    if r & 1:
        x = 3 - x
    if r & 2:
        y = 1 - y
    return y * 8 + x * 2 + c


def head_swap(value, r):
    return lax.ppermute(value, "ctx", [(i, exchanged(i, r)) for i in range(CTX)])


def class_swap(value):
    return lax.ppermute(value, "ctx", [(i, i ^ 2) for i in range(CTX)])


def core_swap(value):
    return lax.ppermute(value, "ctx", [(i, i ^ 1) for i in range(CTX)])


def block_swap(value, step):
    return lax.ppermute(value, "ctx", [(i, i ^ step) for i in range(CTX)])


def head_rows(head):
    return pl.ds(pl.multiple_of(head * ATT_DIM, 16), ATT_DIM)


Q_ROWS = slice(0, ATT_DIM)
K_ROWS = slice(ATT_DIM, 2 * ATT_DIM)
V_ROWS = slice(2 * ATT_DIM, 3 * ATT_DIM)


def pack_kernel(info, q_in, k_in, v_in, q_own, kv_own, all_1, all_2, all_3, raw, rows_ref, sems):
    copies = [pltpu.make_async_copy(src, raw.at[i], sems.at[i]) for i, src in enumerate((q_in, k_in, v_in))]
    for copy in copies:
        copy.start()
    for i, (out, first) in enumerate(((q_own, 0), (kv_own, 0), (kv_own, ATT_DIM))):
        copies[i].wait()
        rows_ref[i] = raw[i].T
        out[first : first + ATT_DIM, :] = rows_ref[i, head_rows(info[0]), :]
        for r, away in ((1, all_1), (2, all_2), (3, all_3)):
            away[i * ATT_DIM : (i + 1) * ATT_DIM, :] = rows_ref[i, head_rows(info[0] ^ r), :]


def unpack_kernel(info, _, *refs):
    pieces, out_ref, rows_ref = refs[:4], refs[4], refs[5]
    for r in range(4):
        rows_ref[head_rows(info[0] ^ r), :] = pieces[r][...]
    out_ref[...] = rows_ref[...].T


def attend_kernel(stage, info, *refs):
    hid, kind, core = info[0], info[1], info[2]
    scale = ATT_DIM ** (-0.5) * LOG2E
    if stage == 0:
        q_in, (kv_own, core_0, core_1, core_2, near_0, near_core_0), refs = refs[:3], refs[3:9], refs[9:]
        acc, stats_ref, ks, vs, mark, qs = refs
        pieces = [(0, 0, kv_own, 0), (1, 0, q_in[1], ATT_DIM), (2, 0, q_in[2], ATT_DIM)]
        pieces += [(0, 1, core_0, 0), (1, 1, core_1, 0), (2, 1, core_2, 0)]
        pieces += [(3, 0, near_0, 0), (3, 1, near_core_0, 0)]
    elif stage == 1:
        q_in, (core_3, near_1, near_core_1, near_2, near_core_2, _), refs = refs[:4], refs[4:10], refs[10:]
        ks_early, vs_early, acc_in, stats_in, acc, stats_ref, mark, ks, vs, qs = refs
        pieces = [(0, 0, q_in[3], ATT_DIM), (0, 1, core_3, 0)]
        pieces += [(1, 0, near_1, 0), (1, 1, near_core_1, 0), (2, 0, near_2, 0), (2, 1, near_core_2, 0)]
    else:
        q_in, (near_3, near_core_3, _), refs = refs[:4], refs[4:7], refs[7:]
        acc_in, stats_in, *o_out, mark, ks, vs, qs, acc, os = refs
        pieces = [(0, 0, near_3, 0), (0, 1, near_core_3, 0)]
    for slot, other, piece, first in pieces:
        start = pl.multiple_of((core ^ other) * TOK, TOK)
        ks[slot, pl.ds(start, TOK), :] = piece[first : first + ATT_DIM, :].T
        vs[slot, :, pl.ds(start, TOK)] = piece[first + ATT_DIM : first + 2 * ATT_DIM, :]
    for r, queries in enumerate(q_in):
        qs[r] = queries[Q_ROWS, :]
    mark[...] = jnp.zeros_like(mark)

    def one_queries(r, carry):
        chip = hid ^ r

        def visit(keys, values, stats, masked):
            lanes = [slice(half * HALF, (half + 1) * HALF) for half in range(2)]
            scores = [
                jnp.dot(keys, qs[r, :, lanes[half]], preferred_element_type=F32) for half in range(2)
            ]
            new_stats, low, shrinks = [], [], []
            for half in range(2):
                (top, total), s = stats[half], scores[half]
                if masked:
                    k_pos = lax.broadcasted_iota(jnp.int32, s.shape, 0)
                    q_pos = lax.broadcasted_iota(jnp.int32, s.shape, 1) + half * HALF
                    s = jnp.where(k_pos <= q_pos, s, -1e30)
                new_top = jnp.maximum(top, jnp.max(s, axis=0, keepdims=True))
                p = jnp.exp2((s - new_top) * scale)
                shrink = jnp.exp2((top - new_top) * scale)
                total = total * shrink + jnp.sum(p, axis=0, keepdims=True)
                new_stats.append((new_top, total))
                low.append(p.astype(BF16))
                shrinks.append(shrink)
            for half in range(2):
                acc[r, :, lanes[half]] = acc[r, :, lanes[half]] * shrinks[half] + jnp.dot(
                    values, low[half], preferred_element_type=F32
                )
            return tuple(new_stats)

        def sweep(count, key_ref, value_ref, seen, stats):
            def one(k, now):
                times = jnp.where(seen(k), 1, 0)
                return lax.fori_loop(
                    0, times, lambda _, inner: visit(key_ref[k], value_ref[k], inner, False), now
                )

            return lax.fori_loop(0, count, one, stats)

        def near_seen(k):
            limit = jnp.where(kind == 0, ((chip + 1) >> 1) * 2, (chip >> 1) * 2 + 1)
            return (hid ^ k) < limit

        def diagonal(slot, stats):
            def part(start, now, masked):
                start = pl.multiple_of(start, TOK)
                return visit(ks[slot, pl.ds(start, TOK), :], vs[slot, :, pl.ds(start, TOK)], now, masked)

            stats = lax.fori_loop(0, core, lambda _, now: part(0, now, False), stats)
            return part(core * TOK, stats, True)

        if stage == 0:
            acc[r] = jnp.zeros((ATT_DIM, TOK), F32)
            first = (jnp.full((1, HALF), -1e30, F32), jnp.zeros((1, HALF), F32))
            stats = (first, first)
        else:
            acc[r] = acc_in[r]
            stats = tuple(
                (
                    stats_in[r, 0:1, half * HALF : (half + 1) * HALF],
                    stats_in[r, 8:9, half * HALF : (half + 1) * HALF],
                )
                for half in range(2)
            )

        if stage == 0:

            def early(now):
                now = sweep(4, ks, vs, lambda k: jnp.where(k == 3, near_seen(0), (hid ^ k) < chip), now)
                return diagonal(r, now)

            stats = lax.fori_loop(0, jnp.where(r == 3, 0, 1), lambda _, now: early(now), stats)
        elif stage == 1:
            last = jnp.where(r == 3, 1, 0)
            stats = sweep(
                4 * last, ks_early, vs_early, lambda k: jnp.where(k == 3, near_seen(0), (hid ^ k) < chip), stats
            )
            stats = sweep(3, ks, vs, lambda k: jnp.where(k == 0, (hid ^ 3) < chip, near_seen(k)), stats)
            stats = lax.fori_loop(0, last, lambda _, now: diagonal(0, now), stats)
        else:
            stats = sweep(1, ks, vs, lambda k: near_seen(3), stats)

        for half in range(2):
            lanes = slice(half * HALF, (half + 1) * HALF)
            if stage == 2:
                os[r, :, lanes] = (acc[r, :, lanes] / stats[half][1]).astype(BF16)
            else:
                stats_ref[r, 0:8, lanes] = jnp.broadcast_to(stats[half][0], (8, HALF))
                stats_ref[r, 8:16, lanes] = jnp.broadcast_to(stats[half][1], (8, HALF))
        return carry

    lax.fori_loop(0, 4, one_queries, 0)
    if stage == 2:
        for r in range(4):
            o_out[r][...] = os[r]


def pair_of(low, columns, h):
    return jnp.where(low, columns[:, h : h + 1], columns[:, h + 1 : h + 2])


def softplus(v):
    return jnp.maximum(v, 0.0) + jnp.log1p(jnp.exp(-jnp.abs(v)))


SPAN = slice(STATE_DIM, STATE_DIM + 8)
SPAN_LOW = slice(STATE_DIM + 8, STATE_DIM + 16)
HELD, SENT = STATE_DIM + 8, STATE_DIM + 16


def send_state(pay_ref, lanes, state, span):
    span_high = span.astype(BF16)
    pay_ref[0:STATE_DIM, lanes] = state.astype(BF16)
    pay_ref[STATE_DIM:SENT, lanes] = jnp.concatenate(
        [span_high.astype(F32), span - span_high.astype(F32)], axis=0
    ).astype(BF16)


def ssm_local_kernel(
    x_ref, write_t_ref, read_t_ref, step_t_ref, rate_ref, gain_ref, out_ref, total_ref, pay_ref, cum_ref
):
    heads = step_t_ref.shape[0]
    high = lax.Precision.HIGHEST
    row = lax.broadcasted_iota(jnp.int32, (TOK, TOK), 0)
    col = lax.broadcasted_iota(jnp.int32, (TOK, TOK), 1)
    rate = jnp.broadcast_to(-jnp.exp(rate_ref[...]) * LOG2E, (8, heads)).T[:, 0:1]
    step_t = softplus(step_t_ref[...])
    cum_t = jnp.dot(
        rate * step_t, jnp.where(row <= col, 1.0, 0.0), precision=high, preferred_element_type=F32
    )
    key_row = jnp.log2(step_t) - cum_t
    cum = cum_t.T
    step = step_t.T
    cum_ref[...] = cum
    last = cum[TOK - 1 : TOK, :]
    tail = jnp.exp2(last - cum) * step
    gain = gain_ref[...]

    near = lax.dot_general(
        read_t_ref[...], write_t_ref[...], (((0,), (0,)), ((), ())), preferred_element_type=F32
    )
    near = jnp.where(col <= row, near, 0.0)
    low = lax.broadcasted_iota(jnp.int32, (1, 128), 1) < SSM_DIM
    for h in range(0, heads, 2):
        lanes = slice(h * SSM_DIM, (h + 2) * SSM_DIM)
        x_pair = x_ref[:, lanes]
        x_f = x_pair.astype(F32)
        weighted = (x_f * pair_of(low, tail, h)).astype(BF16)
        state = jnp.dot(write_t_ref[...], weighted, preferred_element_type=F32)
        span = jnp.broadcast_to(pair_of(low, last, h), (8, 128))
        total_ref[0:STATE_DIM, lanes] = state
        total_ref[SPAN, lanes] = span
        send_state(pay_ref, lanes, state, span)
        for t in range(2):
            t_rows = slice(t * HALF, (t + 1) * HALF)
            both = []
            for k in range(2):
                total = None
                for s in range(t + 1):
                    s_rows = slice(s * HALF, (s + 1) * HALF)
                    weights = (
                        jnp.exp2(cum[t_rows, h + k : h + k + 1] + key_row[h + k : h + k + 1, s_rows])
                        * near[t_rows, s_rows]
                    )
                    part = jnp.dot(weights.astype(BF16), x_pair[s_rows, :], preferred_element_type=F32)
                    total = part if total is None else total + part
                both.append(total)
            out_ref[t_rows, lanes] = (
                jnp.where(low, both[0], both[1]) + pair_of(low, gain, h) * x_f[t_rows, :]
            )


def ssm_merge_kernel(level, info, got_ref, total_ref, before_ref, total_out, before_out, pay_ref):
    later = ((info[3] >> level) & 1).astype(F32)
    got = got_ref[0:STATE_DIM, :].astype(F32)
    got_span = got_ref[STATE_DIM:SENT, :].astype(F32)
    got_span = got_span[0:8, :] + got_span[8:16, :]
    total, total_span = total_ref[0:STATE_DIM, :], total_ref[SPAN, :]
    before, before_span = before_ref[0:STATE_DIM, :], before_ref[SPAN, :]
    before_out[0:STATE_DIM, :] = before + later * (got * jnp.exp2(before_span[0:1, :]))
    before_out[SPAN, :] = before_span + later * got_span
    after_got = got * jnp.exp2(total_span[0:1, :]) + total
    after_total = total * jnp.exp2(got_span[0:1, :]) + got
    total = later * after_got + (1.0 - later) * after_total
    span = total_span + got_span
    total_out[0:STATE_DIM, :] = total
    total_out[SPAN, :] = span
    send_state(pay_ref, slice(None), total, span)


def ssm_carry_kernel(state_ref, mixed_ref, cum_ref, read_t_ref, gate_ref, gated_ref, square_ref):
    heads = cum_ref.shape[1]
    state = state_ref[0:STATE_DIM, :]
    state_high = state.astype(BF16)
    state_low = (state - state_high.astype(F32)).astype(BF16)
    reach = jnp.exp2(cum_ref[...])
    read = read_t_ref[...].T
    low = lax.broadcasted_iota(jnp.int32, (1, 128), 1) < SSM_DIM
    squares = jnp.zeros((TOK, 128), F32)
    for h in range(0, heads, 2):
        lanes = slice(h * SSM_DIM, (h + 2) * SSM_DIM)
        carried = jnp.dot(read, state_high[:, lanes], preferred_element_type=F32)
        carried = carried + jnp.dot(read, state_low[:, lanes], preferred_element_type=F32)
        mixed = mixed_ref[:, lanes] + carried * pair_of(low, reach, h)
        gate = gate_ref[:, lanes].astype(F32)
        gated = mixed * (gate / (1.0 + jnp.exp(-gate)))
        gated_ref[:, lanes] = gated
        squares = squares + gated * gated
    square_ref[...] = jnp.broadcast_to(jnp.sum(squares.T, axis=0, keepdims=True), square_ref.shape)


def vmem(count):
    return [pl.BlockSpec(memory_space=pltpu.VMEM)] * count


SMEM = pl.BlockSpec(memory_space=pltpu.SMEM)
ANY = pl.BlockSpec(memory_space=pl.ANY)


SMALL = pl.CostEstimate(flops=1000, bytes_accessed=1000, transcendentals=0)


def params(mib):
    return pltpu.CompilerParams(vmem_limit_bytes=mib * 1024 * 1024)


def shape(dims, kind):
    return jax.ShapeDtypeStruct(dims, kind)


def pack(info, query_rows, key_rows, value_rows):
    width = HEADS * ATT_DIM
    rows = [ATT_DIM, 2 * ATT_DIM] + [3 * ATT_DIM] * 3
    return pl.pallas_call(
        pack_kernel,
        out_shape=[shape((count, TOK), BF16) for count in rows],
        in_specs=[SMEM] + [ANY] * 3,
        out_specs=vmem(len(rows)),
        scratch_shapes=[
            pltpu.VMEM((3, TOK, width), BF16),
            pltpu.VMEM((3, width, TOK), BF16),
            pltpu.SemaphoreType.DMA((3,)),
        ],
        compiler_params=params(60),
    )(info, query_rows, key_rows, value_rows)


def attend(stage, info, *operands):
    slots = (4, 3, 1)[stage]
    keys, values = (slots, 2 * TOK, ATT_DIM), (slots, ATT_DIM, 2 * TOK)
    state = [shape((4, ATT_DIM, TOK), F32), shape((4, 16, TOK), F32)]
    queries = pltpu.VMEM((4, ATT_DIM, TOK), BF16)
    mark = [shape((8, 128), F32)]
    if stage == 0:
        out = state + [shape(keys, BF16), shape(values, BF16)] + mark
        scratch = [queries]
    elif stage == 1:
        out = state + mark
        scratch = [pltpu.VMEM(keys, BF16), pltpu.VMEM(values, BF16), queries]
    else:
        out = [shape((ATT_DIM, TOK), BF16)] * 4 + mark
        scratch = [pltpu.VMEM(keys, BF16), pltpu.VMEM(values, BF16), queries]
        scratch += [pltpu.VMEM((4, ATT_DIM, TOK), F32), queries]
    return pl.pallas_call(
        functools.partial(attend_kernel, stage),
        out_shape=out,
        in_specs=[SMEM] + vmem(len(operands)),
        out_specs=vmem(len(out)),
        scratch_shapes=scratch,
        compiler_params=params(24),
        cost_estimate=SMALL,
    )(info, *operands)


def unpack(info, mark, pieces):
    width = HEADS * ATT_DIM
    return pl.pallas_call(
        unpack_kernel,
        out_shape=shape((TOK, width), BF16),
        in_specs=[SMEM, ANY] + vmem(4),
        out_specs=vmem(1)[0],
        scratch_shapes=[pltpu.VMEM((width, TOK), BF16)],
        compiler_params=params(40),
    )(info, mark, *pieces)


def ssm_local(ssm_inputs, write_t, read_t, step_t, rate, gain):
    tokens, width = ssm_inputs.shape
    heads = step_t.shape[0]
    return pl.pallas_call(
        ssm_local_kernel,
        out_shape=[
            shape((tokens, width), F32),
            shape((HELD, width), F32),
            shape((SENT, width), BF16),
            shape((tokens, heads), F32),
        ],
        in_specs=vmem(6),
        out_specs=vmem(4),
        compiler_params=params(40),
        cost_estimate=SMALL,
    )(ssm_inputs, write_t, read_t, step_t, rate, gain)


def ssm_merge(level, info, got, total, before):
    held, sent = shape(total.shape, F32), shape(got.shape, BF16)
    return pl.pallas_call(
        functools.partial(ssm_merge_kernel, level),
        out_shape=[held, held, sent],
        in_specs=[SMEM] + vmem(3),
        out_specs=vmem(3),
        compiler_params=params(40),
        cost_estimate=SMALL,
    )(info, got, total, before)


def ssm_carry(count, state, mixed, cum, read_t, gate):
    tokens, width = mixed.shape
    return pl.pallas_call(
        ssm_carry_kernel,
        out_shape=[shape((tokens, width), F32), shape((8 * count, tokens), F32)],
        in_specs=vmem(5),
        out_specs=vmem(2),
        compiler_params=params(40),
        cost_estimate=SMALL,
    )(state, mixed, cum, read_t, gate)


def on_device(
    query_rows,
    key_rows,
    value_rows,
    ssm_inputs,
    ssm_gate,
    write_vecs,
    read_vecs,
    step_raw,
    decay_log,
    skip_gain,
    norm_gain,
):
    me = lax.axis_index("ctx")
    y, x, core = me >> 3, (me >> 1) & 3, me & 1
    info = jnp.stack([y * 2 + (x >> 1), (x ^ (x >> 1)) & 1, core, me]).astype(jnp.int32)
    tie = lax.optimization_barrier

    q_own, kv_own, all_1, all_2, all_3 = pack(info, query_rows, key_rows, value_rows)
    here, near, from_core, near_core = [None] * 4, [None] * 4, [None] * 4, [None] * 4
    here[1], here[2] = head_swap(all_1, 1), head_swap(all_2, 2)
    near[0] = class_swap(kv_own)
    from_core[0] = core_swap(kv_own)

    from_core[0], ssm_inputs = tie((from_core[0], ssm_inputs))
    read_t = read_vecs.T
    mixed, total, sent, cum = ssm_local(
        ssm_inputs, write_vecs.T, read_t, step_raw.T, decay_log[None, :], skip_gain[None, :]
    )
    before = jnp.zeros_like(total)
    total, before, sent = ssm_merge(0, info, core_swap(sent), total, before)
    got = class_swap(sent)
    near[0], sent = tie((near[0], sent))
    near_core[0] = core_swap(near[0])

    total, before, sent = ssm_merge(1, info, got, total, before)
    got = block_swap(sent, 4)
    here[1], here[2], near_core[0], got = tie((here[1], here[2], near_core[0], got))
    for r in (1, 2):
        kv = here[r][ATT_DIM:]
        near[r] = class_swap(kv)
        from_core[r] = core_swap(kv)
    total, before, sent = ssm_merge(2, info, got, total, before)
    got = block_swap(sent, 8)
    got, all_3 = tie((got, all_3))
    here[3] = head_swap(all_3, 3)
    total, before, sent = ssm_merge(3, info, got, total, before)
    count = lax.axis_size("tp")
    gated, squares = ssm_carry(count, before, mixed, cum, read_t, ssm_gate)
    *state, ks, vs, mark = attend(
        0, info, q_own, here[1], here[2], kv_own, *from_core[:3], near[0], near_core[0]
    )
    squares, mark = tie((squares, mark))
    squares = lax.all_to_all(squares, "tp", 0, 0, tiled=True).reshape(count, 8, TOK)

    here[3], near[1], near[2], squares, mark = tie((here[3], near[1], near[2], squares, mark))
    kv = here[3][ATT_DIM:]
    near[3] = class_swap(kv)
    from_core[3] = core_swap(kv)
    near_core[1], near_core[2] = core_swap(near[1]), core_swap(near[2])
    queries = (q_own, here[1], here[2], here[3])
    *state, mark = attend(
        1, info, *queries, from_core[3], near[1], near_core[1], near[2], near_core[2], mark, ks, vs, *state
    )

    near[3], mark = tie((near[3], mark))
    near_core[3] = core_swap(near[3])
    *results, mark = attend(2, info, *queries, near[3], near_core[3], mark, *state)
    back = [results[0]] + [head_swap(results[r], r) for r in range(1, 4)]
    gated, mark = tie((gated, mark))
    factor = lax.rsqrt(jnp.sum(squares[:, 0], axis=0) / SSM_WIDTH + 1e-05)
    mixer_out = (gated * factor[:, None] * norm_gain[None, :]).astype(BF16)
    return (unpack(info, mark, back), mixer_out)


def solution(mesh):
    placed = (
        P("ctx", "tp"),
        P("ctx", "tp"),
        P("ctx", "tp"),
        P("ctx", "tp"),
        P("ctx", "tp"),
        P("ctx", None),
        P("ctx", None),
        P("ctx", "tp"),
        P("tp"),
        P("tp"),
        P("tp"),
    )
    return jax.shard_map(
        on_device,
        mesh=mesh,
        in_specs=placed,
        out_specs=(P("ctx", "tp"), P("ctx", "tp")),
        check_vma=False,
    )
```

```python
import functools
import math

import jax
import jax.numpy as jnp
from jax import lax
from jax.experimental import pallas as pl
from jax.experimental.pallas import tpu as pltpu
from jax.sharding import PartitionSpec as P

ATT_DIM = 224
SSM_DIM = 64
STATE_DIM = 64
SSM_WIDTH = 7168
TOK = 512
HEADS = 4
CTX = 16
HALF = 256
LOG2E = math.log2(math.e)
F32 = jnp.float32
BF16 = jnp.bfloat16


def exchanged(i, r):
    y, x, c = i >> 3, (i >> 1) & 3, i & 1
    if r & 1:
        x = 3 - x
    if r & 2:
        y = 1 - y
    return y * 8 + x * 2 + c


def head_swap(value, r):
    return lax.ppermute(value, "ctx", [(i, exchanged(i, r)) for i in range(CTX)])


def class_swap(value):
    return lax.ppermute(value, "ctx", [(i, i ^ 2) for i in range(CTX)])


def core_swap(value):
    return lax.ppermute(value, "ctx", [(i, i ^ 1) for i in range(CTX)])


def block_swap(value, step):
    return lax.ppermute(value, "ctx", [(i, i ^ step) for i in range(CTX)])


def step_swap(value, step):
    return lax.ppermute(value, "tp", [(i, i ^ step) for i in range(8)])


def head_rows(head):
    return pl.ds(pl.multiple_of(head * ATT_DIM, 16), ATT_DIM)


Q_ROWS = slice(0, ATT_DIM)
K_ROWS = slice(ATT_DIM, 2 * ATT_DIM)
V_ROWS = slice(2 * ATT_DIM, 3 * ATT_DIM)


def pack_kernel(info, q_in, k_in, v_in, q_own, kv_own, all_1, all_2, all_3, raw, rows_ref, sems):
    copies = [pltpu.make_async_copy(src, raw.at[i], sems.at[i]) for i, src in enumerate((q_in, k_in, v_in))]
    for copy in copies:
        copy.start()
    for i, (out, first) in enumerate(((q_own, 0), (kv_own, 0), (kv_own, ATT_DIM))):
        copies[i].wait()
        rows_ref[i] = raw[i].T
        out[first : first + ATT_DIM, :] = rows_ref[i, head_rows(info[0]), :]
        for r, away in ((1, all_1), (2, all_2), (3, all_3)):
            away[i * ATT_DIM : (i + 1) * ATT_DIM, :] = rows_ref[i, head_rows(info[0] ^ r), :]


def unpack_kernel(info, _, *refs):
    pieces, out_ref, rows_ref = refs[:4], refs[4], refs[5]
    for r in range(4):
        rows_ref[head_rows(info[0] ^ r), :] = pieces[r][...]
    out_ref[...] = rows_ref[...].T


def attend_kernel(stage, info, *refs):
    hid, kind, core = info[0], info[1], info[2]
    scale = ATT_DIM ** (-0.5) * LOG2E
    if stage == 0:
        q_in, (kv_own, core_0, core_1, core_2, near_0, near_core_0), refs = refs[:3], refs[3:9], refs[9:]
        acc, stats_ref, ks, vs, mark, qs = refs
        pieces = [(0, 0, kv_own, 0), (1, 0, q_in[1], ATT_DIM), (2, 0, q_in[2], ATT_DIM)]
        pieces += [(0, 1, core_0, 0), (1, 1, core_1, 0), (2, 1, core_2, 0)]
        pieces += [(3, 0, near_0, 0), (3, 1, near_core_0, 0)]
    elif stage == 1:
        q_in, (core_3, near_1, near_core_1, near_2, near_core_2, _), refs = refs[:4], refs[4:10], refs[10:]
        ks_early, vs_early, acc_in, stats_in, acc, stats_ref, mark, ks, vs, qs = refs
        pieces = [(0, 0, q_in[3], ATT_DIM), (0, 1, core_3, 0)]
        pieces += [(1, 0, near_1, 0), (1, 1, near_core_1, 0), (2, 0, near_2, 0), (2, 1, near_core_2, 0)]
    else:
        q_in, (near_3, near_core_3, _), refs = refs[:4], refs[4:7], refs[7:]
        acc_in, stats_in, *o_out, mark, ks, vs, qs, acc, os = refs
        pieces = [(0, 0, near_3, 0), (0, 1, near_core_3, 0)]
    for slot, other, piece, first in pieces:
        start = pl.multiple_of((core ^ other) * TOK, TOK)
        ks[slot, pl.ds(start, TOK), :] = piece[first : first + ATT_DIM, :].T
        vs[slot, :, pl.ds(start, TOK)] = piece[first + ATT_DIM : first + 2 * ATT_DIM, :]
    for r, queries in enumerate(q_in):
        qs[r] = queries[Q_ROWS, :]
    mark[...] = jnp.zeros_like(mark)

    def one_queries(r, carry):
        chip = hid ^ r

        def visit(keys, values, stats, masked):
            lanes = [slice(half * HALF, (half + 1) * HALF) for half in range(2)]
            scores = [
                jnp.dot(keys, qs[r, :, lanes[half]], preferred_element_type=F32) for half in range(2)
            ]
            new_stats, low, shrinks = [], [], []
            for half in range(2):
                (top, total), s = stats[half], scores[half]
                if masked:
                    k_pos = lax.broadcasted_iota(jnp.int32, s.shape, 0)
                    q_pos = lax.broadcasted_iota(jnp.int32, s.shape, 1) + half * HALF
                    s = jnp.where(k_pos <= q_pos, s, -1e30)
                new_top = jnp.maximum(top, jnp.max(s, axis=0, keepdims=True))
                p = jnp.exp2((s - new_top) * scale)
                shrink = jnp.exp2((top - new_top) * scale)
                total = total * shrink + jnp.sum(p, axis=0, keepdims=True)
                new_stats.append((new_top, total))
                low.append(p.astype(BF16))
                shrinks.append(shrink)
            for half in range(2):
                acc[r, :, lanes[half]] = acc[r, :, lanes[half]] * shrinks[half] + jnp.dot(
                    values, low[half], preferred_element_type=F32
                )
            return tuple(new_stats)

        def sweep(count, key_ref, value_ref, seen, stats):
            def one(k, now):
                times = jnp.where(seen(k), 1, 0)
                return lax.fori_loop(
                    0, times, lambda _, inner: visit(key_ref[k], value_ref[k], inner, False), now
                )

            return lax.fori_loop(0, count, one, stats)

        def near_seen(k):
            limit = jnp.where(kind == 0, ((chip + 1) >> 1) * 2, (chip >> 1) * 2 + 1)
            return (hid ^ k) < limit

        def diagonal(slot, stats):
            def part(start, now, masked):
                start = pl.multiple_of(start, TOK)
                return visit(ks[slot, pl.ds(start, TOK), :], vs[slot, :, pl.ds(start, TOK)], now, masked)

            stats = lax.fori_loop(0, core, lambda _, now: part(0, now, False), stats)
            return part(core * TOK, stats, True)

        if stage == 0:
            acc[r] = jnp.zeros((ATT_DIM, TOK), F32)
            first = (jnp.full((1, HALF), -1e30, F32), jnp.zeros((1, HALF), F32))
            stats = (first, first)
        else:
            acc[r] = acc_in[r]
            stats = tuple(
                (
                    stats_in[r, 0:1, half * HALF : (half + 1) * HALF],
                    stats_in[r, 8:9, half * HALF : (half + 1) * HALF],
                )
                for half in range(2)
            )

        if stage == 0:

            def early(now):
                now = sweep(4, ks, vs, lambda k: jnp.where(k == 3, near_seen(0), (hid ^ k) < chip), now)
                return diagonal(r, now)

            stats = lax.fori_loop(0, jnp.where(r == 3, 0, 1), lambda _, now: early(now), stats)
        elif stage == 1:
            last = jnp.where(r == 3, 1, 0)
            stats = sweep(
                4 * last, ks_early, vs_early, lambda k: jnp.where(k == 3, near_seen(0), (hid ^ k) < chip), stats
            )
            stats = sweep(3, ks, vs, lambda k: jnp.where(k == 0, (hid ^ 3) < chip, near_seen(k)), stats)
            stats = lax.fori_loop(0, last, lambda _, now: diagonal(0, now), stats)
        else:
            stats = sweep(1, ks, vs, lambda k: near_seen(3), stats)

        for half in range(2):
            lanes = slice(half * HALF, (half + 1) * HALF)
            if stage == 2:
                os[r, :, lanes] = (acc[r, :, lanes] / stats[half][1]).astype(BF16)
            else:
                stats_ref[r, 0:8, lanes] = jnp.broadcast_to(stats[half][0], (8, HALF))
                stats_ref[r, 8:16, lanes] = jnp.broadcast_to(stats[half][1], (8, HALF))
        return carry

    lax.fori_loop(0, 4, one_queries, 0)
    if stage == 2:
        for r in range(4):
            o_out[r][...] = os[r]


def pair_of(low, columns, h):
    return jnp.where(low, columns[:, h : h + 1], columns[:, h + 1 : h + 2])


def softplus(v):
    return jnp.maximum(v, 0.0) + jnp.log1p(jnp.exp(-jnp.abs(v)))


SPAN = slice(STATE_DIM, STATE_DIM + 8)
SPAN_LOW = slice(STATE_DIM + 8, STATE_DIM + 16)
HELD, SENT = STATE_DIM + 8, STATE_DIM + 16


def send_state(pay_ref, lanes, state, span):
    span_high = span.astype(BF16)
    pay_ref[0:STATE_DIM, lanes] = state.astype(BF16)
    pay_ref[STATE_DIM:SENT, lanes] = jnp.concatenate(
        [span_high.astype(F32), span - span_high.astype(F32)], axis=0
    ).astype(BF16)


def ssm_local_kernel(
    x_ref, write_t_ref, read_t_ref, step_t_ref, rate_ref, gain_ref, out_ref, total_ref, pay_ref, cum_ref
):
    heads = step_t_ref.shape[0]
    high = lax.Precision.HIGHEST
    row = lax.broadcasted_iota(jnp.int32, (TOK, TOK), 0)
    col = lax.broadcasted_iota(jnp.int32, (TOK, TOK), 1)
    rate = jnp.broadcast_to(-jnp.exp(rate_ref[...]) * LOG2E, (8, heads)).T[:, 0:1]
    step_t = softplus(step_t_ref[...])
    cum_t = jnp.dot(
        rate * step_t, jnp.where(row <= col, 1.0, 0.0), precision=high, preferred_element_type=F32
    )
    key_row = jnp.log2(step_t) - cum_t
    cum = cum_t.T
    step = step_t.T
    cum_ref[...] = cum
    last = cum[TOK - 1 : TOK, :]
    tail = jnp.exp2(last - cum) * step
    gain = gain_ref[...]

    near = lax.dot_general(
        read_t_ref[...], write_t_ref[...], (((0,), (0,)), ((), ())), preferred_element_type=F32
    )
    near = jnp.where(col <= row, near, 0.0)
    low = lax.broadcasted_iota(jnp.int32, (1, 128), 1) < SSM_DIM
    for h in range(0, heads, 2):
        lanes = slice(h * SSM_DIM, (h + 2) * SSM_DIM)
        x_pair = x_ref[:, lanes]
        x_f = x_pair.astype(F32)
        weighted = (x_f * pair_of(low, tail, h)).astype(BF16)
        state = jnp.dot(write_t_ref[...], weighted, preferred_element_type=F32)
        span = jnp.broadcast_to(pair_of(low, last, h), (8, 128))
        total_ref[0:STATE_DIM, lanes] = state
        total_ref[SPAN, lanes] = span
        send_state(pay_ref, lanes, state, span)
        for t in range(2):
            t_rows = slice(t * HALF, (t + 1) * HALF)
            both = []
            for k in range(2):
                total = None
                for s in range(t + 1):
                    s_rows = slice(s * HALF, (s + 1) * HALF)
                    weights = (
                        jnp.exp2(cum[t_rows, h + k : h + k + 1] + key_row[h + k : h + k + 1, s_rows])
                        * near[t_rows, s_rows]
                    )
                    part = jnp.dot(weights.astype(BF16), x_pair[s_rows, :], preferred_element_type=F32)
                    total = part if total is None else total + part
                both.append(total)
            out_ref[t_rows, lanes] = (
                jnp.where(low, both[0], both[1]) + pair_of(low, gain, h) * x_f[t_rows, :]
            )


def ssm_merge_kernel(level, info, got_ref, total_ref, before_ref, total_out, before_out, pay_ref):
    later = ((info[3] >> level) & 1).astype(F32)
    got = got_ref[0:STATE_DIM, :].astype(F32)
    got_span = got_ref[STATE_DIM:SENT, :].astype(F32)
    got_span = got_span[0:8, :] + got_span[8:16, :]
    total, total_span = total_ref[0:STATE_DIM, :], total_ref[SPAN, :]
    before, before_span = before_ref[0:STATE_DIM, :], before_ref[SPAN, :]
    before_out[0:STATE_DIM, :] = before + later * (got * jnp.exp2(before_span[0:1, :]))
    before_out[SPAN, :] = before_span + later * got_span
    after_got = got * jnp.exp2(total_span[0:1, :]) + total
    after_total = total * jnp.exp2(got_span[0:1, :]) + got
    total = later * after_got + (1.0 - later) * after_total
    span = total_span + got_span
    total_out[0:STATE_DIM, :] = total
    total_out[SPAN, :] = span
    send_state(pay_ref, slice(None), total, span)


def ssm_carry_kernel(state_ref, mixed_ref, cum_ref, read_t_ref, gate_ref, gated_ref, square_ref):
    heads = cum_ref.shape[1]
    state = state_ref[0:STATE_DIM, :]
    state_high = state.astype(BF16)
    state_low = (state - state_high.astype(F32)).astype(BF16)
    reach = jnp.exp2(cum_ref[...])
    read = read_t_ref[...].T
    low = lax.broadcasted_iota(jnp.int32, (1, 128), 1) < SSM_DIM
    squares = jnp.zeros((TOK, 128), F32)
    for h in range(0, heads, 2):
        lanes = slice(h * SSM_DIM, (h + 2) * SSM_DIM)
        carried = jnp.dot(read, state_high[:, lanes], preferred_element_type=F32)
        carried = carried + jnp.dot(read, state_low[:, lanes], preferred_element_type=F32)
        mixed = mixed_ref[:, lanes] + carried * pair_of(low, reach, h)
        gate = gate_ref[:, lanes].astype(F32)
        gated = mixed * (gate / (1.0 + jnp.exp(-gate)))
        gated_ref[:, lanes] = gated
        squares = squares + gated * gated
    square_ref[...] = jnp.sum(squares.T, axis=0, keepdims=True)


def vmem(count):
    return [pl.BlockSpec(memory_space=pltpu.VMEM)] * count


SMEM = pl.BlockSpec(memory_space=pltpu.SMEM)
ANY = pl.BlockSpec(memory_space=pl.ANY)


SMALL = pl.CostEstimate(flops=1000, bytes_accessed=1000, transcendentals=0)


def params(mib):
    return pltpu.CompilerParams(vmem_limit_bytes=mib * 1024 * 1024)


def shape(dims, kind):
    return jax.ShapeDtypeStruct(dims, kind)


def pack(info, query_rows, key_rows, value_rows):
    width = HEADS * ATT_DIM
    rows = [ATT_DIM, 2 * ATT_DIM] + [3 * ATT_DIM] * 3
    return pl.pallas_call(
        pack_kernel,
        out_shape=[shape((count, TOK), BF16) for count in rows],
        in_specs=[SMEM] + [ANY] * 3,
        out_specs=vmem(len(rows)),
        scratch_shapes=[
            pltpu.VMEM((3, TOK, width), BF16),
            pltpu.VMEM((3, width, TOK), BF16),
            pltpu.SemaphoreType.DMA((3,)),
        ],
        compiler_params=params(60),
    )(info, query_rows, key_rows, value_rows)


def attend(stage, info, *operands):
    slots = (4, 3, 1)[stage]
    keys, values = (slots, 2 * TOK, ATT_DIM), (slots, ATT_DIM, 2 * TOK)
    state = [shape((4, ATT_DIM, TOK), F32), shape((4, 16, TOK), F32)]
    queries = pltpu.VMEM((4, ATT_DIM, TOK), BF16)
    mark = [shape((8, 128), F32)]
    if stage == 0:
        out = state + [shape(keys, BF16), shape(values, BF16)] + mark
        scratch = [queries]
    elif stage == 1:
        out = state + mark
        scratch = [pltpu.VMEM(keys, BF16), pltpu.VMEM(values, BF16), queries]
    else:
        out = [shape((ATT_DIM, TOK), BF16)] * 4 + mark
        scratch = [pltpu.VMEM(keys, BF16), pltpu.VMEM(values, BF16), queries]
        scratch += [pltpu.VMEM((4, ATT_DIM, TOK), F32), queries]
    return pl.pallas_call(
        functools.partial(attend_kernel, stage),
        out_shape=out,
        in_specs=[SMEM] + vmem(len(operands)),
        out_specs=vmem(len(out)),
        scratch_shapes=scratch,
        compiler_params=params(24),
        cost_estimate=SMALL,
    )(info, *operands)


def unpack(info, mark, pieces):
    width = HEADS * ATT_DIM
    return pl.pallas_call(
        unpack_kernel,
        out_shape=shape((TOK, width), BF16),
        in_specs=[SMEM, ANY] + vmem(4),
        out_specs=vmem(1)[0],
        scratch_shapes=[pltpu.VMEM((width, TOK), BF16)],
        compiler_params=params(40),
    )(info, mark, *pieces)


def ssm_local(ssm_inputs, write_t, read_t, step_t, rate, gain):
    tokens, width = ssm_inputs.shape
    heads = step_t.shape[0]
    return pl.pallas_call(
        ssm_local_kernel,
        out_shape=[
            shape((tokens, width), F32),
            shape((HELD, width), F32),
            shape((SENT, width), BF16),
            shape((tokens, heads), F32),
        ],
        in_specs=vmem(6),
        out_specs=vmem(4),
        compiler_params=params(40),
        cost_estimate=SMALL,
    )(ssm_inputs, write_t, read_t, step_t, rate, gain)


def ssm_merge(level, info, got, total, before):
    held, sent = shape(total.shape, F32), shape(got.shape, BF16)
    return pl.pallas_call(
        functools.partial(ssm_merge_kernel, level),
        out_shape=[held, held, sent],
        in_specs=[SMEM] + vmem(3),
        out_specs=vmem(3),
        compiler_params=params(40),
        cost_estimate=SMALL,
    )(info, got, total, before)


def ssm_carry(state, mixed, cum, read_t, gate):
    tokens, width = mixed.shape
    return pl.pallas_call(
        ssm_carry_kernel,
        out_shape=[shape((tokens, width), F32), shape((1, tokens), F32)],
        in_specs=vmem(5),
        out_specs=vmem(2),
        compiler_params=params(40),
        cost_estimate=SMALL,
    )(state, mixed, cum, read_t, gate)


def on_device(
    query_rows,
    key_rows,
    value_rows,
    ssm_inputs,
    ssm_gate,
    write_vecs,
    read_vecs,
    step_raw,
    decay_log,
    skip_gain,
    norm_gain,
):
    me = lax.axis_index("ctx")
    y, x, core = me >> 3, (me >> 1) & 3, me & 1
    info = jnp.stack([y * 2 + (x >> 1), (x ^ (x >> 1)) & 1, core, me]).astype(jnp.int32)
    tie = lax.optimization_barrier

    q_own, kv_own, all_1, all_2, all_3 = pack(info, query_rows, key_rows, value_rows)
    here, near, from_core, near_core = [None] * 4, [None] * 4, [None] * 4, [None] * 4
    here[1], here[2] = head_swap(all_1, 1), head_swap(all_2, 2)
    near[0] = class_swap(kv_own)
    from_core[0] = core_swap(kv_own)

    from_core[0], ssm_inputs = tie((from_core[0], ssm_inputs))
    read_t = read_vecs.T
    mixed, total, sent, cum = ssm_local(
        ssm_inputs, write_vecs.T, read_t, step_raw.T, decay_log[None, :], skip_gain[None, :]
    )
    before = jnp.zeros_like(total)
    total, before, sent = ssm_merge(0, info, core_swap(sent), total, before)
    got = class_swap(sent)

    near[0], sent = tie((near[0], sent))
    near_core[0] = core_swap(near[0])

    here[1], here[2], near_core[0], got = tie((here[1], here[2], near_core[0], got))
    for r in (1, 2):
        kv = here[r][ATT_DIM:]
        near[r] = class_swap(kv)
        from_core[r] = core_swap(kv)
    total, before, sent = ssm_merge(1, info, got, total, before)
    got, all_3 = tie((block_swap(sent, 4), all_3))
    here[3] = head_swap(all_3, 3)
    total, before, sent = ssm_merge(2, info, got, total, before)
    got = block_swap(sent, 8)
    *state, ks, vs, mark = attend(
        0, info, q_own, here[1], here[2], kv_own, *from_core[:3], near[0], near_core[0]
    )

    here[3], mark = tie((here[3], mark))
    kv = here[3][ATT_DIM:]
    near[3] = class_swap(kv)
    from_core[3] = core_swap(kv)
    from_core[3], near[1], near[2], got, mark = tie((from_core[3], near[1], near[2], got, mark))
    near_core[1], near_core[2] = core_swap(near[1]), core_swap(near[2])
    queries = (q_own, here[1], here[2], here[3])
    *state, mark = attend(
        1, info, *queries, from_core[3], near[1], near_core[1], near[2], near_core[2], mark, ks, vs, *state
    )

    near[3], got, mark = tie((near[3], got, mark))
    near_core[3] = core_swap(near[3])
    total, before, sent = ssm_merge(3, info, got, total, before)
    gated, squares = ssm_carry(before, mixed, cum, read_t, ssm_gate)
    gated, squares, mark = tie((gated, squares, mark))
    others = step_swap(squares, 4)
    *results, mark = attend(2, info, *queries, near[3], near_core[3], mark, *state)
    back = [results[0]] + [head_swap(results[r], r) for r in range(1, 4)]
    others, mark = tie((others, mark))
    squares = squares + others
    for step in (1, 2):
        squares = squares + step_swap(squares, step)
    *back, squares = tie((*back, squares))
    factor = lax.rsqrt(squares.reshape(TOK) / SSM_WIDTH + 1e-05)
    mixer_out = (gated * factor[:, None] * norm_gain[None, :]).astype(BF16)
    return (unpack(info, mark, back), mixer_out)


def solution(mesh):
    placed = (
        P("ctx", "tp"),
        P("ctx", "tp"),
        P("ctx", "tp"),
        P("ctx", "tp"),
        P("ctx", "tp"),
        P("ctx", None),
        P("ctx", None),
        P("ctx", "tp"),
        P("tp"),
        P("tp"),
        P("tp"),
    )
    return jax.shard_map(
        on_device,
        mesh=mesh,
        in_specs=placed,
        out_specs=(P("ctx", "tp"), P("ctx", "tp")),
        check_vma=False,
    )
```

```python
import functools
import math

import jax
import jax.numpy as jnp
from jax import lax
from jax.experimental import pallas as pl
from jax.experimental.pallas import tpu as pltpu
from jax.sharding import PartitionSpec as P

ATT_DIM = 224
SSM_DIM = 64
STATE_DIM = 64
SSM_WIDTH = 7168
TOK = 512
HEADS = 4
CTX = 16
HALF = 256
LOG2E = math.log2(math.e)
F32 = jnp.float32
BF16 = jnp.bfloat16


def exchanged(i, r):
    y, x, c = i >> 3, (i >> 1) & 3, i & 1
    if r & 1:
        x = 3 - x
    if r & 2:
        y = 1 - y
    return y * 8 + x * 2 + c


def head_swap(value, r):
    return lax.ppermute(value, "ctx", [(i, exchanged(i, r)) for i in range(CTX)])


def class_swap(value):
    return lax.ppermute(value, "ctx", [(i, i ^ 2) for i in range(CTX)])


def core_swap(value):
    return lax.ppermute(value, "ctx", [(i, i ^ 1) for i in range(CTX)])


def block_swap(value, step):
    return lax.ppermute(value, "ctx", [(i, i ^ step) for i in range(CTX)])


def step_swap(value, step):
    return lax.ppermute(value, "tp", [(i, i ^ step) for i in range(8)])


def head_rows(head):
    return pl.ds(pl.multiple_of(head * ATT_DIM, 16), ATT_DIM)


Q_ROWS = slice(0, ATT_DIM)
K_ROWS = slice(ATT_DIM, 2 * ATT_DIM)
V_ROWS = slice(2 * ATT_DIM, 3 * ATT_DIM)


def pack_kernel(info, q_in, k_in, v_in, q_own, kv_own, all_1, all_2, all_3, raw, rows_ref, sems):
    copies = [pltpu.make_async_copy(src, raw.at[i], sems.at[i]) for i, src in enumerate((q_in, k_in, v_in))]
    for copy in copies:
        copy.start()
    for i, (out, first) in enumerate(((q_own, 0), (kv_own, 0), (kv_own, ATT_DIM))):
        copies[i].wait()
        rows_ref[i] = raw[i].T
        out[first : first + ATT_DIM, :] = rows_ref[i, head_rows(info[0]), :]
        for r, away in ((1, all_1), (2, all_2), (3, all_3)):
            away[i * ATT_DIM : (i + 1) * ATT_DIM, :] = rows_ref[i, head_rows(info[0] ^ r), :]


def unpack_kernel(info, _, *refs):
    pieces, out_ref, rows_ref = refs[:4], refs[4], refs[5]
    for r in range(4):
        rows_ref[head_rows(info[0] ^ r), :] = pieces[r][...]
    out_ref[...] = rows_ref[...].T


def attend_kernel(stage, info, *refs):
    hid, kind, core = info[0], info[1], info[2]
    scale = ATT_DIM ** (-0.5) * LOG2E
    if stage == 0:
        q_in, (kv_own, core_0, core_1, core_2, near_0, near_core_0), refs = refs[:3], refs[3:9], refs[9:]
        acc, stats_ref, ks, vs, mark, qs = refs
        pieces = [(0, 0, kv_own, 0), (1, 0, q_in[1], ATT_DIM), (2, 0, q_in[2], ATT_DIM)]
        pieces += [(0, 1, core_0, 0), (1, 1, core_1, 0), (2, 1, core_2, 0)]
        pieces += [(3, 0, near_0, 0), (3, 1, near_core_0, 0)]
    elif stage == 1:
        q_in, (core_3, near_1, near_core_1, near_2, near_core_2, _), refs = refs[:4], refs[4:10], refs[10:]
        ks_early, vs_early, acc_in, stats_in, acc, stats_ref, mark, ks, vs, qs = refs
        pieces = [(0, 0, q_in[3], ATT_DIM), (0, 1, core_3, 0)]
        pieces += [(1, 0, near_1, 0), (1, 1, near_core_1, 0), (2, 0, near_2, 0), (2, 1, near_core_2, 0)]
    else:
        q_in, (near_3, near_core_3, _), refs = refs[:4], refs[4:7], refs[7:]
        acc_in, stats_in, *o_out, mark, ks, vs, qs, acc, os = refs
        pieces = [(0, 0, near_3, 0), (0, 1, near_core_3, 0)]
    for slot, other, piece, first in pieces:
        start = pl.multiple_of((core ^ other) * TOK, TOK)
        ks[slot, pl.ds(start, TOK), :] = piece[first : first + ATT_DIM, :].T
        vs[slot, :, pl.ds(start, TOK)] = piece[first + ATT_DIM : first + 2 * ATT_DIM, :]
    for r, queries in enumerate(q_in):
        qs[r] = queries[Q_ROWS, :]
    mark[...] = jnp.zeros_like(mark)

    def one_queries(r, carry):
        chip = hid ^ r

        def visit(keys, values, stats, masked):
            lanes = [slice(half * HALF, (half + 1) * HALF) for half in range(2)]
            scores = [
                jnp.dot(keys, qs[r, :, lanes[half]], preferred_element_type=F32) for half in range(2)
            ]
            new_stats, low, shrinks = [], [], []
            for half in range(2):
                (top, total), s = stats[half], scores[half]
                if masked:
                    k_pos = lax.broadcasted_iota(jnp.int32, s.shape, 0)
                    q_pos = lax.broadcasted_iota(jnp.int32, s.shape, 1) + half * HALF
                    s = jnp.where(k_pos <= q_pos, s, -1e30)
                new_top = jnp.maximum(top, jnp.max(s, axis=0, keepdims=True))
                p = jnp.exp2((s - new_top) * scale)
                shrink = jnp.exp2((top - new_top) * scale)
                total = total * shrink + jnp.sum(p, axis=0, keepdims=True)
                new_stats.append((new_top, total))
                low.append(p.astype(BF16))
                shrinks.append(shrink)
            for half in range(2):
                acc[r, :, lanes[half]] = acc[r, :, lanes[half]] * shrinks[half] + jnp.dot(
                    values, low[half], preferred_element_type=F32
                )
            return tuple(new_stats)

        def sweep(count, key_ref, value_ref, seen, stats):
            def one(k, now):
                times = jnp.where(seen(k), 1, 0)
                return lax.fori_loop(
                    0, times, lambda _, inner: visit(key_ref[k], value_ref[k], inner, False), now
                )

            return lax.fori_loop(0, count, one, stats)

        def near_seen(k):
            limit = jnp.where(kind == 0, ((chip + 1) >> 1) * 2, (chip >> 1) * 2 + 1)
            return (hid ^ k) < limit

        def diagonal(slot, stats):
            def part(start, now, masked):
                start = pl.multiple_of(start, TOK)
                return visit(ks[slot, pl.ds(start, TOK), :], vs[slot, :, pl.ds(start, TOK)], now, masked)

            stats = lax.fori_loop(0, core, lambda _, now: part(0, now, False), stats)
            return part(core * TOK, stats, True)

        if stage == 0:
            acc[r] = jnp.zeros((ATT_DIM, TOK), F32)
            first = (jnp.full((1, HALF), -1e30, F32), jnp.zeros((1, HALF), F32))
            stats = (first, first)
        else:
            acc[r] = acc_in[r]
            stats = tuple(
                (
                    stats_in[r, 0:1, half * HALF : (half + 1) * HALF],
                    stats_in[r, 8:9, half * HALF : (half + 1) * HALF],
                )
                for half in range(2)
            )

        if stage == 0:

            def early(now):
                now = sweep(4, ks, vs, lambda k: jnp.where(k == 3, near_seen(0), (hid ^ k) < chip), now)
                return diagonal(r, now)

            stats = lax.fori_loop(0, jnp.where(r == 3, 0, 1), lambda _, now: early(now), stats)
        elif stage == 1:
            last = jnp.where(r == 3, 1, 0)
            stats = sweep(
                4 * last, ks_early, vs_early, lambda k: jnp.where(k == 3, near_seen(0), (hid ^ k) < chip), stats
            )
            stats = sweep(3, ks, vs, lambda k: jnp.where(k == 0, (hid ^ 3) < chip, near_seen(k)), stats)
            stats = lax.fori_loop(0, last, lambda _, now: diagonal(0, now), stats)
        else:
            stats = sweep(1, ks, vs, lambda k: near_seen(3), stats)

        for half in range(2):
            lanes = slice(half * HALF, (half + 1) * HALF)
            if stage == 2:
                os[r, :, lanes] = (acc[r, :, lanes] / stats[half][1]).astype(BF16)
            else:
                stats_ref[r, 0:8, lanes] = jnp.broadcast_to(stats[half][0], (8, HALF))
                stats_ref[r, 8:16, lanes] = jnp.broadcast_to(stats[half][1], (8, HALF))
        return carry

    lax.fori_loop(0, 4, one_queries, 0)
    if stage == 2:
        for r in range(4):
            o_out[r][...] = os[r]


def pair_of(low, columns, h):
    return jnp.where(low, columns[:, h : h + 1], columns[:, h + 1 : h + 2])


def softplus(v):
    return jnp.maximum(v, 0.0) + jnp.log1p(jnp.exp(-jnp.abs(v)))


SPAN = slice(STATE_DIM, STATE_DIM + 8)
SPAN_LOW = slice(STATE_DIM + 8, STATE_DIM + 16)
HELD, SENT = STATE_DIM + 8, STATE_DIM + 16


def send_state(pay_ref, lanes, state, span):
    span_high = span.astype(BF16)
    pay_ref[0:STATE_DIM, lanes] = state.astype(BF16)
    pay_ref[STATE_DIM:SENT, lanes] = jnp.concatenate(
        [span_high.astype(F32), span - span_high.astype(F32)], axis=0
    ).astype(BF16)


def ssm_local_kernel(
    x_ref, write_t_ref, read_t_ref, step_t_ref, rate_ref, gain_ref, out_ref, total_ref, pay_ref, cum_ref
):
    heads = step_t_ref.shape[0]
    high = lax.Precision.HIGHEST
    row = lax.broadcasted_iota(jnp.int32, (TOK, TOK), 0)
    col = lax.broadcasted_iota(jnp.int32, (TOK, TOK), 1)
    rate = jnp.broadcast_to(-jnp.exp(rate_ref[...]) * LOG2E, (8, heads)).T[:, 0:1]
    step_t = softplus(step_t_ref[...])
    cum_t = jnp.dot(
        rate * step_t, jnp.where(row <= col, 1.0, 0.0), precision=high, preferred_element_type=F32
    )
    key_row = jnp.log2(step_t) - cum_t
    cum = cum_t.T
    step = step_t.T
    cum_ref[...] = cum
    last = cum[TOK - 1 : TOK, :]
    tail = jnp.exp2(last - cum) * step
    gain = gain_ref[...]

    near = lax.dot_general(
        read_t_ref[...], write_t_ref[...], (((0,), (0,)), ((), ())), preferred_element_type=F32
    )
    near = jnp.where(col <= row, near, 0.0)
    low = lax.broadcasted_iota(jnp.int32, (1, 128), 1) < SSM_DIM
    for h in range(0, heads, 2):
        lanes = slice(h * SSM_DIM, (h + 2) * SSM_DIM)
        x_pair = x_ref[:, lanes]
        x_f = x_pair.astype(F32)
        weighted = (x_f * pair_of(low, tail, h)).astype(BF16)
        state = jnp.dot(write_t_ref[...], weighted, preferred_element_type=F32)
        span = jnp.broadcast_to(pair_of(low, last, h), (8, 128))
        total_ref[0:STATE_DIM, lanes] = state
        total_ref[SPAN, lanes] = span
        send_state(pay_ref, lanes, state, span)
        for t in range(2):
            t_rows = slice(t * HALF, (t + 1) * HALF)
            both = []
            for k in range(2):
                total = None
                for s in range(t + 1):
                    s_rows = slice(s * HALF, (s + 1) * HALF)
                    weights = (
                        jnp.exp2(cum[t_rows, h + k : h + k + 1] + key_row[h + k : h + k + 1, s_rows])
                        * near[t_rows, s_rows]
                    )
                    part = jnp.dot(weights.astype(BF16), x_pair[s_rows, :], preferred_element_type=F32)
                    total = part if total is None else total + part
                both.append(total)
            out_ref[t_rows, lanes] = (
                jnp.where(low, both[0], both[1]) + pair_of(low, gain, h) * x_f[t_rows, :]
            )


def ssm_merge_kernel(level, info, got_ref, total_ref, before_ref, total_out, before_out, pay_ref):
    later = ((info[3] >> level) & 1).astype(F32)
    got = got_ref[0:STATE_DIM, :].astype(F32)
    got_span = got_ref[STATE_DIM:SENT, :].astype(F32)
    got_span = got_span[0:8, :] + got_span[8:16, :]
    total, total_span = total_ref[0:STATE_DIM, :], total_ref[SPAN, :]
    before, before_span = before_ref[0:STATE_DIM, :], before_ref[SPAN, :]
    before_out[0:STATE_DIM, :] = before + later * (got * jnp.exp2(before_span[0:1, :]))
    before_out[SPAN, :] = before_span + later * got_span
    after_got = got * jnp.exp2(total_span[0:1, :]) + total
    after_total = total * jnp.exp2(got_span[0:1, :]) + got
    total = later * after_got + (1.0 - later) * after_total
    span = total_span + got_span
    total_out[0:STATE_DIM, :] = total
    total_out[SPAN, :] = span
    send_state(pay_ref, slice(None), total, span)


def ssm_carry_kernel(state_ref, mixed_ref, cum_ref, read_t_ref, gate_ref, gated_ref, square_ref):
    heads = cum_ref.shape[1]
    state = state_ref[0:STATE_DIM, :]
    state_high = state.astype(BF16)
    state_low = (state - state_high.astype(F32)).astype(BF16)
    reach = jnp.exp2(cum_ref[...])
    read = read_t_ref[...].T
    low = lax.broadcasted_iota(jnp.int32, (1, 128), 1) < SSM_DIM
    squares = jnp.zeros((TOK, 128), F32)
    for h in range(0, heads, 2):
        lanes = slice(h * SSM_DIM, (h + 2) * SSM_DIM)
        carried = jnp.dot(read, state_high[:, lanes], preferred_element_type=F32)
        carried = carried + jnp.dot(read, state_low[:, lanes], preferred_element_type=F32)
        mixed = mixed_ref[:, lanes] + carried * pair_of(low, reach, h)
        gate = gate_ref[:, lanes].astype(F32)
        gated = mixed * (gate / (1.0 + jnp.exp(-gate)))
        gated_ref[:, lanes] = gated
        squares = squares + gated * gated
    square_ref[...] = jnp.sum(squares.T, axis=0, keepdims=True)


def vmem(count):
    return [pl.BlockSpec(memory_space=pltpu.VMEM)] * count


SMEM = pl.BlockSpec(memory_space=pltpu.SMEM)
ANY = pl.BlockSpec(memory_space=pl.ANY)


SMALL = pl.CostEstimate(flops=1000, bytes_accessed=1000, transcendentals=0)


def params(mib):
    return pltpu.CompilerParams(vmem_limit_bytes=mib * 1024 * 1024)


def shape(dims, kind):
    return jax.ShapeDtypeStruct(dims, kind)


def pack(info, query_rows, key_rows, value_rows):
    width = HEADS * ATT_DIM
    rows = [ATT_DIM, 2 * ATT_DIM] + [3 * ATT_DIM] * 3
    return pl.pallas_call(
        pack_kernel,
        out_shape=[shape((count, TOK), BF16) for count in rows],
        in_specs=[SMEM] + [ANY] * 3,
        out_specs=vmem(len(rows)),
        scratch_shapes=[
            pltpu.VMEM((3, TOK, width), BF16),
            pltpu.VMEM((3, width, TOK), BF16),
            pltpu.SemaphoreType.DMA((3,)),
        ],
        compiler_params=params(60),
    )(info, query_rows, key_rows, value_rows)


def attend(stage, info, *operands):
    slots = (4, 3, 1)[stage]
    keys, values = (slots, 2 * TOK, ATT_DIM), (slots, ATT_DIM, 2 * TOK)
    state = [shape((4, ATT_DIM, TOK), F32), shape((4, 16, TOK), F32)]
    queries = pltpu.VMEM((4, ATT_DIM, TOK), BF16)
    mark = [shape((8, 128), F32)]
    if stage == 0:
        out = state + [shape(keys, BF16), shape(values, BF16)] + mark
        scratch = [queries]
    elif stage == 1:
        out = state + mark
        scratch = [pltpu.VMEM(keys, BF16), pltpu.VMEM(values, BF16), queries]
    else:
        out = [shape((ATT_DIM, TOK), BF16)] * 4 + mark
        scratch = [pltpu.VMEM(keys, BF16), pltpu.VMEM(values, BF16), queries]
        scratch += [pltpu.VMEM((4, ATT_DIM, TOK), F32), queries]
    return pl.pallas_call(
        functools.partial(attend_kernel, stage),
        out_shape=out,
        in_specs=[SMEM] + vmem(len(operands)),
        out_specs=vmem(len(out)),
        scratch_shapes=scratch,
        compiler_params=params(24),
        cost_estimate=SMALL,
    )(info, *operands)


def unpack(info, mark, pieces):
    width = HEADS * ATT_DIM
    return pl.pallas_call(
        unpack_kernel,
        out_shape=shape((TOK, width), BF16),
        in_specs=[SMEM, ANY] + vmem(4),
        out_specs=vmem(1)[0],
        scratch_shapes=[pltpu.VMEM((width, TOK), BF16)],
        compiler_params=params(40),
    )(info, mark, *pieces)


def ssm_local(ssm_inputs, write_t, read_t, step_t, rate, gain):
    tokens, width = ssm_inputs.shape
    heads = step_t.shape[0]
    return pl.pallas_call(
        ssm_local_kernel,
        out_shape=[
            shape((tokens, width), F32),
            shape((HELD, width), F32),
            shape((SENT, width), BF16),
            shape((tokens, heads), F32),
        ],
        in_specs=vmem(6),
        out_specs=vmem(4),
        compiler_params=params(40),
        cost_estimate=SMALL,
    )(ssm_inputs, write_t, read_t, step_t, rate, gain)


def ssm_merge(level, info, got, total, before):
    held, sent = shape(total.shape, F32), shape(got.shape, BF16)
    return pl.pallas_call(
        functools.partial(ssm_merge_kernel, level),
        out_shape=[held, held, sent],
        in_specs=[SMEM] + vmem(3),
        out_specs=vmem(3),
        compiler_params=params(40),
        cost_estimate=SMALL,
    )(info, got, total, before)


def ssm_carry(state, mixed, cum, read_t, gate):
    tokens, width = mixed.shape
    return pl.pallas_call(
        ssm_carry_kernel,
        out_shape=[shape((tokens, width), F32), shape((1, tokens), F32)],
        in_specs=vmem(5),
        out_specs=vmem(2),
        compiler_params=params(40),
        cost_estimate=SMALL,
    )(state, mixed, cum, read_t, gate)


def on_device(
    query_rows,
    key_rows,
    value_rows,
    ssm_inputs,
    ssm_gate,
    write_vecs,
    read_vecs,
    step_raw,
    decay_log,
    skip_gain,
    norm_gain,
):
    me = lax.axis_index("ctx")
    y, x, core = me >> 3, (me >> 1) & 3, me & 1
    info = jnp.stack([y * 2 + (x >> 1), (x ^ (x >> 1)) & 1, core, me]).astype(jnp.int32)
    tie = lax.optimization_barrier

    q_own, kv_own, all_1, all_2, all_3 = pack(info, query_rows, key_rows, value_rows)
    here, near, from_core, near_core = [None] * 4, [None] * 4, [None] * 4, [None] * 4
    here[1], here[2] = head_swap(all_1, 1), head_swap(all_2, 2)
    near[0] = class_swap(kv_own)
    from_core[0] = core_swap(kv_own)

    from_core[0], ssm_inputs = tie((from_core[0], ssm_inputs))
    read_t = read_vecs.T
    mixed, total, sent, cum = ssm_local(
        ssm_inputs, write_vecs.T, read_t, step_raw.T, decay_log[None, :], skip_gain[None, :]
    )
    before = jnp.zeros_like(total)
    total, before, sent = ssm_merge(0, info, core_swap(sent), total, before)
    got = class_swap(sent)

    near[0], sent = tie((near[0], sent))
    near_core[0] = core_swap(near[0])

    here[1], here[2], near_core[0], all_3, got = tie((here[1], here[2], near_core[0], all_3, got))
    kv = [piece[ATT_DIM:] for piece in here[1:3]]
    near[1], near[2] = class_swap(kv[0]), class_swap(kv[1])
    here[3] = head_swap(all_3, 3)
    total, before, sent = ssm_merge(1, info, got, total, before)
    *kv, sent = tie((*kv, sent))
    from_core[1], from_core[2] = core_swap(kv[0]), core_swap(kv[1])
    from_core[1], from_core[2], sent = tie((from_core[1], from_core[2], sent))
    got = block_swap(sent, 4)
    *state, ks, vs, mark = attend(
        0, info, q_own, here[1], here[2], kv_own, *from_core[:3], near[0], near_core[0]
    )

    here[3], near[1], near[2], mark = tie((here[3], near[1], near[2], mark))
    kv = here[3][ATT_DIM:]
    from_core[3] = core_swap(kv)
    near_core[1], near_core[2] = core_swap(near[1]), core_swap(near[2])
    kv, got = tie((kv, got))
    near[3] = class_swap(kv)
    total, before, sent = ssm_merge(2, info, got, total, before)
    sent, mark = tie((sent, mark))
    got = block_swap(sent, 8)
    queries = (q_own, here[1], here[2], here[3])
    *state, mark = attend(
        1, info, *queries, from_core[3], near[1], near_core[1], near[2], near_core[2], mark, ks, vs, *state
    )

    near[3], got, mark = tie((near[3], got, mark))
    near_core[3] = core_swap(near[3])
    total, before, sent = ssm_merge(3, info, got, total, before)
    gated, squares = ssm_carry(before, mixed, cum, read_t, ssm_gate)
    gated, squares, mark = tie((gated, squares, mark))
    *results, mark = attend(2, info, *queries, near[3], near_core[3], mark, *state)
    back = [results[0]] + [head_swap(results[r], r) for r in range(1, 4)]
    squares, mark = tie((squares, mark))
    for step in (1, 2, 4):
        squares = squares + step_swap(squares, step)
    *back, squares = tie((*back, squares))
    factor = lax.rsqrt(squares.reshape(TOK) / SSM_WIDTH + 1e-05)
    mixer_out = (gated * factor[:, None] * norm_gain[None, :]).astype(BF16)
    return (unpack(info, mark, back), mixer_out)


def solution(mesh):
    placed = (
        P("ctx", "tp"),
        P("ctx", "tp"),
        P("ctx", "tp"),
        P("ctx", "tp"),
        P("ctx", "tp"),
        P("ctx", None),
        P("ctx", None),
        P("ctx", "tp"),
        P("tp"),
        P("tp"),
        P("tp"),
    )
    return jax.shard_map(
        on_device,
        mesh=mesh,
        in_specs=placed,
        out_specs=(P("ctx", "tp"), P("ctx", "tp")),
        check_vma=False,
    )
```

```python
import functools
import math

import jax
import jax.numpy as jnp
from jax import lax
from jax.experimental import pallas as pl
from jax.experimental.pallas import tpu as pltpu
from jax.sharding import PartitionSpec as P

ATT_DIM = 224
SSM_DIM = 64
STATE_DIM = 64
SSM_WIDTH = 7168
TOK = 512
HEADS = 4
CTX = 16
HALF = 256
LOG2E = math.log2(math.e)
F32 = jnp.float32
BF16 = jnp.bfloat16


def exchanged(i, r):
    y, x, c = i >> 3, (i >> 1) & 3, i & 1
    if r & 1:
        x = 3 - x
    if r & 2:
        y = 1 - y
    return y * 8 + x * 2 + c


def head_swap(value, r):
    return lax.ppermute(value, "ctx", [(i, exchanged(i, r)) for i in range(CTX)])


def class_swap(value):
    return lax.ppermute(value, "ctx", [(i, i ^ 2) for i in range(CTX)])


def core_swap(value):
    return lax.ppermute(value, "ctx", [(i, i ^ 1) for i in range(CTX)])


def block_swap(value, step):
    return lax.ppermute(value, "ctx", [(i, i ^ step) for i in range(CTX)])


def step_swap(value, step):
    return lax.ppermute(value, "tp", [(i, i ^ step) for i in range(8)])


def head_rows(head):
    return pl.ds(pl.multiple_of(head * ATT_DIM, 16), ATT_DIM)


Q_ROWS = slice(0, ATT_DIM)
K_ROWS = slice(ATT_DIM, 2 * ATT_DIM)
V_ROWS = slice(2 * ATT_DIM, 3 * ATT_DIM)


def pack_kernel(info, q_in, k_in, v_in, q_own, kv_own, all_1, all_2, all_3, raw, rows_ref, sems):
    copies = [pltpu.make_async_copy(src, raw.at[i], sems.at[i]) for i, src in enumerate((q_in, k_in, v_in))]
    for copy in copies:
        copy.start()
    for i, (out, first) in enumerate(((q_own, 0), (kv_own, 0), (kv_own, ATT_DIM))):
        copies[i].wait()
        rows_ref[i] = raw[i].T
        out[first : first + ATT_DIM, :] = rows_ref[i, head_rows(info[0]), :]
        for r, away in ((1, all_1), (2, all_2), (3, all_3)):
            away[i * ATT_DIM : (i + 1) * ATT_DIM, :] = rows_ref[i, head_rows(info[0] ^ r), :]


def unpack_kernel(info, _, *refs):
    pieces, out_ref, rows_ref = refs[:4], refs[4], refs[5]
    for r in range(4):
        rows_ref[head_rows(info[0] ^ r), :] = pieces[r][...]
    out_ref[...] = rows_ref[...].T


def attend_kernel(stage, info, *refs):
    hid, kind, core = info[0], info[1], info[2]
    scale = ATT_DIM ** (-0.5) * LOG2E
    if stage == 0:
        q_in, (kv_own, core_0, core_1, core_2, near_0, near_core_0), refs = refs[:3], refs[3:9], refs[9:]
        acc, stats_ref, ks, vs, mark, qs = refs
        pieces = [(0, 0, kv_own, 0), (1, 0, q_in[1], ATT_DIM), (2, 0, q_in[2], ATT_DIM)]
        pieces += [(0, 1, core_0, 0), (1, 1, core_1, 0), (2, 1, core_2, 0)]
        pieces += [(3, 0, near_0, 0), (3, 1, near_core_0, 0)]
    elif stage == 1:
        q_in, (core_keys_3, core_values_3, _), refs = refs[:4], refs[4:7], refs[7:]
        ks_early, vs_early, acc_in, stats_in, acc, stats_ref, mark, ks, vs, qs = refs
        pieces = [(0, 0, q_in[3], ATT_DIM), (0, 1, (core_keys_3, core_values_3), 0)]
    elif stage == 2:
        q_in, (near_1, near_core_1, near_2, near_core_2, _), refs = refs[:4], refs[4:9], refs[9:]
        acc_in, stats_in, acc, stats_ref, mark, ks, vs, qs = refs
        pieces = [(0, 0, near_1, 0), (0, 1, near_core_1, 0), (1, 0, near_2, 0), (1, 1, near_core_2, 0)]
    else:
        q_in, (near_3, near_core_3, _), refs = refs[:4], refs[4:7], refs[7:]
        acc_in, stats_in, *o_out, mark, ks, vs, qs, acc, os = refs
        pieces = [(0, 0, near_3, 0), (0, 1, near_core_3, 0)]
    for slot, other, piece, first in pieces:
        start = pl.multiple_of((core ^ other) * TOK, TOK)
        if isinstance(piece, tuple):
            ks[slot, pl.ds(start, TOK), :] = piece[0][...].T
            vs[slot, :, pl.ds(start, TOK)] = piece[1][...]
            continue
        ks[slot, pl.ds(start, TOK), :] = piece[first : first + ATT_DIM, :].T
        vs[slot, :, pl.ds(start, TOK)] = piece[first + ATT_DIM : first + 2 * ATT_DIM, :]
    for r, queries in enumerate(q_in):
        qs[r] = queries[Q_ROWS, :]
    mark[...] = jnp.zeros_like(mark)

    def one_queries(r, carry):
        chip = hid ^ r

        def visit(keys, values, stats, masked):
            lanes = [slice(half * HALF, (half + 1) * HALF) for half in range(2)]
            scores = [
                jnp.dot(keys, qs[r, :, lanes[half]], preferred_element_type=F32) for half in range(2)
            ]
            new_stats, low, shrinks = [], [], []
            for half in range(2):
                (top, total), s = stats[half], scores[half]
                if masked:
                    k_pos = lax.broadcasted_iota(jnp.int32, s.shape, 0)
                    q_pos = lax.broadcasted_iota(jnp.int32, s.shape, 1) + half * HALF
                    s = jnp.where(k_pos <= q_pos, s, -1e30)
                new_top = jnp.maximum(top, jnp.max(s, axis=0, keepdims=True))
                p = jnp.exp2((s - new_top) * scale)
                shrink = jnp.exp2((top - new_top) * scale)
                total = total * shrink + jnp.sum(p, axis=0, keepdims=True)
                new_stats.append((new_top, total))
                low.append(p.astype(BF16))
                shrinks.append(shrink)
            for half in range(2):
                acc[r, :, lanes[half]] = acc[r, :, lanes[half]] * shrinks[half] + jnp.dot(
                    values, low[half], preferred_element_type=F32
                )
            return tuple(new_stats)

        def sweep(count, key_ref, value_ref, seen, stats):
            def one(k, now):
                times = jnp.where(seen(k), 1, 0)
                return lax.fori_loop(
                    0, times, lambda _, inner: visit(key_ref[k], value_ref[k], inner, False), now
                )

            return lax.fori_loop(0, count, one, stats)

        def near_seen(k):
            limit = jnp.where(kind == 0, ((chip + 1) >> 1) * 2, (chip >> 1) * 2 + 1)
            return (hid ^ k) < limit

        def diagonal(slot, stats):
            def part(start, now, masked):
                start = pl.multiple_of(start, TOK)
                return visit(ks[slot, pl.ds(start, TOK), :], vs[slot, :, pl.ds(start, TOK)], now, masked)

            stats = lax.fori_loop(0, core, lambda _, now: part(0, now, False), stats)
            return part(core * TOK, stats, True)

        if stage == 0:
            acc[r] = jnp.zeros((ATT_DIM, TOK), F32)
            first = (jnp.full((1, HALF), -1e30, F32), jnp.zeros((1, HALF), F32))
            stats = (first, first)
        else:
            acc[r] = acc_in[r]
            stats = tuple(
                (
                    stats_in[r, 0:1, half * HALF : (half + 1) * HALF],
                    stats_in[r, 8:9, half * HALF : (half + 1) * HALF],
                )
                for half in range(2)
            )

        if stage == 0:

            def early(now):
                now = sweep(4, ks, vs, lambda k: jnp.where(k == 3, near_seen(0), (hid ^ k) < chip), now)
                return diagonal(r, now)

            stats = lax.fori_loop(0, jnp.where(r == 3, 0, 1), lambda _, now: early(now), stats)
        elif stage == 1:
            last = jnp.where(r == 3, 1, 0)
            stats = sweep(
                4 * last, ks_early, vs_early, lambda k: jnp.where(k == 3, near_seen(0), (hid ^ k) < chip), stats
            )
            stats = sweep(1, ks, vs, lambda k: (hid ^ 3) < chip, stats)
            stats = lax.fori_loop(0, last, lambda _, now: diagonal(0, now), stats)
        elif stage == 2:
            stats = sweep(2, ks, vs, lambda k: near_seen(k + 1), stats)
        else:
            stats = sweep(1, ks, vs, lambda k: near_seen(3), stats)

        for half in range(2):
            lanes = slice(half * HALF, (half + 1) * HALF)
            if stage == 3:
                os[r, :, lanes] = (acc[r, :, lanes] / stats[half][1]).astype(BF16)
            else:
                stats_ref[r, 0:8, lanes] = jnp.broadcast_to(stats[half][0], (8, HALF))
                stats_ref[r, 8:16, lanes] = jnp.broadcast_to(stats[half][1], (8, HALF))
        return carry

    lax.fori_loop(0, 4, one_queries, 0)
    if stage == 3:
        for r in range(4):
            o_out[r][...] = os[r]


def pair_of(low, columns, h):
    return jnp.where(low, columns[:, h : h + 1], columns[:, h + 1 : h + 2])


def softplus(v):
    return jnp.maximum(v, 0.0) + jnp.log1p(jnp.exp(-jnp.abs(v)))


SPAN = slice(STATE_DIM, STATE_DIM + 8)
SPAN_LOW = slice(STATE_DIM + 8, STATE_DIM + 16)
HELD, SENT = STATE_DIM + 8, STATE_DIM + 16


def send_state(pay_ref, lanes, state, span):
    span_high = span.astype(BF16)
    pay_ref[0:STATE_DIM, lanes] = state.astype(BF16)
    pay_ref[STATE_DIM:SENT, lanes] = jnp.concatenate(
        [span_high.astype(F32), span - span_high.astype(F32)], axis=0
    ).astype(BF16)


def ssm_local_kernel(
    x_ref, write_t_ref, read_t_ref, step_t_ref, rate_ref, gain_ref, out_ref, total_ref, pay_ref, cum_ref
):
    heads = step_t_ref.shape[0]
    high = lax.Precision.HIGHEST
    row = lax.broadcasted_iota(jnp.int32, (TOK, TOK), 0)
    col = lax.broadcasted_iota(jnp.int32, (TOK, TOK), 1)
    rate = jnp.broadcast_to(-jnp.exp(rate_ref[...]) * LOG2E, (8, heads)).T[:, 0:1]
    step_t = softplus(step_t_ref[...])
    cum_t = jnp.dot(
        rate * step_t, jnp.where(row <= col, 1.0, 0.0), precision=high, preferred_element_type=F32
    )
    key_row = jnp.log2(step_t) - cum_t
    cum = cum_t.T
    step = step_t.T
    cum_ref[...] = cum
    last = cum[TOK - 1 : TOK, :]
    tail = jnp.exp2(last - cum) * step
    gain = gain_ref[...]

    near = lax.dot_general(
        read_t_ref[...], write_t_ref[...], (((0,), (0,)), ((), ())), preferred_element_type=F32
    )
    near = jnp.where(col <= row, near, 0.0)
    low = lax.broadcasted_iota(jnp.int32, (1, 128), 1) < SSM_DIM
    for h in range(0, heads, 2):
        lanes = slice(h * SSM_DIM, (h + 2) * SSM_DIM)
        x_pair = x_ref[:, lanes]
        x_f = x_pair.astype(F32)
        weighted = (x_f * pair_of(low, tail, h)).astype(BF16)
        state = jnp.dot(write_t_ref[...], weighted, preferred_element_type=F32)
        span = jnp.broadcast_to(pair_of(low, last, h), (8, 128))
        total_ref[0:STATE_DIM, lanes] = state
        total_ref[SPAN, lanes] = span
        send_state(pay_ref, lanes, state, span)
        for t in range(2):
            t_rows = slice(t * HALF, (t + 1) * HALF)
            both = []
            for k in range(2):
                total = None
                for s in range(t + 1):
                    s_rows = slice(s * HALF, (s + 1) * HALF)
                    weights = (
                        jnp.exp2(cum[t_rows, h + k : h + k + 1] + key_row[h + k : h + k + 1, s_rows])
                        * near[t_rows, s_rows]
                    )
                    part = jnp.dot(weights.astype(BF16), x_pair[s_rows, :], preferred_element_type=F32)
                    total = part if total is None else total + part
                both.append(total)
            out_ref[t_rows, lanes] = (
                jnp.where(low, both[0], both[1]) + pair_of(low, gain, h) * x_f[t_rows, :]
            )


def ssm_merge_kernel(level, info, got_ref, total_ref, before_ref, total_out, before_out, pay_ref):
    later = ((info[3] >> level) & 1).astype(F32)
    got = got_ref[0:STATE_DIM, :].astype(F32)
    got_span = got_ref[STATE_DIM:SENT, :].astype(F32)
    got_span = got_span[0:8, :] + got_span[8:16, :]
    total, total_span = total_ref[0:STATE_DIM, :], total_ref[SPAN, :]
    before, before_span = before_ref[0:STATE_DIM, :], before_ref[SPAN, :]
    before_out[0:STATE_DIM, :] = before + later * (got * jnp.exp2(before_span[0:1, :]))
    before_out[SPAN, :] = before_span + later * got_span
    after_got = got * jnp.exp2(total_span[0:1, :]) + total
    after_total = total * jnp.exp2(got_span[0:1, :]) + got
    total = later * after_got + (1.0 - later) * after_total
    span = total_span + got_span
    total_out[0:STATE_DIM, :] = total
    total_out[SPAN, :] = span
    send_state(pay_ref, slice(None), total, span)


def ssm_carry_kernel(state_ref, mixed_ref, cum_ref, read_t_ref, gate_ref, gated_ref, square_ref):
    heads = cum_ref.shape[1]
    state = state_ref[0:STATE_DIM, :]
    state_high = state.astype(BF16)
    state_low = (state - state_high.astype(F32)).astype(BF16)
    reach = jnp.exp2(cum_ref[...])
    read = read_t_ref[...].T
    low = lax.broadcasted_iota(jnp.int32, (1, 128), 1) < SSM_DIM
    squares = jnp.zeros((TOK, 128), F32)
    for h in range(0, heads, 2):
        lanes = slice(h * SSM_DIM, (h + 2) * SSM_DIM)
        carried = jnp.dot(read, state_high[:, lanes], preferred_element_type=F32)
        carried = carried + jnp.dot(read, state_low[:, lanes], preferred_element_type=F32)
        mixed = mixed_ref[:, lanes] + carried * pair_of(low, reach, h)
        gate = gate_ref[:, lanes].astype(F32)
        gated = mixed * (gate / (1.0 + jnp.exp(-gate)))
        gated_ref[:, lanes] = gated
        squares = squares + gated * gated
    square_ref[...] = jnp.sum(squares.T, axis=0, keepdims=True)


def vmem(count):
    return [pl.BlockSpec(memory_space=pltpu.VMEM)] * count


SMEM = pl.BlockSpec(memory_space=pltpu.SMEM)
ANY = pl.BlockSpec(memory_space=pl.ANY)


SMALL = pl.CostEstimate(flops=1000, bytes_accessed=1000, transcendentals=0)


def params(mib):
    return pltpu.CompilerParams(vmem_limit_bytes=mib * 1024 * 1024)


def shape(dims, kind):
    return jax.ShapeDtypeStruct(dims, kind)


def pack(info, query_rows, key_rows, value_rows):
    width = HEADS * ATT_DIM
    rows = [ATT_DIM, 2 * ATT_DIM] + [3 * ATT_DIM] * 3
    return pl.pallas_call(
        pack_kernel,
        out_shape=[shape((count, TOK), BF16) for count in rows],
        in_specs=[SMEM] + [ANY] * 3,
        out_specs=vmem(len(rows)),
        scratch_shapes=[
            pltpu.VMEM((3, TOK, width), BF16),
            pltpu.VMEM((3, width, TOK), BF16),
            pltpu.SemaphoreType.DMA((3,)),
        ],
        compiler_params=params(60),
    )(info, query_rows, key_rows, value_rows)


def attend(stage, info, *operands):
    slots = (4, 1, 2, 1)[stage]
    keys, values = (slots, 2 * TOK, ATT_DIM), (slots, ATT_DIM, 2 * TOK)
    state = [shape((4, ATT_DIM, TOK), F32), shape((4, 16, TOK), F32)]
    queries = pltpu.VMEM((4, ATT_DIM, TOK), BF16)
    mark = [shape((8, 128), F32)]
    if stage == 0:
        out = state + [shape(keys, BF16), shape(values, BF16)] + mark
        scratch = [queries]
    elif stage < 3:
        out = state + mark
        scratch = [pltpu.VMEM(keys, BF16), pltpu.VMEM(values, BF16), queries]
    else:
        out = [shape((ATT_DIM, TOK), BF16)] * 4 + mark
        scratch = [pltpu.VMEM(keys, BF16), pltpu.VMEM(values, BF16), queries]
        scratch += [pltpu.VMEM((4, ATT_DIM, TOK), F32), queries]
    return pl.pallas_call(
        functools.partial(attend_kernel, stage),
        out_shape=out,
        in_specs=[SMEM] + vmem(len(operands)),
        out_specs=vmem(len(out)),
        scratch_shapes=scratch,
        compiler_params=params(24),
        cost_estimate=SMALL,
    )(info, *operands)


def unpack(info, mark, pieces):
    width = HEADS * ATT_DIM
    return pl.pallas_call(
        unpack_kernel,
        out_shape=shape((TOK, width), BF16),
        in_specs=[SMEM, ANY] + vmem(4),
        out_specs=vmem(1)[0],
        scratch_shapes=[pltpu.VMEM((width, TOK), BF16)],
        compiler_params=params(40),
    )(info, mark, *pieces)


def ssm_local(ssm_inputs, write_t, read_t, step_t, rate, gain):
    tokens, width = ssm_inputs.shape
    heads = step_t.shape[0]
    return pl.pallas_call(
        ssm_local_kernel,
        out_shape=[
            shape((tokens, width), F32),
            shape((HELD, width), F32),
            shape((SENT, width), BF16),
            shape((tokens, heads), F32),
        ],
        in_specs=vmem(6),
        out_specs=vmem(4),
        compiler_params=params(40),
        cost_estimate=SMALL,
    )(ssm_inputs, write_t, read_t, step_t, rate, gain)


def ssm_merge(level, info, got, total, before):
    held, sent = shape(total.shape, F32), shape(got.shape, BF16)
    return pl.pallas_call(
        functools.partial(ssm_merge_kernel, level),
        out_shape=[held, held, sent],
        in_specs=[SMEM] + vmem(3),
        out_specs=vmem(3),
        compiler_params=params(40),
        cost_estimate=SMALL,
    )(info, got, total, before)


def ssm_carry(state, mixed, cum, read_t, gate):
    tokens, width = mixed.shape
    return pl.pallas_call(
        ssm_carry_kernel,
        out_shape=[shape((tokens, width), F32), shape((1, tokens), F32)],
        in_specs=vmem(5),
        out_specs=vmem(2),
        compiler_params=params(40),
        cost_estimate=SMALL,
    )(state, mixed, cum, read_t, gate)


def on_device(
    query_rows,
    key_rows,
    value_rows,
    ssm_inputs,
    ssm_gate,
    write_vecs,
    read_vecs,
    step_raw,
    decay_log,
    skip_gain,
    norm_gain,
):
    me = lax.axis_index("ctx")
    y, x, core = me >> 3, (me >> 1) & 3, me & 1
    info = jnp.stack([y * 2 + (x >> 1), (x ^ (x >> 1)) & 1, core, me]).astype(jnp.int32)
    tie = lax.optimization_barrier

    q_own, kv_own, all_1, all_2, all_3 = pack(info, query_rows, key_rows, value_rows)
    here, near, from_core, near_core = [None] * 4, [None] * 4, [None] * 4, [None] * 4
    here[1], here[2] = head_swap(all_1, 1), head_swap(all_2, 2)
    near[0] = class_swap(kv_own)
    from_core[0] = core_swap(kv_own)

    from_core[0], ssm_inputs = tie((from_core[0], ssm_inputs))
    read_t = read_vecs.T
    mixed, total, sent, cum = ssm_local(
        ssm_inputs, write_vecs.T, read_t, step_raw.T, decay_log[None, :], skip_gain[None, :]
    )
    before = jnp.zeros_like(total)
    total, before, sent = ssm_merge(0, info, core_swap(sent), total, before)
    got = class_swap(sent)

    near[0], sent = tie((near[0], sent))
    near_core[0] = core_swap(near[0])

    here[1], here[2], near_core[0], all_3, got = tie((here[1], here[2], near_core[0], all_3, got))
    kv = [piece[ATT_DIM:] for piece in here[1:3]]
    near[1], near[2] = class_swap(kv[0]), class_swap(kv[1])
    here[3] = head_swap(all_3, 3)
    total, before, sent = ssm_merge(1, info, got, total, before)
    *kv, sent = tie((*kv, sent))
    from_core[1], from_core[2] = core_swap(kv[0]), core_swap(kv[1])
    from_core[1], from_core[2], sent = tie((from_core[1], from_core[2], sent))
    got = block_swap(sent, 4)
    *state, ks, vs, mark = attend(
        0, info, q_own, here[1], here[2], kv_own, *from_core[:3], near[0], near_core[0]
    )

    here[3], mark = tie((here[3], mark))
    kv = here[3][ATT_DIM:]
    from_core[3] = (core_swap(here[3][K_ROWS]), core_swap(here[3][V_ROWS]))
    queries = (q_own, here[1], here[2], here[3])
    *state, mark = attend(1, info, *queries, *from_core[3], mark, ks, vs, *state)

    near[1], near[2], mark = tie((near[1], near[2], mark))
    near_core[1], near_core[2] = core_swap(near[1]), core_swap(near[2])
    kv, got = tie((kv, got))
    near[3] = class_swap(kv)
    total, before, sent = ssm_merge(2, info, got, total, before)
    sent, mark = tie((sent, mark))
    got = block_swap(sent, 8)
    *state, mark = attend(2, info, *queries, near[1], near_core[1], near[2], near_core[2], mark, *state)

    got, mark = tie((got, mark))
    total, before, sent = ssm_merge(3, info, got, total, before)
    gated, squares = ssm_carry(before, mixed, cum, read_t, ssm_gate)
    squares = squares + step_swap(squares, 1)
    near[3], gated, squares, mark = tie((near[3], gated, squares, mark))
    near_core[3] = core_swap(near[3])
    *results, mark = attend(3, info, *queries, near[3], near_core[3], mark, *state)
    back = [results[0]] + [head_swap(results[r], r) for r in range(1, 4)]
    squares, mark = tie((squares, mark))
    for step in (2, 4):
        squares = squares + step_swap(squares, step)
    *back, squares = tie((*back, squares))
    factor = lax.rsqrt(squares.reshape(TOK) / SSM_WIDTH + 1e-05)
    mixer_out = (gated * factor[:, None] * norm_gain[None, :]).astype(BF16)
    return (unpack(info, mark, back), mixer_out)


def solution(mesh):
    placed = (
        P("ctx", "tp"),
        P("ctx", "tp"),
        P("ctx", "tp"),
        P("ctx", "tp"),
        P("ctx", "tp"),
        P("ctx", None),
        P("ctx", None),
        P("ctx", "tp"),
        P("tp"),
        P("tp"),
        P("tp"),
    )
    return jax.shard_map(
        on_device,
        mesh=mesh,
        in_specs=placed,
        out_specs=(P("ctx", "tp"), P("ctx", "tp")),
        check_vma=False,
    )
```

```python
import functools
import math

import jax
import jax.numpy as jnp
from jax import lax
from jax.experimental import pallas as pl
from jax.experimental.pallas import tpu as pltpu
from jax.sharding import PartitionSpec as P

ATT_DIM = 224
SSM_DIM = 64
STATE_DIM = 64
SSM_WIDTH = 7168
TOK = 512
HEADS = 4
CTX = 16
HALF = 256
LOG2E = math.log2(math.e)
F32 = jnp.float32
BF16 = jnp.bfloat16


def exchanged(i, r):
    y, x, c = i >> 3, (i >> 1) & 3, i & 1
    if r & 1:
        x = 3 - x
    if r & 2:
        y = 1 - y
    return y * 8 + x * 2 + c


def head_swap(value, r):
    return lax.ppermute(value, "ctx", [(i, exchanged(i, r)) for i in range(CTX)])


def class_swap(value):
    return lax.ppermute(value, "ctx", [(i, i ^ 2) for i in range(CTX)])


def core_swap(value):
    return lax.ppermute(value, "ctx", [(i, i ^ 1) for i in range(CTX)])


def block_swap(value, step):
    return lax.ppermute(value, "ctx", [(i, i ^ step) for i in range(CTX)])


def step_swap(value, step):
    return lax.ppermute(value, "tp", [(i, i ^ step) for i in range(8)])


def head_rows(head):
    return pl.ds(pl.multiple_of(head * ATT_DIM, 16), ATT_DIM)


Q_ROWS = slice(0, ATT_DIM)
K_ROWS = slice(ATT_DIM, 2 * ATT_DIM)
V_ROWS = slice(2 * ATT_DIM, 3 * ATT_DIM)


def pack_kernel(info, q_in, k_in, v_in, q_own, kv_own, all_1, all_2, all_3, raw, rows_ref, sems):
    copies = [pltpu.make_async_copy(src, raw.at[i], sems.at[i]) for i, src in enumerate((q_in, k_in, v_in))]
    for copy in copies:
        copy.start()
    for i, (out, first) in enumerate(((q_own, 0), (kv_own, 0), (kv_own, ATT_DIM))):
        copies[i].wait()
        rows_ref[i] = raw[i].T
        out[first : first + ATT_DIM, :] = rows_ref[i, head_rows(info[0]), :]
        for r, away in ((1, all_1), (2, all_2), (3, all_3)):
            away[i * ATT_DIM : (i + 1) * ATT_DIM, :] = rows_ref[i, head_rows(info[0] ^ r), :]


def unpack_kernel(info, _, *refs):
    pieces, out_ref, rows_ref = refs[:4], refs[4], refs[5]
    for r in range(4):
        rows_ref[head_rows(info[0] ^ r), :] = pieces[r][...]
    out_ref[...] = rows_ref[...].T


def attend_kernel(stage, info, *refs):
    hid, kind, core = info[0], info[1], info[2]
    scale = ATT_DIM ** (-0.5) * LOG2E
    if stage == 0:
        q_in, (kv_own, core_0, core_1, core_2, near_0, near_core_0), refs = refs[:3], refs[3:9], refs[9:]
        acc, stats_ref, ks, vs, mark, qs = refs
        pieces = [(0, 0, kv_own, 0), (1, 0, q_in[1], ATT_DIM), (2, 0, q_in[2], ATT_DIM)]
        pieces += [(0, 1, core_0, 0), (1, 1, core_1, 0), (2, 1, core_2, 0)]
        pieces += [(3, 0, near_0, 0), (3, 1, near_core_0, 0)]
    elif stage == 1:
        q_in, (core_keys_3, core_values_3, _), refs = refs[:4], refs[4:7], refs[7:]
        ks_early, vs_early, acc_in, stats_in, acc, stats_ref, mark, ks, vs, qs = refs
        pieces = [(0, 0, q_in[3], ATT_DIM), (0, 1, (core_keys_3, core_values_3), 0)]
    elif stage == 2:
        q_in, (near_1, near_core_1, near_2, near_core_2, _), refs = refs[:4], refs[4:9], refs[9:]
        acc_in, stats_in, acc, stats_ref, mark, ks, vs, qs = refs
        pieces = [(0, 0, near_1, 0), (0, 1, near_core_1, 0), (1, 0, near_2, 0), (1, 1, near_core_2, 0)]
    else:
        q_in, (near_3, near_core_3, _), refs = refs[:4], refs[4:7], refs[7:]
        acc_in, stats_in, *o_out, mark, ks, vs, qs, acc, os = refs
        pieces = [(0, 0, near_3, 0), (0, 1, near_core_3, 0)]
    for slot, other, piece, first in pieces:
        start = pl.multiple_of((core ^ other) * TOK, TOK)
        if isinstance(piece, tuple):
            ks[slot, pl.ds(start, TOK), :] = piece[0][...].T
            vs[slot, :, pl.ds(start, TOK)] = piece[1][...]
            continue
        ks[slot, pl.ds(start, TOK), :] = piece[first : first + ATT_DIM, :].T
        vs[slot, :, pl.ds(start, TOK)] = piece[first + ATT_DIM : first + 2 * ATT_DIM, :]
    for r, queries in enumerate(q_in):
        qs[r] = queries[Q_ROWS, :]
    mark[...] = jnp.zeros_like(mark)

    def one_queries(r, carry):
        chip = hid ^ r

        def visit(keys, values, stats, masked):
            lanes = [slice(half * HALF, (half + 1) * HALF) for half in range(2)]
            scores = [
                jnp.dot(keys, qs[r, :, lanes[half]], preferred_element_type=F32) for half in range(2)
            ]
            new_stats, low, shrinks = [], [], []
            for half in range(2):
                (top, total), s = stats[half], scores[half]
                if masked:
                    k_pos = lax.broadcasted_iota(jnp.int32, s.shape, 0)
                    q_pos = lax.broadcasted_iota(jnp.int32, s.shape, 1) + half * HALF
                    s = jnp.where(k_pos <= q_pos, s, -1e30)
                new_top = jnp.maximum(top, jnp.max(s, axis=0, keepdims=True))
                p = jnp.exp2((s - new_top) * scale)
                shrink = jnp.exp2((top - new_top) * scale)
                total = total * shrink + jnp.sum(p, axis=0, keepdims=True)
                new_stats.append((new_top, total))
                low.append(p.astype(BF16))
                shrinks.append(shrink)
            for half in range(2):
                acc[r, :, lanes[half]] = acc[r, :, lanes[half]] * shrinks[half] + jnp.dot(
                    values, low[half], preferred_element_type=F32
                )
            return tuple(new_stats)

        def sweep(count, key_ref, value_ref, seen, stats):
            def one(k, now):
                times = jnp.where(seen(k), 1, 0)
                return lax.fori_loop(
                    0, times, lambda _, inner: visit(key_ref[k], value_ref[k], inner, False), now
                )

            return lax.fori_loop(0, count, one, stats)

        def near_seen(k):
            limit = jnp.where(kind == 0, ((chip + 1) >> 1) * 2, (chip >> 1) * 2 + 1)
            return (hid ^ k) < limit

        def diagonal(slot, stats):
            def part(start, now, masked):
                start = pl.multiple_of(start, TOK)
                return visit(ks[slot, pl.ds(start, TOK), :], vs[slot, :, pl.ds(start, TOK)], now, masked)

            stats = lax.fori_loop(0, core, lambda _, now: part(0, now, False), stats)
            return part(core * TOK, stats, True)

        if stage == 0:
            acc[r] = jnp.zeros((ATT_DIM, TOK), F32)
            first = (jnp.full((1, HALF), -1e30, F32), jnp.zeros((1, HALF), F32))
            stats = (first, first)
        else:
            acc[r] = acc_in[r]
            stats = tuple(
                (
                    stats_in[r, 0:1, half * HALF : (half + 1) * HALF],
                    stats_in[r, 8:9, half * HALF : (half + 1) * HALF],
                )
                for half in range(2)
            )

        if stage == 0:

            def early(now):
                now = sweep(4, ks, vs, lambda k: jnp.where(k == 3, near_seen(0), (hid ^ k) < chip), now)
                return diagonal(r, now)

            stats = lax.fori_loop(0, jnp.where(r == 3, 0, 1), lambda _, now: early(now), stats)
        elif stage == 1:
            last = jnp.where(r == 3, 1, 0)
            stats = sweep(
                4 * last, ks_early, vs_early, lambda k: jnp.where(k == 3, near_seen(0), (hid ^ k) < chip), stats
            )
            stats = sweep(1, ks, vs, lambda k: (hid ^ 3) < chip, stats)
            stats = lax.fori_loop(0, last, lambda _, now: diagonal(0, now), stats)
        elif stage == 2:
            stats = sweep(2, ks, vs, lambda k: near_seen(k + 1), stats)
        else:
            stats = sweep(1, ks, vs, lambda k: near_seen(3), stats)

        for half in range(2):
            lanes = slice(half * HALF, (half + 1) * HALF)
            if stage == 3:
                os[r, :, lanes] = (acc[r, :, lanes] / stats[half][1]).astype(BF16)
            else:
                stats_ref[r, 0:8, lanes] = jnp.broadcast_to(stats[half][0], (8, HALF))
                stats_ref[r, 8:16, lanes] = jnp.broadcast_to(stats[half][1], (8, HALF))
        return carry

    lax.fori_loop(0, 4, one_queries, 0)
    if stage == 3:
        for r in range(4):
            o_out[r][...] = os[r]


def pair_of(low, columns, h):
    return jnp.where(low, columns[:, h : h + 1], columns[:, h + 1 : h + 2])


def softplus(v):
    return jnp.maximum(v, 0.0) + jnp.log1p(jnp.exp(-jnp.abs(v)))


SPAN = slice(STATE_DIM, STATE_DIM + 8)
SPAN_LOW = slice(STATE_DIM + 8, STATE_DIM + 16)
HELD, SENT = STATE_DIM + 8, STATE_DIM + 16


def send_state(pay_ref, lanes, state, span):
    span_high = span.astype(BF16)
    pay_ref[0:STATE_DIM, lanes] = state.astype(BF16)
    pay_ref[STATE_DIM:SENT, lanes] = jnp.concatenate(
        [span_high.astype(F32), span - span_high.astype(F32)], axis=0
    ).astype(BF16)


def ssm_local_kernel(
    x_ref, write_t_ref, read_t_ref, step_t_ref, rate_ref, gain_ref, out_ref, total_ref, pay_ref, cum_ref
):
    heads = step_t_ref.shape[0]
    high = lax.Precision.HIGHEST
    row = lax.broadcasted_iota(jnp.int32, (TOK, TOK), 0)
    col = lax.broadcasted_iota(jnp.int32, (TOK, TOK), 1)
    rate = jnp.broadcast_to(-jnp.exp(rate_ref[...]) * LOG2E, (8, heads)).T[:, 0:1]
    step_t = softplus(step_t_ref[...])
    cum_t = jnp.dot(
        rate * step_t, jnp.where(row <= col, 1.0, 0.0), precision=high, preferred_element_type=F32
    )
    key_row = jnp.log2(step_t) - cum_t
    cum = cum_t.T
    step = step_t.T
    cum_ref[...] = cum
    last = cum[TOK - 1 : TOK, :]
    tail = jnp.exp2(last - cum) * step
    gain = gain_ref[...]

    near = lax.dot_general(
        read_t_ref[...], write_t_ref[...], (((0,), (0,)), ((), ())), preferred_element_type=F32
    )
    near = jnp.where(col <= row, near, 0.0)
    low = lax.broadcasted_iota(jnp.int32, (1, 128), 1) < SSM_DIM
    for h in range(0, heads, 2):
        lanes = slice(h * SSM_DIM, (h + 2) * SSM_DIM)
        x_pair = x_ref[:, lanes]
        x_f = x_pair.astype(F32)
        weighted = (x_f * pair_of(low, tail, h)).astype(BF16)
        state = jnp.dot(write_t_ref[...], weighted, preferred_element_type=F32)
        span = jnp.broadcast_to(pair_of(low, last, h), (8, 128))
        total_ref[0:STATE_DIM, lanes] = state
        total_ref[SPAN, lanes] = span
        send_state(pay_ref, lanes, state, span)
        for t in range(2):
            t_rows = slice(t * HALF, (t + 1) * HALF)
            both = []
            for k in range(2):
                total = None
                for s in range(t + 1):
                    s_rows = slice(s * HALF, (s + 1) * HALF)
                    weights = (
                        jnp.exp2(cum[t_rows, h + k : h + k + 1] + key_row[h + k : h + k + 1, s_rows])
                        * near[t_rows, s_rows]
                    )
                    part = jnp.dot(weights.astype(BF16), x_pair[s_rows, :], preferred_element_type=F32)
                    total = part if total is None else total + part
                both.append(total)
            out_ref[t_rows, lanes] = (
                jnp.where(low, both[0], both[1]) + pair_of(low, gain, h) * x_f[t_rows, :]
            )


def ssm_merge_kernel(level, info, got_ref, total_ref, before_ref, total_out, before_out, pay_ref):
    later = ((info[3] >> level) & 1).astype(F32)
    got = got_ref[0:STATE_DIM, :].astype(F32)
    got_span = got_ref[STATE_DIM:SENT, :].astype(F32)
    got_span = got_span[0:8, :] + got_span[8:16, :]
    total, total_span = total_ref[0:STATE_DIM, :], total_ref[SPAN, :]
    before, before_span = before_ref[0:STATE_DIM, :], before_ref[SPAN, :]
    before_out[0:STATE_DIM, :] = before + later * (got * jnp.exp2(before_span[0:1, :]))
    before_out[SPAN, :] = before_span + later * got_span
    after_got = got * jnp.exp2(total_span[0:1, :]) + total
    after_total = total * jnp.exp2(got_span[0:1, :]) + got
    total = later * after_got + (1.0 - later) * after_total
    span = total_span + got_span
    total_out[0:STATE_DIM, :] = total
    total_out[SPAN, :] = span
    send_state(pay_ref, slice(None), total, span)


def ssm_carry_kernel(state_ref, mixed_ref, cum_ref, read_t_ref, gate_ref, gated_ref, square_ref):
    heads = cum_ref.shape[1]
    state = state_ref[0:STATE_DIM, :]
    state_high = state.astype(BF16)
    state_low = (state - state_high.astype(F32)).astype(BF16)
    reach = jnp.exp2(cum_ref[...])
    read = read_t_ref[...].T
    low = lax.broadcasted_iota(jnp.int32, (1, 128), 1) < SSM_DIM
    squares = jnp.zeros((TOK, 128), F32)
    for h in range(0, heads, 2):
        lanes = slice(h * SSM_DIM, (h + 2) * SSM_DIM)
        carried = jnp.dot(read, state_high[:, lanes], preferred_element_type=F32)
        carried = carried + jnp.dot(read, state_low[:, lanes], preferred_element_type=F32)
        mixed = mixed_ref[:, lanes] + carried * pair_of(low, reach, h)
        gate = gate_ref[:, lanes].astype(F32)
        gated = mixed * (gate / (1.0 + jnp.exp(-gate)))
        gated_ref[:, lanes] = gated
        squares = squares + gated * gated
    square_ref[...] = jnp.sum(squares.T, axis=0, keepdims=True)


def vmem(count):
    return [pl.BlockSpec(memory_space=pltpu.VMEM)] * count


SMEM = pl.BlockSpec(memory_space=pltpu.SMEM)
ANY = pl.BlockSpec(memory_space=pl.ANY)


SMALL = pl.CostEstimate(flops=1000, bytes_accessed=1000, transcendentals=0)


def params(mib):
    return pltpu.CompilerParams(vmem_limit_bytes=mib * 1024 * 1024)


def shape(dims, kind):
    return jax.ShapeDtypeStruct(dims, kind)


def pack(info, query_rows, key_rows, value_rows):
    width = HEADS * ATT_DIM
    rows = [ATT_DIM, 2 * ATT_DIM] + [3 * ATT_DIM] * 3
    return pl.pallas_call(
        pack_kernel,
        out_shape=[shape((count, TOK), BF16) for count in rows],
        in_specs=[SMEM] + [ANY] * 3,
        out_specs=vmem(len(rows)),
        scratch_shapes=[
            pltpu.VMEM((3, TOK, width), BF16),
            pltpu.VMEM((3, width, TOK), BF16),
            pltpu.SemaphoreType.DMA((3,)),
        ],
        compiler_params=params(60),
    )(info, query_rows, key_rows, value_rows)


def attend(stage, info, *operands):
    slots = (4, 1, 2, 1)[stage]
    keys, values = (slots, 2 * TOK, ATT_DIM), (slots, ATT_DIM, 2 * TOK)
    state = [shape((4, ATT_DIM, TOK), F32), shape((4, 16, TOK), F32)]
    queries = pltpu.VMEM((4, ATT_DIM, TOK), BF16)
    mark = [shape((8, 128), F32)]
    if stage == 0:
        out = state + [shape(keys, BF16), shape(values, BF16)] + mark
        scratch = [queries]
    elif stage < 3:
        out = state + mark
        scratch = [pltpu.VMEM(keys, BF16), pltpu.VMEM(values, BF16), queries]
    else:
        out = [shape((ATT_DIM, TOK), BF16)] * 4 + mark
        scratch = [pltpu.VMEM(keys, BF16), pltpu.VMEM(values, BF16), queries]
        scratch += [pltpu.VMEM((4, ATT_DIM, TOK), F32), queries]
    return pl.pallas_call(
        functools.partial(attend_kernel, stage),
        out_shape=out,
        in_specs=[SMEM] + vmem(len(operands)),
        out_specs=vmem(len(out)),
        scratch_shapes=scratch,
        compiler_params=params(24),
        cost_estimate=SMALL,
    )(info, *operands)


def unpack(info, mark, pieces):
    width = HEADS * ATT_DIM
    return pl.pallas_call(
        unpack_kernel,
        out_shape=shape((TOK, width), BF16),
        in_specs=[SMEM, ANY] + vmem(4),
        out_specs=vmem(1)[0],
        scratch_shapes=[pltpu.VMEM((width, TOK), BF16)],
        compiler_params=params(40),
    )(info, mark, *pieces)


def ssm_local(ssm_inputs, write_t, read_t, step_t, rate, gain):
    tokens, width = ssm_inputs.shape
    heads = step_t.shape[0]
    return pl.pallas_call(
        ssm_local_kernel,
        out_shape=[
            shape((tokens, width), F32),
            shape((HELD, width), F32),
            shape((SENT, width), BF16),
            shape((tokens, heads), F32),
        ],
        in_specs=vmem(6),
        out_specs=vmem(4),
        compiler_params=params(40),
        cost_estimate=SMALL,
    )(ssm_inputs, write_t, read_t, step_t, rate, gain)


def ssm_merge(level, info, got, total, before):
    held, sent = shape(total.shape, F32), shape(got.shape, BF16)
    return pl.pallas_call(
        functools.partial(ssm_merge_kernel, level),
        out_shape=[held, held, sent],
        in_specs=[SMEM] + vmem(3),
        out_specs=vmem(3),
        compiler_params=params(40),
        cost_estimate=SMALL,
    )(info, got, total, before)


def ssm_carry(state, mixed, cum, read_t, gate):
    tokens, width = mixed.shape
    return pl.pallas_call(
        ssm_carry_kernel,
        out_shape=[shape((tokens, width), F32), shape((1, tokens), F32)],
        in_specs=vmem(5),
        out_specs=vmem(2),
        compiler_params=params(40),
        cost_estimate=SMALL,
    )(state, mixed, cum, read_t, gate)


def on_device(
    query_rows,
    key_rows,
    value_rows,
    ssm_inputs,
    ssm_gate,
    write_vecs,
    read_vecs,
    step_raw,
    decay_log,
    skip_gain,
    norm_gain,
):
    me = lax.axis_index("ctx")
    y, x, core = me >> 3, (me >> 1) & 3, me & 1
    info = jnp.stack([y * 2 + (x >> 1), (x ^ (x >> 1)) & 1, core, me]).astype(jnp.int32)
    tie = lax.optimization_barrier

    q_own, kv_own, all_1, all_2, all_3 = pack(info, query_rows, key_rows, value_rows)
    here, near, from_core, near_core = [None] * 4, [None] * 4, [None] * 4, [None] * 4
    here[1], here[2] = head_swap(all_1, 1), head_swap(all_2, 2)
    near[0] = class_swap(kv_own)
    from_core[0] = core_swap(kv_own)

    from_core[0], ssm_inputs = tie((from_core[0], ssm_inputs))
    read_t = read_vecs.T
    mixed, total, sent, cum = ssm_local(
        ssm_inputs, write_vecs.T, read_t, step_raw.T, decay_log[None, :], skip_gain[None, :]
    )
    before = jnp.zeros_like(total)
    total, before, sent = ssm_merge(0, info, core_swap(sent), total, before)
    got = class_swap(sent)

    near[0], sent = tie((near[0], sent))
    near_core[0] = core_swap(near[0])

    here[1], here[2], near_core[0], all_3, got = tie((here[1], here[2], near_core[0], all_3, got))
    kv = [piece[ATT_DIM:] for piece in here[1:3]]
    near[1], near[2] = class_swap(kv[0]), class_swap(kv[1])
    here[3] = head_swap(all_3, 3)
    total, before, sent = ssm_merge(1, info, got, total, before)
    *kv, sent = tie((*kv, sent))
    from_core[1], from_core[2] = core_swap(kv[0]), core_swap(kv[1])
    from_core[1], from_core[2], sent = tie((from_core[1], from_core[2], sent))
    got = block_swap(sent, 4)
    *state, ks, vs, mark = attend(
        0, info, q_own, here[1], here[2], kv_own, *from_core[:3], near[0], near_core[0]
    )

    here[3], mark = tie((here[3], mark))
    kv = here[3][ATT_DIM:]
    from_core[3] = (core_swap(here[3][K_ROWS]), core_swap(here[3][V_ROWS]))
    queries = (q_own, here[1], here[2], here[3])
    *state, mark = attend(1, info, *queries, *from_core[3], mark, ks, vs, *state)

    near[1], near[2], mark = tie((near[1], near[2], mark))
    near_core[1], near_core[2] = core_swap(near[1]), core_swap(near[2])
    kv, got = tie((kv, got))
    near[3] = class_swap(kv)
    total, before, sent = ssm_merge(2, info, got, total, before)
    sent, mark = tie((sent, mark))
    got = block_swap(sent, 8)
    *state, mark = attend(2, info, *queries, near[1], near_core[1], near[2], near_core[2], mark, *state)

    got, mark = tie((got, mark))
    total, before, sent = ssm_merge(3, info, got, total, before)
    gated, squares = ssm_carry(before, mixed, cum, read_t, ssm_gate)
    near[3], gated, squares, mark = tie((near[3], gated, squares, mark))
    near_core[3] = core_swap(near[3])
    squares = squares + step_swap(squares, 4)
    near_core[3], squares = tie((near_core[3], squares))
    *results, mark = attend(3, info, *queries, near[3], near_core[3], mark, *state)
    back = [results[0]] + [head_swap(results[r], r) for r in range(1, 4)]
    squares, mark = tie((squares, mark))
    for step in (1, 2):
        squares = squares + step_swap(squares, step)
    *back, squares = tie((*back, squares))
    factor = lax.rsqrt(squares.reshape(TOK) / SSM_WIDTH + 1e-05)
    mixer_out = (gated * factor[:, None] * norm_gain[None, :]).astype(BF16)
    return (unpack(info, mark, back), mixer_out)


def solution(mesh):
    placed = (
        P("ctx", "tp"),
        P("ctx", "tp"),
        P("ctx", "tp"),
        P("ctx", "tp"),
        P("ctx", "tp"),
        P("ctx", None),
        P("ctx", None),
        P("ctx", "tp"),
        P("tp"),
        P("tp"),
        P("tp"),
    )
    return jax.shard_map(
        on_device,
        mesh=mesh,
        in_specs=placed,
        out_specs=(P("ctx", "tp"), P("ctx", "tp")),
        check_vma=False,
    )
```

```python
import functools
import math

import jax
import jax.numpy as jnp
from jax import lax
from jax.experimental import pallas as pl
from jax.experimental.pallas import tpu as pltpu
from jax.sharding import PartitionSpec as P

ATT_DIM = 224
SSM_DIM = 64
STATE_DIM = 64
SSM_WIDTH = 7168
TOK = 512
HEADS = 4
CTX = 16
HALF = 256
LOG2E = math.log2(math.e)
F32 = jnp.float32
BF16 = jnp.bfloat16


def exchanged(i, r):
    y, x, c = i >> 3, (i >> 1) & 3, i & 1
    if r & 1:
        x = 3 - x
    if r & 2:
        y = 1 - y
    return y * 8 + x * 2 + c


def head_swap(value, r):
    return lax.ppermute(value, "ctx", [(i, exchanged(i, r)) for i in range(CTX)])


def class_swap(value):
    return lax.ppermute(value, "ctx", [(i, i ^ 2) for i in range(CTX)])


def core_swap(value):
    return lax.ppermute(value, "ctx", [(i, i ^ 1) for i in range(CTX)])


def block_swap(value, step):
    return lax.ppermute(value, "ctx", [(i, i ^ step) for i in range(CTX)])


def step_swap(value, step):
    return lax.ppermute(value, "tp", [(i, i ^ step) for i in range(8)])


def head_rows(head):
    return pl.ds(pl.multiple_of(head * ATT_DIM, 16), ATT_DIM)


Q_ROWS = slice(0, ATT_DIM)
K_ROWS = slice(ATT_DIM, 2 * ATT_DIM)
V_ROWS = slice(2 * ATT_DIM, 3 * ATT_DIM)


def pack_kernel(info, q_in, k_in, v_in, q_own, kv_own, all_1, all_2, all_3, raw, rows_ref, sems):
    copies = [pltpu.make_async_copy(src, raw.at[i], sems.at[i]) for i, src in enumerate((q_in, k_in, v_in))]
    for copy in copies:
        copy.start()
    for i, (out, first) in enumerate(((q_own, 0), (kv_own, 0), (kv_own, ATT_DIM))):
        copies[i].wait()
        rows_ref[i] = raw[i].T
        out[first : first + ATT_DIM, :] = rows_ref[i, head_rows(info[0]), :]
        for r, away in ((1, all_1), (2, all_2), (3, all_3)):
            away[i * ATT_DIM : (i + 1) * ATT_DIM, :] = rows_ref[i, head_rows(info[0] ^ r), :]


def unpack_kernel(info, _, *refs):
    pieces, out_ref, rows_ref = refs[:4], refs[4], refs[5]
    for r in range(4):
        rows_ref[head_rows(info[0] ^ r), :] = pieces[r][...]
    out_ref[...] = rows_ref[...].T


def attend_kernel(stage, info, *refs):
    hid, kind, core = info[0], info[1], info[2]
    scale = ATT_DIM ** (-0.5) * LOG2E
    if stage == 0:
        q_in, (kv_own, core_0, core_1, core_2, near_0, near_core_0), refs = refs[:3], refs[3:9], refs[9:]
        acc, stats_ref, ks, vs, mark, qs = refs
        pieces = [(0, 0, kv_own, 0), (1, 0, q_in[1], ATT_DIM), (2, 0, q_in[2], ATT_DIM)]
        pieces += [(0, 1, core_0, 0), (1, 1, core_1, 0), (2, 1, core_2, 0)]
        pieces += [(3, 0, near_0, 0), (3, 1, near_core_0, 0)]
    elif stage == 1:
        q_in, (core_keys_3, core_values_3, _), refs = refs[:4], refs[4:7], refs[7:]
        ks_early, vs_early, acc_in, stats_in, acc, stats_ref, mark, ks, vs, qs = refs
        pieces = [(0, 0, q_in[3], ATT_DIM), (0, 1, (core_keys_3, core_values_3), 0)]
    elif stage == 2:
        q_in, (near_1, near_core_1, near_2, near_core_2, _), refs = refs[:4], refs[4:9], refs[9:]
        acc_in, stats_in, acc, stats_ref, mark, ks, vs, qs = refs
        pieces = [(0, 0, near_1, 0), (0, 1, near_core_1, 0), (1, 0, near_2, 0), (1, 1, near_core_2, 0)]
    else:
        q_in, (near_3, near_core_3, _), refs = refs[:4], refs[4:7], refs[7:]
        acc_in, stats_in, *o_out, mark, ks, vs, qs, acc, os = refs
        pieces = [(0, 0, near_3, 0), (0, 1, near_core_3, 0)]
    for slot, other, piece, first in pieces:
        start = pl.multiple_of((core ^ other) * TOK, TOK)
        if isinstance(piece, tuple):
            ks[slot, pl.ds(start, TOK), :] = piece[0][...].T
            vs[slot, :, pl.ds(start, TOK)] = piece[1][...]
            continue
        ks[slot, pl.ds(start, TOK), :] = piece[first : first + ATT_DIM, :].T
        vs[slot, :, pl.ds(start, TOK)] = piece[first + ATT_DIM : first + 2 * ATT_DIM, :]
    for r, queries in enumerate(q_in):
        qs[r] = queries[Q_ROWS, :]
    mark[...] = jnp.zeros_like(mark)

    def one_queries(r, carry):
        chip = hid ^ r

        def visit(keys, values, stats, masked):
            lanes = [slice(half * HALF, (half + 1) * HALF) for half in range(2)]
            scores = [
                jnp.dot(keys, qs[r, :, lanes[half]], preferred_element_type=F32) for half in range(2)
            ]
            new_stats = []
            for half in range(2):
                (top, total), s = stats[half], scores[half]
                if masked:
                    k_pos = lax.broadcasted_iota(jnp.int32, s.shape, 0)
                    q_pos = lax.broadcasted_iota(jnp.int32, s.shape, 1) + half * HALF
                    s = jnp.where(k_pos <= q_pos, s, -1e30)
                new_top = jnp.maximum(top, jnp.max(s, axis=0, keepdims=True))
                p = jnp.exp2((s - new_top) * scale)
                shrink = jnp.exp2((top - new_top) * scale)
                total = total * shrink + jnp.sum(p, axis=0, keepdims=True)
                new_stats.append((new_top, total))
                acc[r, :, lanes[half]] = acc[r, :, lanes[half]] * shrink + jnp.dot(
                    values, p.astype(BF16), preferred_element_type=F32
                )
            return tuple(new_stats)

        def sweep(count, key_ref, value_ref, seen, stats):
            def one(k, now):
                times = jnp.where(seen(k), 1, 0)
                return lax.fori_loop(
                    0, times, lambda _, inner: visit(key_ref[k], value_ref[k], inner, False), now
                )

            return lax.fori_loop(0, count, one, stats)

        def near_seen(k):
            limit = jnp.where(kind == 0, ((chip + 1) >> 1) * 2, (chip >> 1) * 2 + 1)
            return (hid ^ k) < limit

        def diagonal(slot, stats):
            def part(start, now, masked):
                start = pl.multiple_of(start, TOK)
                return visit(ks[slot, pl.ds(start, TOK), :], vs[slot, :, pl.ds(start, TOK)], now, masked)

            stats = lax.fori_loop(0, core, lambda _, now: part(0, now, False), stats)
            return part(core * TOK, stats, True)

        if stage == 0:
            acc[r] = jnp.zeros((ATT_DIM, TOK), F32)
            first = (jnp.full((1, HALF), -1e30, F32), jnp.zeros((1, HALF), F32))
            stats = (first, first)
        else:
            acc[r] = acc_in[r]
            stats = tuple(
                (
                    stats_in[r, 0:1, half * HALF : (half + 1) * HALF],
                    stats_in[r, 8:9, half * HALF : (half + 1) * HALF],
                )
                for half in range(2)
            )

        if stage == 0:

            def early(now):
                now = sweep(4, ks, vs, lambda k: jnp.where(k == 3, near_seen(0), (hid ^ k) < chip), now)
                return diagonal(r, now)

            stats = lax.fori_loop(0, jnp.where(r == 3, 0, 1), lambda _, now: early(now), stats)
        elif stage == 1:
            last = jnp.where(r == 3, 1, 0)
            stats = sweep(
                4 * last, ks_early, vs_early, lambda k: jnp.where(k == 3, near_seen(0), (hid ^ k) < chip), stats
            )
            stats = sweep(1, ks, vs, lambda k: (hid ^ 3) < chip, stats)
            stats = lax.fori_loop(0, last, lambda _, now: diagonal(0, now), stats)
        elif stage == 2:
            stats = sweep(2, ks, vs, lambda k: near_seen(k + 1), stats)
        else:
            stats = sweep(1, ks, vs, lambda k: near_seen(3), stats)

        for half in range(2):
            lanes = slice(half * HALF, (half + 1) * HALF)
            if stage == 3:
                os[r, :, lanes] = (acc[r, :, lanes] / stats[half][1]).astype(BF16)
            else:
                stats_ref[r, 0:8, lanes] = jnp.broadcast_to(stats[half][0], (8, HALF))
                stats_ref[r, 8:16, lanes] = jnp.broadcast_to(stats[half][1], (8, HALF))
        return carry

    lax.fori_loop(0, 4, one_queries, 0)
    if stage == 3:
        for r in range(4):
            o_out[r][...] = os[r]


def pair_of(low, columns, h):
    return jnp.where(low, columns[:, h : h + 1], columns[:, h + 1 : h + 2])


def softplus(v):
    return jnp.maximum(v, 0.0) + jnp.log1p(jnp.exp(-jnp.abs(v)))


SPAN = slice(STATE_DIM, STATE_DIM + 8)
SPAN_LOW = slice(STATE_DIM + 8, STATE_DIM + 16)
HELD, SENT = STATE_DIM + 8, STATE_DIM + 16


def send_state(pay_ref, lanes, state, span):
    span_high = span.astype(BF16)
    pay_ref[0:STATE_DIM, lanes] = state.astype(BF16)
    pay_ref[STATE_DIM:SENT, lanes] = jnp.concatenate(
        [span_high.astype(F32), span - span_high.astype(F32)], axis=0
    ).astype(BF16)


def ssm_local_kernel(
    x_ref, write_t_ref, read_t_ref, step_t_ref, rate_ref, gain_ref, out_ref, total_ref, pay_ref, cum_ref
):
    heads = step_t_ref.shape[0]
    high = lax.Precision.HIGHEST
    row = lax.broadcasted_iota(jnp.int32, (TOK, TOK), 0)
    col = lax.broadcasted_iota(jnp.int32, (TOK, TOK), 1)
    rate = jnp.broadcast_to(-jnp.exp(rate_ref[...]) * LOG2E, (8, heads)).T[:, 0:1]
    step_t = softplus(step_t_ref[...])
    cum_t = jnp.dot(
        rate * step_t, jnp.where(row <= col, 1.0, 0.0), precision=high, preferred_element_type=F32
    )
    key_row = jnp.log2(step_t) - cum_t
    cum = cum_t.T
    step = step_t.T
    cum_ref[...] = cum
    last = cum[TOK - 1 : TOK, :]
    tail = jnp.exp2(last - cum) * step
    gain = gain_ref[...]

    near = lax.dot_general(
        read_t_ref[...], write_t_ref[...], (((0,), (0,)), ((), ())), preferred_element_type=F32
    )
    near = jnp.where(col <= row, near, 0.0)
    low = lax.broadcasted_iota(jnp.int32, (1, 128), 1) < SSM_DIM
    for h in range(0, heads, 2):
        lanes = slice(h * SSM_DIM, (h + 2) * SSM_DIM)
        x_pair = x_ref[:, lanes]
        x_f = x_pair.astype(F32)
        weighted = (x_f * pair_of(low, tail, h)).astype(BF16)
        state = jnp.dot(write_t_ref[...], weighted, preferred_element_type=F32)
        span = jnp.broadcast_to(pair_of(low, last, h), (8, 128))
        total_ref[0:STATE_DIM, lanes] = state
        total_ref[SPAN, lanes] = span
        send_state(pay_ref, lanes, state, span)
        for t in range(2):
            t_rows = slice(t * HALF, (t + 1) * HALF)
            both = []
            for k in range(2):
                total = None
                for s in range(t + 1):
                    s_rows = slice(s * HALF, (s + 1) * HALF)
                    weights = (
                        jnp.exp2(cum[t_rows, h + k : h + k + 1] + key_row[h + k : h + k + 1, s_rows])
                        * near[t_rows, s_rows]
                    )
                    part = jnp.dot(weights.astype(BF16), x_pair[s_rows, :], preferred_element_type=F32)
                    total = part if total is None else total + part
                both.append(total)
            out_ref[t_rows, lanes] = (
                jnp.where(low, both[0], both[1]) + pair_of(low, gain, h) * x_f[t_rows, :]
            )


def ssm_merge_kernel(level, info, got_ref, total_ref, before_ref, total_out, before_out, pay_ref):
    later = ((info[3] >> level) & 1).astype(F32)
    got = got_ref[0:STATE_DIM, :].astype(F32)
    got_span = got_ref[STATE_DIM:SENT, :].astype(F32)
    got_span = got_span[0:8, :] + got_span[8:16, :]
    total, total_span = total_ref[0:STATE_DIM, :], total_ref[SPAN, :]
    before, before_span = before_ref[0:STATE_DIM, :], before_ref[SPAN, :]
    before_out[0:STATE_DIM, :] = before + later * (got * jnp.exp2(before_span[0:1, :]))
    before_out[SPAN, :] = before_span + later * got_span
    after_got = got * jnp.exp2(total_span[0:1, :]) + total
    after_total = total * jnp.exp2(got_span[0:1, :]) + got
    total = later * after_got + (1.0 - later) * after_total
    span = total_span + got_span
    total_out[0:STATE_DIM, :] = total
    total_out[SPAN, :] = span
    send_state(pay_ref, slice(None), total, span)


def ssm_carry_kernel(state_ref, mixed_ref, cum_ref, read_t_ref, gate_ref, gated_ref, square_ref):
    heads = cum_ref.shape[1]
    state = state_ref[0:STATE_DIM, :]
    state_high = state.astype(BF16)
    state_low = (state - state_high.astype(F32)).astype(BF16)
    reach = jnp.exp2(cum_ref[...])
    read = read_t_ref[...].T
    low = lax.broadcasted_iota(jnp.int32, (1, 128), 1) < SSM_DIM
    squares = jnp.zeros((TOK, 128), F32)
    for h in range(0, heads, 2):
        lanes = slice(h * SSM_DIM, (h + 2) * SSM_DIM)
        carried = jnp.dot(read, state_high[:, lanes], preferred_element_type=F32)
        carried = carried + jnp.dot(read, state_low[:, lanes], preferred_element_type=F32)
        mixed = mixed_ref[:, lanes] + carried * pair_of(low, reach, h)
        gate = gate_ref[:, lanes].astype(F32)
        gated = mixed * (gate / (1.0 + jnp.exp(-gate)))
        gated_ref[:, lanes] = gated
        squares = squares + gated * gated
    square_ref[...] = jnp.sum(squares.T, axis=0, keepdims=True)


def vmem(count):
    return [pl.BlockSpec(memory_space=pltpu.VMEM)] * count


SMEM = pl.BlockSpec(memory_space=pltpu.SMEM)
ANY = pl.BlockSpec(memory_space=pl.ANY)


SMALL = pl.CostEstimate(flops=1000, bytes_accessed=1000, transcendentals=0)


def params(mib):
    return pltpu.CompilerParams(vmem_limit_bytes=mib * 1024 * 1024)


def shape(dims, kind):
    return jax.ShapeDtypeStruct(dims, kind)


def pack(info, query_rows, key_rows, value_rows):
    width = HEADS * ATT_DIM
    rows = [ATT_DIM, 2 * ATT_DIM] + [3 * ATT_DIM] * 3
    return pl.pallas_call(
        pack_kernel,
        out_shape=[shape((count, TOK), BF16) for count in rows],
        in_specs=[SMEM] + [ANY] * 3,
        out_specs=vmem(len(rows)),
        scratch_shapes=[
            pltpu.VMEM((3, TOK, width), BF16),
            pltpu.VMEM((3, width, TOK), BF16),
            pltpu.SemaphoreType.DMA((3,)),
        ],
        compiler_params=params(60),
    )(info, query_rows, key_rows, value_rows)


def attend(stage, info, *operands):
    slots = (4, 1, 2, 1)[stage]
    keys, values = (slots, 2 * TOK, ATT_DIM), (slots, ATT_DIM, 2 * TOK)
    state = [shape((4, ATT_DIM, TOK), F32), shape((4, 16, TOK), F32)]
    queries = pltpu.VMEM((4, ATT_DIM, TOK), BF16)
    mark = [shape((8, 128), F32)]
    if stage == 0:
        out = state + [shape(keys, BF16), shape(values, BF16)] + mark
        scratch = [queries]
    elif stage < 3:
        out = state + mark
        scratch = [pltpu.VMEM(keys, BF16), pltpu.VMEM(values, BF16), queries]
    else:
        out = [shape((ATT_DIM, TOK), BF16)] * 4 + mark
        scratch = [pltpu.VMEM(keys, BF16), pltpu.VMEM(values, BF16), queries]
        scratch += [pltpu.VMEM((4, ATT_DIM, TOK), F32), queries]
    return pl.pallas_call(
        functools.partial(attend_kernel, stage),
        out_shape=out,
        in_specs=[SMEM] + vmem(len(operands)),
        out_specs=vmem(len(out)),
        scratch_shapes=scratch,
        compiler_params=params(24),
        cost_estimate=SMALL,
    )(info, *operands)


def unpack(info, mark, pieces):
    width = HEADS * ATT_DIM
    return pl.pallas_call(
        unpack_kernel,
        out_shape=shape((TOK, width), BF16),
        in_specs=[SMEM, ANY] + vmem(4),
        out_specs=vmem(1)[0],
        scratch_shapes=[pltpu.VMEM((width, TOK), BF16)],
        compiler_params=params(40),
    )(info, mark, *pieces)


def ssm_local(ssm_inputs, write_t, read_t, step_t, rate, gain):
    tokens, width = ssm_inputs.shape
    heads = step_t.shape[0]
    return pl.pallas_call(
        ssm_local_kernel,
        out_shape=[
            shape((tokens, width), F32),
            shape((HELD, width), F32),
            shape((SENT, width), BF16),
            shape((tokens, heads), F32),
        ],
        in_specs=vmem(6),
        out_specs=vmem(4),
        compiler_params=params(40),
        cost_estimate=SMALL,
    )(ssm_inputs, write_t, read_t, step_t, rate, gain)


def ssm_merge(level, info, got, total, before):
    held, sent = shape(total.shape, F32), shape(got.shape, BF16)
    return pl.pallas_call(
        functools.partial(ssm_merge_kernel, level),
        out_shape=[held, held, sent],
        in_specs=[SMEM] + vmem(3),
        out_specs=vmem(3),
        compiler_params=params(40),
        cost_estimate=SMALL,
    )(info, got, total, before)


def ssm_carry(state, mixed, cum, read_t, gate):
    tokens, width = mixed.shape
    return pl.pallas_call(
        ssm_carry_kernel,
        out_shape=[shape((tokens, width), F32), shape((1, tokens), F32)],
        in_specs=vmem(5),
        out_specs=vmem(2),
        compiler_params=params(40),
        cost_estimate=SMALL,
    )(state, mixed, cum, read_t, gate)


def on_device(
    query_rows,
    key_rows,
    value_rows,
    ssm_inputs,
    ssm_gate,
    write_vecs,
    read_vecs,
    step_raw,
    decay_log,
    skip_gain,
    norm_gain,
):
    me = lax.axis_index("ctx")
    y, x, core = me >> 3, (me >> 1) & 3, me & 1
    info = jnp.stack([y * 2 + (x >> 1), (x ^ (x >> 1)) & 1, core, me]).astype(jnp.int32)
    tie = lax.optimization_barrier

    q_own, kv_own, all_1, all_2, all_3 = pack(info, query_rows, key_rows, value_rows)
    here, near, from_core, near_core = [None] * 4, [None] * 4, [None] * 4, [None] * 4
    here[1], here[2] = head_swap(all_1, 1), head_swap(all_2, 2)
    near[0] = class_swap(kv_own)
    from_core[0] = core_swap(kv_own)

    from_core[0], ssm_inputs = tie((from_core[0], ssm_inputs))
    read_t = read_vecs.T
    mixed, total, sent, cum = ssm_local(
        ssm_inputs, write_vecs.T, read_t, step_raw.T, decay_log[None, :], skip_gain[None, :]
    )
    before = jnp.zeros_like(total)
    total, before, sent = ssm_merge(0, info, core_swap(sent), total, before)
    got = class_swap(sent)

    near[0], sent = tie((near[0], sent))
    near_core[0] = core_swap(near[0])

    here[1], here[2], near_core[0], all_3, got = tie((here[1], here[2], near_core[0], all_3, got))
    kv = [piece[ATT_DIM:] for piece in here[1:3]]
    near[1], near[2] = class_swap(kv[0]), class_swap(kv[1])
    here[3] = head_swap(all_3, 3)
    total, before, sent = ssm_merge(1, info, got, total, before)
    *kv, sent = tie((*kv, sent))
    from_core[1], from_core[2] = core_swap(kv[0]), core_swap(kv[1])
    from_core[1], from_core[2], sent = tie((from_core[1], from_core[2], sent))
    got = block_swap(sent, 4)
    *state, ks, vs, mark = attend(
        0, info, q_own, here[1], here[2], kv_own, *from_core[:3], near[0], near_core[0]
    )

    here[3], mark = tie((here[3], mark))
    kv = here[3][ATT_DIM:]
    from_core[3] = (core_swap(here[3][K_ROWS]), core_swap(here[3][V_ROWS]))
    queries = (q_own, here[1], here[2], here[3])
    *state, mark = attend(1, info, *queries, *from_core[3], mark, ks, vs, *state)

    near[1], near[2], mark = tie((near[1], near[2], mark))
    near_core[1], near_core[2] = core_swap(near[1]), core_swap(near[2])
    kv, got = tie((kv, got))
    near[3] = class_swap(kv)
    total, before, sent = ssm_merge(2, info, got, total, before)
    sent, mark = tie((sent, mark))
    got = block_swap(sent, 8)
    *state, mark = attend(2, info, *queries, near[1], near_core[1], near[2], near_core[2], mark, *state)

    got, mark = tie((got, mark))
    total, before, sent = ssm_merge(3, info, got, total, before)
    gated, squares = ssm_carry(before, mixed, cum, read_t, ssm_gate)
    near[3], gated, squares, mark = tie((near[3], gated, squares, mark))
    near_core[3] = core_swap(near[3])
    squares = squares + step_swap(squares, 4)
    near_core[3], squares = tie((near_core[3], squares))
    *results, mark = attend(3, info, *queries, near[3], near_core[3], mark, *state)
    back = [results[0]] + [head_swap(results[r], r) for r in range(1, 4)]
    squares, mark = tie((squares, mark))
    for step in (1, 2):
        squares = squares + step_swap(squares, step)
    *back, squares = tie((*back, squares))
    factor = lax.rsqrt(squares.reshape(TOK) / SSM_WIDTH + 1e-05)
    mixer_out = (gated * factor[:, None] * norm_gain[None, :]).astype(BF16)
    return (unpack(info, mark, back), mixer_out)


def solution(mesh):
    placed = (
        P("ctx", "tp"),
        P("ctx", "tp"),
        P("ctx", "tp"),
        P("ctx", "tp"),
        P("ctx", "tp"),
        P("ctx", None),
        P("ctx", None),
        P("ctx", "tp"),
        P("tp"),
        P("tp"),
        P("tp"),
    )
    return jax.shard_map(
        on_device,
        mesh=mesh,
        in_specs=placed,
        out_specs=(P("ctx", "tp"), P("ctx", "tp")),
        check_vma=False,
    )
```

```python
import functools
import math

import jax
import jax.numpy as jnp
from jax import lax
from jax.experimental import pallas as pl
from jax.experimental.pallas import tpu as pltpu
from jax.sharding import PartitionSpec as P

ATT_DIM = 224
SSM_DIM = 64
STATE_DIM = 64
SSM_WIDTH = 7168
TOK = 512
HEADS = 4
CTX = 16
VALUE_ROWS = ATT_DIM + 16
HALF = 256
LOG2E = math.log2(math.e)
F32 = jnp.float32
BF16 = jnp.bfloat16


def exchanged(i, r):
    y, x, c = i >> 3, (i >> 1) & 3, i & 1
    if r & 1:
        x = 3 - x
    if r & 2:
        y = 1 - y
    return y * 8 + x * 2 + c


def head_swap(value, r):
    return lax.ppermute(value, "ctx", [(i, exchanged(i, r)) for i in range(CTX)])


def class_swap(value):
    return lax.ppermute(value, "ctx", [(i, i ^ 2) for i in range(CTX)])


def core_swap(value):
    return lax.ppermute(value, "ctx", [(i, i ^ 1) for i in range(CTX)])


def block_swap(value, step):
    return lax.ppermute(value, "ctx", [(i, i ^ step) for i in range(CTX)])


def step_swap(value, step):
    return lax.ppermute(value, "tp", [(i, i ^ step) for i in range(8)])


def head_rows(head):
    return pl.ds(pl.multiple_of(head * ATT_DIM, 16), ATT_DIM)


Q_ROWS = slice(0, ATT_DIM)
K_ROWS = slice(ATT_DIM, 2 * ATT_DIM)
V_ROWS = slice(2 * ATT_DIM, 3 * ATT_DIM)


def pack_kernel(info, q_in, k_in, v_in, q_own, kv_own, all_1, all_2, all_3, raw, rows_ref, sems):
    copies = [pltpu.make_async_copy(src, raw.at[i], sems.at[i]) for i, src in enumerate((q_in, k_in, v_in))]
    for copy in copies:
        copy.start()
    for i, (out, first) in enumerate(((q_own, 0), (kv_own, 0), (kv_own, ATT_DIM))):
        copies[i].wait()
        rows_ref[i] = raw[i].T
        out[first : first + ATT_DIM, :] = rows_ref[i, head_rows(info[0]), :]
        for r, away in ((1, all_1), (2, all_2), (3, all_3)):
            away[i * ATT_DIM : (i + 1) * ATT_DIM, :] = rows_ref[i, head_rows(info[0] ^ r), :]


def unpack_kernel(info, _, *refs):
    pieces, out_ref, rows_ref = refs[:4], refs[4], refs[5]
    for r in range(4):
        rows_ref[head_rows(info[0] ^ r), :] = pieces[r][...]
    out_ref[...] = rows_ref[...].T


def attend_kernel(stage, info, *refs):
    hid, kind, core = info[0], info[1], info[2]
    scale = ATT_DIM ** (-0.5) * LOG2E
    if stage == 0:
        q_in, (kv_own, core_0, core_1, core_2, near_0, near_core_0), refs = refs[:3], refs[3:9], refs[9:]
        acc, stats_ref, ks, vs, mark, qs = refs
        pieces = [(0, 0, kv_own, 0), (1, 0, q_in[1], ATT_DIM), (2, 0, q_in[2], ATT_DIM)]
        pieces += [(0, 1, core_0, 0), (1, 1, core_1, 0), (2, 1, core_2, 0)]
        pieces += [(3, 0, near_0, 0), (3, 1, near_core_0, 0)]
    elif stage == 1:
        q_in, (core_keys_3, core_values_3, _), refs = refs[:4], refs[4:7], refs[7:]
        ks_early, vs_early, acc_in, stats_in, acc, stats_ref, mark, ks, vs, qs = refs
        pieces = [(0, 0, q_in[3], ATT_DIM), (0, 1, (core_keys_3, core_values_3), 0)]
    elif stage == 2:
        q_in, (near_1, near_core_1, near_2, near_core_2, _), refs = refs[:4], refs[4:9], refs[9:]
        acc_in, stats_in, acc, stats_ref, mark, ks, vs, qs = refs
        pieces = [(0, 0, near_1, 0), (0, 1, near_core_1, 0), (1, 0, near_2, 0), (1, 1, near_core_2, 0)]
    else:
        q_in, (near_3, near_core_3, _), refs = refs[:4], refs[4:7], refs[7:]
        acc_in, stats_in, *o_out, mark, ks, vs, qs, acc, os = refs
        pieces = [(0, 0, near_3, 0), (0, 1, near_core_3, 0)]
    for slot, other, piece, first in pieces:
        start = pl.multiple_of((core ^ other) * TOK, TOK)
        vs[slot, ATT_DIM:VALUE_ROWS, pl.ds(start, TOK)] = jnp.ones((VALUE_ROWS - ATT_DIM, TOK), BF16)
        if isinstance(piece, tuple):
            ks[slot, pl.ds(start, TOK), :] = piece[0][...].T
            vs[slot, 0:ATT_DIM, pl.ds(start, TOK)] = piece[1][...]
            continue
        ks[slot, pl.ds(start, TOK), :] = piece[first : first + ATT_DIM, :].T
        vs[slot, 0:ATT_DIM, pl.ds(start, TOK)] = piece[first + ATT_DIM : first + 2 * ATT_DIM, :]
    for r, queries in enumerate(q_in):
        qs[r] = queries[Q_ROWS, :]
    mark[...] = jnp.zeros_like(mark)

    def one_queries(r, carry):
        chip = hid ^ r

        def visit(keys, values, stats, masked):
            lanes = [slice(half * HALF, (half + 1) * HALF) for half in range(2)]
            scores = [
                jnp.dot(keys, qs[r, :, lanes[half]], preferred_element_type=F32) for half in range(2)
            ]
            new_stats, low, shrinks = [], [], []
            for half in range(2):
                top, s = stats[half], scores[half]
                if masked:
                    k_pos = lax.broadcasted_iota(jnp.int32, s.shape, 0)
                    q_pos = lax.broadcasted_iota(jnp.int32, s.shape, 1) + half * HALF
                    s = jnp.where(k_pos <= q_pos, s, -1e30)
                new_top = jnp.maximum(top, jnp.max(s, axis=0, keepdims=True))
                p = jnp.exp2((s - new_top) * scale)
                shrink = jnp.exp2((top - new_top) * scale)
                new_stats.append(new_top)
                low.append(p.astype(BF16))
                shrinks.append(shrink)
            for half in range(2):
                acc[r, :, lanes[half]] = acc[r, :, lanes[half]] * shrinks[half] + jnp.dot(
                    values, low[half], preferred_element_type=F32
                )
            return tuple(new_stats)

        def sweep(count, key_ref, value_ref, seen, stats):
            def one(k, now):
                times = jnp.where(seen(k), 1, 0)
                return lax.fori_loop(
                    0, times, lambda _, inner: visit(key_ref[k], value_ref[k], inner, False), now
                )

            return lax.fori_loop(0, count, one, stats)

        def near_seen(k):
            limit = jnp.where(kind == 0, ((chip + 1) >> 1) * 2, (chip >> 1) * 2 + 1)
            return (hid ^ k) < limit

        def diagonal(slot, stats):
            def part(start, now, masked):
                start = pl.multiple_of(start, TOK)
                return visit(ks[slot, pl.ds(start, TOK), :], vs[slot, :, pl.ds(start, TOK)], now, masked)

            stats = lax.fori_loop(0, core, lambda _, now: part(0, now, False), stats)
            return part(core * TOK, stats, True)

        if stage == 0:
            acc[r] = jnp.zeros((VALUE_ROWS, TOK), F32)
            first = jnp.full((1, HALF), -1e30, F32)
            stats = (first, first)
        else:
            acc[r] = acc_in[r]
            stats = tuple(stats_in[r, 0:1, half * HALF : (half + 1) * HALF] for half in range(2))

        if stage == 0:

            def early(now):
                now = sweep(4, ks, vs, lambda k: jnp.where(k == 3, near_seen(0), (hid ^ k) < chip), now)
                return diagonal(r, now)

            stats = lax.fori_loop(0, jnp.where(r == 3, 0, 1), lambda _, now: early(now), stats)
        elif stage == 1:
            last = jnp.where(r == 3, 1, 0)
            stats = sweep(
                4 * last, ks_early, vs_early, lambda k: jnp.where(k == 3, near_seen(0), (hid ^ k) < chip), stats
            )
            stats = sweep(1, ks, vs, lambda k: (hid ^ 3) < chip, stats)
            stats = lax.fori_loop(0, last, lambda _, now: diagonal(0, now), stats)
        elif stage == 2:
            stats = sweep(2, ks, vs, lambda k: near_seen(k + 1), stats)
        else:
            stats = sweep(1, ks, vs, lambda k: near_seen(3), stats)

        for half in range(2):
            lanes = slice(half * HALF, (half + 1) * HALF)
            if stage == 3:
                total = acc[r, ATT_DIM : ATT_DIM + 1, lanes]
                os[r, :, lanes] = (acc[r, 0:ATT_DIM, lanes] / total).astype(BF16)
            else:
                stats_ref[r, :, lanes] = jnp.broadcast_to(stats[half], (8, HALF))
        return carry

    lax.fori_loop(0, 4, one_queries, 0)
    if stage == 3:
        for r in range(4):
            o_out[r][...] = os[r]


def pair_of(low, columns, h):
    return jnp.where(low, columns[:, h : h + 1], columns[:, h + 1 : h + 2])


def softplus(v):
    return jnp.maximum(v, 0.0) + jnp.log1p(jnp.exp(-jnp.abs(v)))


SPAN = slice(STATE_DIM, STATE_DIM + 8)
SPAN_LOW = slice(STATE_DIM + 8, STATE_DIM + 16)
HELD, SENT = STATE_DIM + 8, STATE_DIM + 16


def send_state(pay_ref, lanes, state, span):
    span_high = span.astype(BF16)
    pay_ref[0:STATE_DIM, lanes] = state.astype(BF16)
    pay_ref[STATE_DIM:SENT, lanes] = jnp.concatenate(
        [span_high.astype(F32), span - span_high.astype(F32)], axis=0
    ).astype(BF16)


def ssm_local_kernel(
    x_ref, write_t_ref, read_t_ref, step_t_ref, rate_ref, gain_ref, out_ref, total_ref, pay_ref, cum_ref
):
    heads = step_t_ref.shape[0]
    high = lax.Precision.HIGHEST
    row = lax.broadcasted_iota(jnp.int32, (TOK, TOK), 0)
    col = lax.broadcasted_iota(jnp.int32, (TOK, TOK), 1)
    rate = jnp.broadcast_to(-jnp.exp(rate_ref[...]) * LOG2E, (8, heads)).T[:, 0:1]
    step_t = softplus(step_t_ref[...])
    cum_t = jnp.dot(
        rate * step_t, jnp.where(row <= col, 1.0, 0.0), precision=high, preferred_element_type=F32
    )
    key_row = jnp.log2(step_t) - cum_t
    cum = cum_t.T
    step = step_t.T
    cum_ref[...] = cum
    last = cum[TOK - 1 : TOK, :]
    tail = jnp.exp2(last - cum) * step
    gain = gain_ref[...]

    near = lax.dot_general(
        read_t_ref[...], write_t_ref[...], (((0,), (0,)), ((), ())), preferred_element_type=F32
    )
    near = jnp.where(col <= row, near, 0.0)
    low = lax.broadcasted_iota(jnp.int32, (1, 128), 1) < SSM_DIM
    for h in range(0, heads, 2):
        lanes = slice(h * SSM_DIM, (h + 2) * SSM_DIM)
        x_pair = x_ref[:, lanes]
        x_f = x_pair.astype(F32)
        weighted = (x_f * pair_of(low, tail, h)).astype(BF16)
        state = jnp.dot(write_t_ref[...], weighted, preferred_element_type=F32)
        span = jnp.broadcast_to(pair_of(low, last, h), (8, 128))
        total_ref[0:STATE_DIM, lanes] = state
        total_ref[SPAN, lanes] = span
        send_state(pay_ref, lanes, state, span)
        for t in range(2):
            t_rows = slice(t * HALF, (t + 1) * HALF)
            both = []
            for k in range(2):
                total = None
                for s in range(t + 1):
                    s_rows = slice(s * HALF, (s + 1) * HALF)
                    weights = (
                        jnp.exp2(cum[t_rows, h + k : h + k + 1] + key_row[h + k : h + k + 1, s_rows])
                        * near[t_rows, s_rows]
                    )
                    part = jnp.dot(weights.astype(BF16), x_pair[s_rows, :], preferred_element_type=F32)
                    total = part if total is None else total + part
                both.append(total)
            out_ref[t_rows, lanes] = (
                jnp.where(low, both[0], both[1]) + pair_of(low, gain, h) * x_f[t_rows, :]
            )


def ssm_merge_kernel(level, info, got_ref, total_ref, before_ref, total_out, before_out, pay_ref):
    later = ((info[3] >> level) & 1).astype(F32)
    got = got_ref[0:STATE_DIM, :].astype(F32)
    got_span = got_ref[STATE_DIM:SENT, :].astype(F32)
    got_span = got_span[0:8, :] + got_span[8:16, :]
    total, total_span = total_ref[0:STATE_DIM, :], total_ref[SPAN, :]
    before, before_span = before_ref[0:STATE_DIM, :], before_ref[SPAN, :]
    before_out[0:STATE_DIM, :] = before + later * (got * jnp.exp2(before_span[0:1, :]))
    before_out[SPAN, :] = before_span + later * got_span
    after_got = got * jnp.exp2(total_span[0:1, :]) + total
    after_total = total * jnp.exp2(got_span[0:1, :]) + got
    total = later * after_got + (1.0 - later) * after_total
    span = total_span + got_span
    total_out[0:STATE_DIM, :] = total
    total_out[SPAN, :] = span
    send_state(pay_ref, slice(None), total, span)


def ssm_carry_kernel(state_ref, mixed_ref, cum_ref, read_t_ref, gate_ref, gated_ref, square_ref):
    heads = cum_ref.shape[1]
    state = state_ref[0:STATE_DIM, :]
    state_high = state.astype(BF16)
    state_low = (state - state_high.astype(F32)).astype(BF16)
    reach = jnp.exp2(cum_ref[...])
    read = read_t_ref[...].T
    low = lax.broadcasted_iota(jnp.int32, (1, 128), 1) < SSM_DIM
    squares = jnp.zeros((TOK, 128), F32)
    for h in range(0, heads, 2):
        lanes = slice(h * SSM_DIM, (h + 2) * SSM_DIM)
        carried = jnp.dot(read, state_high[:, lanes], preferred_element_type=F32)
        carried = carried + jnp.dot(read, state_low[:, lanes], preferred_element_type=F32)
        mixed = mixed_ref[:, lanes] + carried * pair_of(low, reach, h)
        gate = gate_ref[:, lanes].astype(F32)
        gated = mixed * (gate / (1.0 + jnp.exp(-gate)))
        gated_ref[:, lanes] = gated
        squares = squares + gated * gated
    square_ref[...] = jnp.sum(squares.T, axis=0, keepdims=True)


def vmem(count):
    return [pl.BlockSpec(memory_space=pltpu.VMEM)] * count


SMEM = pl.BlockSpec(memory_space=pltpu.SMEM)
ANY = pl.BlockSpec(memory_space=pl.ANY)


SMALL = pl.CostEstimate(flops=1000, bytes_accessed=1000, transcendentals=0)


def params(mib):
    return pltpu.CompilerParams(vmem_limit_bytes=mib * 1024 * 1024)


def shape(dims, kind):
    return jax.ShapeDtypeStruct(dims, kind)


def pack(info, query_rows, key_rows, value_rows):
    width = HEADS * ATT_DIM
    rows = [ATT_DIM, 2 * ATT_DIM] + [3 * ATT_DIM] * 3
    return pl.pallas_call(
        pack_kernel,
        out_shape=[shape((count, TOK), BF16) for count in rows],
        in_specs=[SMEM] + [ANY] * 3,
        out_specs=vmem(len(rows)),
        scratch_shapes=[
            pltpu.VMEM((3, TOK, width), BF16),
            pltpu.VMEM((3, width, TOK), BF16),
            pltpu.SemaphoreType.DMA((3,)),
        ],
        compiler_params=params(60),
    )(info, query_rows, key_rows, value_rows)


def attend(stage, info, *operands):
    slots = (4, 1, 2, 1)[stage]
    keys, values = (slots, 2 * TOK, ATT_DIM), (slots, VALUE_ROWS, 2 * TOK)
    state = [shape((4, VALUE_ROWS, TOK), F32), shape((4, 8, TOK), F32)]
    queries = pltpu.VMEM((4, ATT_DIM, TOK), BF16)
    mark = [shape((8, 128), F32)]
    if stage == 0:
        out = state + [shape(keys, BF16), shape(values, BF16)] + mark
        scratch = [queries]
    elif stage < 3:
        out = state + mark
        scratch = [pltpu.VMEM(keys, BF16), pltpu.VMEM(values, BF16), queries]
    else:
        out = [shape((ATT_DIM, TOK), BF16)] * 4 + mark
        scratch = [pltpu.VMEM(keys, BF16), pltpu.VMEM(values, BF16), queries]
        scratch += [pltpu.VMEM((4, VALUE_ROWS, TOK), F32), queries]
    return pl.pallas_call(
        functools.partial(attend_kernel, stage),
        out_shape=out,
        in_specs=[SMEM] + vmem(len(operands)),
        out_specs=vmem(len(out)),
        scratch_shapes=scratch,
        compiler_params=params(24),
        cost_estimate=SMALL,
    )(info, *operands)


def unpack(info, mark, pieces):
    width = HEADS * ATT_DIM
    return pl.pallas_call(
        unpack_kernel,
        out_shape=shape((TOK, width), BF16),
        in_specs=[SMEM, ANY] + vmem(4),
        out_specs=vmem(1)[0],
        scratch_shapes=[pltpu.VMEM((width, TOK), BF16)],
        compiler_params=params(40),
    )(info, mark, *pieces)


def ssm_local(ssm_inputs, write_t, read_t, step_t, rate, gain):
    tokens, width = ssm_inputs.shape
    heads = step_t.shape[0]
    return pl.pallas_call(
        ssm_local_kernel,
        out_shape=[
            shape((tokens, width), F32),
            shape((HELD, width), F32),
            shape((SENT, width), BF16),
            shape((tokens, heads), F32),
        ],
        in_specs=vmem(6),
        out_specs=vmem(4),
        compiler_params=params(40),
        cost_estimate=SMALL,
    )(ssm_inputs, write_t, read_t, step_t, rate, gain)


def ssm_merge(level, info, got, total, before):
    held, sent = shape(total.shape, F32), shape(got.shape, BF16)
    return pl.pallas_call(
        functools.partial(ssm_merge_kernel, level),
        out_shape=[held, held, sent],
        in_specs=[SMEM] + vmem(3),
        out_specs=vmem(3),
        compiler_params=params(40),
        cost_estimate=SMALL,
    )(info, got, total, before)


def ssm_carry(state, mixed, cum, read_t, gate):
    tokens, width = mixed.shape
    return pl.pallas_call(
        ssm_carry_kernel,
        out_shape=[shape((tokens, width), F32), shape((1, tokens), F32)],
        in_specs=vmem(5),
        out_specs=vmem(2),
        compiler_params=params(40),
        cost_estimate=SMALL,
    )(state, mixed, cum, read_t, gate)


def on_device(
    query_rows,
    key_rows,
    value_rows,
    ssm_inputs,
    ssm_gate,
    write_vecs,
    read_vecs,
    step_raw,
    decay_log,
    skip_gain,
    norm_gain,
):
    me = lax.axis_index("ctx")
    y, x, core = me >> 3, (me >> 1) & 3, me & 1
    info = jnp.stack([y * 2 + (x >> 1), (x ^ (x >> 1)) & 1, core, me]).astype(jnp.int32)
    tie = lax.optimization_barrier

    q_own, kv_own, all_1, all_2, all_3 = pack(info, query_rows, key_rows, value_rows)
    here, near, from_core, near_core = [None] * 4, [None] * 4, [None] * 4, [None] * 4
    here[1], here[2] = head_swap(all_1, 1), head_swap(all_2, 2)
    near[0] = class_swap(kv_own)
    from_core[0] = core_swap(kv_own)

    from_core[0], ssm_inputs = tie((from_core[0], ssm_inputs))
    read_t = read_vecs.T
    mixed, total, sent, cum = ssm_local(
        ssm_inputs, write_vecs.T, read_t, step_raw.T, decay_log[None, :], skip_gain[None, :]
    )
    before = jnp.zeros_like(total)
    total, before, sent = ssm_merge(0, info, core_swap(sent), total, before)
    got = class_swap(sent)

    near[0], sent = tie((near[0], sent))
    near_core[0] = core_swap(near[0])

    here[1], here[2], near_core[0], all_3, got = tie((here[1], here[2], near_core[0], all_3, got))
    kv = [piece[ATT_DIM:] for piece in here[1:3]]
    near[1], near[2] = class_swap(kv[0]), class_swap(kv[1])
    here[3] = head_swap(all_3, 3)
    total, before, sent = ssm_merge(1, info, got, total, before)
    *kv, sent = tie((*kv, sent))
    from_core[1], from_core[2] = core_swap(kv[0]), core_swap(kv[1])
    from_core[1], from_core[2], sent = tie((from_core[1], from_core[2], sent))
    got = block_swap(sent, 4)
    *state, ks, vs, mark = attend(
        0, info, q_own, here[1], here[2], kv_own, *from_core[:3], near[0], near_core[0]
    )

    here[3], mark = tie((here[3], mark))
    kv = here[3][ATT_DIM:]
    from_core[3] = (core_swap(here[3][K_ROWS]), core_swap(here[3][V_ROWS]))
    queries = (q_own, here[1], here[2], here[3])
    *state, mark = attend(1, info, *queries, *from_core[3], mark, ks, vs, *state)

    near[1], near[2], mark = tie((near[1], near[2], mark))
    near_core[1], near_core[2] = core_swap(near[1]), core_swap(near[2])
    kv, got = tie((kv, got))
    near[3] = class_swap(kv)
    total, before, sent = ssm_merge(2, info, got, total, before)
    sent, mark = tie((sent, mark))
    got = block_swap(sent, 8)
    *state, mark = attend(2, info, *queries, near[1], near_core[1], near[2], near_core[2], mark, *state)

    got, mark = tie((got, mark))
    total, before, sent = ssm_merge(3, info, got, total, before)
    gated, squares = ssm_carry(before, mixed, cum, read_t, ssm_gate)
    near[3], gated, squares, mark = tie((near[3], gated, squares, mark))
    near_core[3] = core_swap(near[3])
    squares = squares + step_swap(squares, 4)
    near_core[3], squares = tie((near_core[3], squares))
    *results, mark = attend(3, info, *queries, near[3], near_core[3], mark, *state)
    back = [results[0]] + [head_swap(results[r], r) for r in range(1, 4)]
    squares, mark = tie((squares, mark))
    for step in (1, 2):
        squares = squares + step_swap(squares, step)
    *back, squares = tie((*back, squares))
    factor = lax.rsqrt(squares.reshape(TOK) / SSM_WIDTH + 1e-05)
    mixer_out = (gated * factor[:, None] * norm_gain[None, :]).astype(BF16)
    return (unpack(info, mark, back), mixer_out)


def solution(mesh):
    placed = (
        P("ctx", "tp"),
        P("ctx", "tp"),
        P("ctx", "tp"),
        P("ctx", "tp"),
        P("ctx", "tp"),
        P("ctx", None),
        P("ctx", None),
        P("ctx", "tp"),
        P("tp"),
        P("tp"),
        P("tp"),
    )
    return jax.shard_map(
        on_device,
        mesh=mesh,
        in_specs=placed,
        out_specs=(P("ctx", "tp"), P("ctx", "tp")),
        check_vma=False,
    )
```

```python
import functools
import math

import jax
import jax.numpy as jnp
from jax import lax
from jax.experimental import pallas as pl
from jax.experimental.pallas import tpu as pltpu
from jax.sharding import PartitionSpec as P

ATT_DIM = 224
SSM_DIM = 64
STATE_DIM = 64
SSM_WIDTH = 7168
TOK = 512
HEADS = 4
CTX = 16
HALF = 256
LOG2E = math.log2(math.e)
F32 = jnp.float32
BF16 = jnp.bfloat16


def exchanged(i, r):
    y, x, c = i >> 3, (i >> 1) & 3, i & 1
    if r & 1:
        x = 3 - x
    if r & 2:
        y = 1 - y
    return y * 8 + x * 2 + c


def head_swap(value, r):
    return lax.ppermute(value, "ctx", [(i, exchanged(i, r)) for i in range(CTX)])


def class_swap(value):
    return lax.ppermute(value, "ctx", [(i, i ^ 2) for i in range(CTX)])


def core_swap(value):
    return lax.ppermute(value, "ctx", [(i, i ^ 1) for i in range(CTX)])


def block_swap(value, step):
    return lax.ppermute(value, "ctx", [(i, i ^ step) for i in range(CTX)])


def step_swap(value, step):
    return lax.ppermute(value, "tp", [(i, i ^ step) for i in range(8)])


def head_rows(head):
    return pl.ds(pl.multiple_of(head * ATT_DIM, 16), ATT_DIM)


Q_ROWS = slice(0, ATT_DIM)
K_ROWS = slice(ATT_DIM, 2 * ATT_DIM)
V_ROWS = slice(2 * ATT_DIM, 3 * ATT_DIM)


def pack_kernel(info, q_in, k_in, v_in, q_own, kv_own, all_1, all_2, all_3, raw, rows_ref, sems):
    copies = [pltpu.make_async_copy(src, raw.at[i], sems.at[i]) for i, src in enumerate((q_in, k_in, v_in))]
    for copy in copies:
        copy.start()
    for i, (out, first) in enumerate(((q_own, 0), (kv_own, 0), (kv_own, ATT_DIM))):
        copies[i].wait()
        rows_ref[i] = raw[i].T
        out[first : first + ATT_DIM, :] = rows_ref[i, head_rows(info[0]), :]
        for r, away in ((1, all_1), (2, all_2), (3, all_3)):
            away[i * ATT_DIM : (i + 1) * ATT_DIM, :] = rows_ref[i, head_rows(info[0] ^ r), :]


def unpack_kernel(info, _, *refs):
    pieces, out_ref, rows_ref = refs[:4], refs[4], refs[5]
    for r in range(4):
        rows_ref[head_rows(info[0] ^ r), :] = pieces[r][...]
    out_ref[...] = rows_ref[...].T


def attend_kernel(stage, info, *refs):
    hid, kind, core = info[0], info[1], info[2]
    scale = ATT_DIM ** (-0.5) * LOG2E
    if stage == 0:
        q_in, (kv_own, core_0, core_1, core_2, near_0, near_core_0), refs = refs[:3], refs[3:9], refs[9:]
        acc, stats_ref, ks, vs, mark, qs = refs
        pieces = [(0, 0, kv_own, 0), (1, 0, q_in[1], ATT_DIM), (2, 0, q_in[2], ATT_DIM)]
        pieces += [(0, 1, core_0, 0), (1, 1, core_1, 0), (2, 1, core_2, 0)]
        pieces += [(3, 0, near_0, 0), (3, 1, near_core_0, 0)]
    elif stage == 1:
        q_in, (core_keys_3, core_values_3, _), refs = refs[:4], refs[4:7], refs[7:]
        ks_early, vs_early, acc_in, stats_in, acc, stats_ref, mark, ks, vs, qs = refs
        pieces = [(0, 0, q_in[3], ATT_DIM), (0, 1, (core_keys_3, core_values_3), 0)]
    elif stage == 2:
        q_in, (near_both, core_both, _), refs = refs[:4], refs[4:7], refs[7:]
        acc_in, stats_in, acc, stats_ref, mark, ks, vs, qs = refs
        pieces = [(k, other, ref, k * 2 * ATT_DIM) for other, ref in enumerate((near_both, core_both)) for k in range(2)]
    else:
        q_in, (near_3, near_core_3, _), refs = refs[:4], refs[4:7], refs[7:]
        acc_in, stats_in, *o_out, mark, ks, vs, qs, acc, os = refs
        pieces = [(0, 0, near_3, 0), (0, 1, near_core_3, 0)]
    for slot, other, piece, first in pieces:
        start = pl.multiple_of((core ^ other) * TOK, TOK)
        if isinstance(piece, tuple):
            ks[slot, pl.ds(start, TOK), :] = piece[0][...].T
            vs[slot, :, pl.ds(start, TOK)] = piece[1][...]
            continue
        ks[slot, pl.ds(start, TOK), :] = piece[first : first + ATT_DIM, :].T
        vs[slot, :, pl.ds(start, TOK)] = piece[first + ATT_DIM : first + 2 * ATT_DIM, :]
    for r, queries in enumerate(q_in):
        qs[r] = queries[Q_ROWS, :]
    mark[...] = jnp.zeros_like(mark)

    def one_queries(r, carry):
        chip = hid ^ r

        def visit(keys, values, stats, masked):
            lanes = [slice(half * HALF, (half + 1) * HALF) for half in range(2)]
            scores = [
                jnp.dot(keys, qs[r, :, lanes[half]], preferred_element_type=F32) for half in range(2)
            ]
            new_stats, low, shrinks = [], [], []
            for half in range(2):
                (top, total), s = stats[half], scores[half]
                if masked:
                    k_pos = lax.broadcasted_iota(jnp.int32, s.shape, 0)
                    q_pos = lax.broadcasted_iota(jnp.int32, s.shape, 1) + half * HALF
                    s = jnp.where(k_pos <= q_pos, s, -1e30)
                new_top = jnp.maximum(top, jnp.max(s, axis=0, keepdims=True))
                p = jnp.exp2((s - new_top) * scale)
                shrink = jnp.exp2((top - new_top) * scale)
                total = total * shrink + jnp.sum(p, axis=0, keepdims=True)
                new_stats.append((new_top, total))
                low.append(p.astype(BF16))
                shrinks.append(shrink)
            for half in range(2):
                acc[r, :, lanes[half]] = acc[r, :, lanes[half]] * shrinks[half] + jnp.dot(
                    values, low[half], preferred_element_type=F32
                )
            return tuple(new_stats)

        def sweep(count, key_ref, value_ref, seen, stats):
            def one(k, now):
                times = jnp.where(seen(k), 1, 0)
                return lax.fori_loop(
                    0, times, lambda _, inner: visit(key_ref[k], value_ref[k], inner, False), now
                )

            return lax.fori_loop(0, count, one, stats)

        def near_seen(k):
            limit = jnp.where(kind == 0, ((chip + 1) >> 1) * 2, (chip >> 1) * 2 + 1)
            return (hid ^ k) < limit

        def diagonal(slot, stats):
            def part(start, now, masked):
                start = pl.multiple_of(start, TOK)
                return visit(ks[slot, pl.ds(start, TOK), :], vs[slot, :, pl.ds(start, TOK)], now, masked)

            stats = lax.fori_loop(0, core, lambda _, now: part(0, now, False), stats)
            return part(core * TOK, stats, True)

        if stage == 0:
            acc[r] = jnp.zeros((ATT_DIM, TOK), F32)
            first = (jnp.full((1, HALF), -1e30, F32), jnp.zeros((1, HALF), F32))
            stats = (first, first)
        else:
            acc[r] = acc_in[r]
            stats = tuple(
                (
                    stats_in[r, 0:1, half * HALF : (half + 1) * HALF],
                    stats_in[r, 8:9, half * HALF : (half + 1) * HALF],
                )
                for half in range(2)
            )

        if stage == 0:

            def early(now):
                now = sweep(4, ks, vs, lambda k: jnp.where(k == 3, near_seen(0), (hid ^ k) < chip), now)
                return diagonal(r, now)

            stats = lax.fori_loop(0, jnp.where(r == 3, 0, 1), lambda _, now: early(now), stats)
        elif stage == 1:
            last = jnp.where(r == 3, 1, 0)
            stats = sweep(
                4 * last, ks_early, vs_early, lambda k: jnp.where(k == 3, near_seen(0), (hid ^ k) < chip), stats
            )
            stats = sweep(1, ks, vs, lambda k: (hid ^ 3) < chip, stats)
            stats = lax.fori_loop(0, last, lambda _, now: diagonal(0, now), stats)
        elif stage == 2:
            stats = sweep(2, ks, vs, lambda k: near_seen(k + 1), stats)
        else:
            stats = sweep(1, ks, vs, lambda k: near_seen(3), stats)

        for half in range(2):
            lanes = slice(half * HALF, (half + 1) * HALF)
            if stage == 3:
                os[r, :, lanes] = (acc[r, :, lanes] / stats[half][1]).astype(BF16)
            else:
                stats_ref[r, 0:8, lanes] = jnp.broadcast_to(stats[half][0], (8, HALF))
                stats_ref[r, 8:16, lanes] = jnp.broadcast_to(stats[half][1], (8, HALF))
        return carry

    lax.fori_loop(0, 4, one_queries, 0)
    if stage == 3:
        for r in range(4):
            o_out[r][...] = os[r]


def pair_of(low, columns, h):
    return jnp.where(low, columns[:, h : h + 1], columns[:, h + 1 : h + 2])


def softplus(v):
    return jnp.maximum(v, 0.0) + jnp.log1p(jnp.exp(-jnp.abs(v)))


SPAN = slice(STATE_DIM, STATE_DIM + 8)
SPAN_LOW = slice(STATE_DIM + 8, STATE_DIM + 16)
HELD, SENT = STATE_DIM + 8, STATE_DIM + 16


def send_state(pay_ref, lanes, state, span):
    span_high = span.astype(BF16)
    pay_ref[0:STATE_DIM, lanes] = state.astype(BF16)
    pay_ref[STATE_DIM:SENT, lanes] = jnp.concatenate(
        [span_high.astype(F32), span - span_high.astype(F32)], axis=0
    ).astype(BF16)


def ssm_local_kernel(
    x_ref, write_t_ref, read_t_ref, step_t_ref, rate_ref, gain_ref, out_ref, total_ref, pay_ref, cum_ref
):
    heads = step_t_ref.shape[0]
    high = lax.Precision.HIGHEST
    row = lax.broadcasted_iota(jnp.int32, (TOK, TOK), 0)
    col = lax.broadcasted_iota(jnp.int32, (TOK, TOK), 1)
    rate = jnp.broadcast_to(-jnp.exp(rate_ref[...]) * LOG2E, (8, heads)).T[:, 0:1]
    step_t = softplus(step_t_ref[...])
    cum_t = jnp.dot(
        rate * step_t, jnp.where(row <= col, 1.0, 0.0), precision=high, preferred_element_type=F32
    )
    key_row = jnp.log2(step_t) - cum_t
    cum = cum_t.T
    step = step_t.T
    cum_ref[...] = cum
    last = cum[TOK - 1 : TOK, :]
    tail = jnp.exp2(last - cum) * step
    gain = gain_ref[...]

    near = lax.dot_general(
        read_t_ref[...], write_t_ref[...], (((0,), (0,)), ((), ())), preferred_element_type=F32
    )
    near = jnp.where(col <= row, near, 0.0)
    low = lax.broadcasted_iota(jnp.int32, (1, 128), 1) < SSM_DIM
    for h in range(0, heads, 2):
        lanes = slice(h * SSM_DIM, (h + 2) * SSM_DIM)
        x_pair = x_ref[:, lanes]
        x_f = x_pair.astype(F32)
        weighted = (x_f * pair_of(low, tail, h)).astype(BF16)
        state = jnp.dot(write_t_ref[...], weighted, preferred_element_type=F32)
        span = jnp.broadcast_to(pair_of(low, last, h), (8, 128))
        total_ref[0:STATE_DIM, lanes] = state
        total_ref[SPAN, lanes] = span
        send_state(pay_ref, lanes, state, span)
        for t in range(2):
            t_rows = slice(t * HALF, (t + 1) * HALF)
            both = []
            for k in range(2):
                total = None
                for s in range(t + 1):
                    s_rows = slice(s * HALF, (s + 1) * HALF)
                    weights = (
                        jnp.exp2(cum[t_rows, h + k : h + k + 1] + key_row[h + k : h + k + 1, s_rows])
                        * near[t_rows, s_rows]
                    )
                    part = jnp.dot(weights.astype(BF16), x_pair[s_rows, :], preferred_element_type=F32)
                    total = part if total is None else total + part
                both.append(total)
            out_ref[t_rows, lanes] = (
                jnp.where(low, both[0], both[1]) + pair_of(low, gain, h) * x_f[t_rows, :]
            )


def ssm_merge_kernel(level, info, got_ref, total_ref, before_ref, total_out, before_out, pay_ref):
    later = ((info[3] >> level) & 1).astype(F32)
    got = got_ref[0:STATE_DIM, :].astype(F32)
    got_span = got_ref[STATE_DIM:SENT, :].astype(F32)
    got_span = got_span[0:8, :] + got_span[8:16, :]
    total, total_span = total_ref[0:STATE_DIM, :], total_ref[SPAN, :]
    before, before_span = before_ref[0:STATE_DIM, :], before_ref[SPAN, :]
    before_out[0:STATE_DIM, :] = before + later * (got * jnp.exp2(before_span[0:1, :]))
    before_out[SPAN, :] = before_span + later * got_span
    after_got = got * jnp.exp2(total_span[0:1, :]) + total
    after_total = total * jnp.exp2(got_span[0:1, :]) + got
    total = later * after_got + (1.0 - later) * after_total
    span = total_span + got_span
    total_out[0:STATE_DIM, :] = total
    total_out[SPAN, :] = span
    send_state(pay_ref, slice(None), total, span)


def ssm_carry_kernel(state_ref, mixed_ref, cum_ref, read_t_ref, gate_ref, gated_ref, square_ref):
    heads = cum_ref.shape[1]
    state = state_ref[0:STATE_DIM, :]
    state_high = state.astype(BF16)
    state_low = (state - state_high.astype(F32)).astype(BF16)
    reach = jnp.exp2(cum_ref[...])
    read = read_t_ref[...].T
    low = lax.broadcasted_iota(jnp.int32, (1, 128), 1) < SSM_DIM
    squares = jnp.zeros((TOK, 128), F32)
    for h in range(0, heads, 2):
        lanes = slice(h * SSM_DIM, (h + 2) * SSM_DIM)
        carried = jnp.dot(read, state_high[:, lanes], preferred_element_type=F32)
        carried = carried + jnp.dot(read, state_low[:, lanes], preferred_element_type=F32)
        mixed = mixed_ref[:, lanes] + carried * pair_of(low, reach, h)
        gate = gate_ref[:, lanes].astype(F32)
        gated = mixed * (gate / (1.0 + jnp.exp(-gate)))
        gated_ref[:, lanes] = gated
        squares = squares + gated * gated
    square_ref[...] = jnp.sum(squares.T, axis=0, keepdims=True)


def vmem(count):
    return [pl.BlockSpec(memory_space=pltpu.VMEM)] * count


SMEM = pl.BlockSpec(memory_space=pltpu.SMEM)
ANY = pl.BlockSpec(memory_space=pl.ANY)


SMALL = pl.CostEstimate(flops=1000, bytes_accessed=1000, transcendentals=0)


def params(mib):
    return pltpu.CompilerParams(vmem_limit_bytes=mib * 1024 * 1024)


def shape(dims, kind):
    return jax.ShapeDtypeStruct(dims, kind)


def pack(info, query_rows, key_rows, value_rows):
    width = HEADS * ATT_DIM
    rows = [ATT_DIM, 2 * ATT_DIM] + [3 * ATT_DIM] * 3
    return pl.pallas_call(
        pack_kernel,
        out_shape=[shape((count, TOK), BF16) for count in rows],
        in_specs=[SMEM] + [ANY] * 3,
        out_specs=vmem(len(rows)),
        scratch_shapes=[
            pltpu.VMEM((3, TOK, width), BF16),
            pltpu.VMEM((3, width, TOK), BF16),
            pltpu.SemaphoreType.DMA((3,)),
        ],
        compiler_params=params(60),
    )(info, query_rows, key_rows, value_rows)


def attend(stage, info, *operands):
    slots = (4, 1, 2, 1)[stage]
    keys, values = (slots, 2 * TOK, ATT_DIM), (slots, ATT_DIM, 2 * TOK)
    state = [shape((4, ATT_DIM, TOK), F32), shape((4, 16, TOK), F32)]
    queries = pltpu.VMEM((4, ATT_DIM, TOK), BF16)
    mark = [shape((8, 128), F32)]
    if stage == 0:
        out = state + [shape(keys, BF16), shape(values, BF16)] + mark
        scratch = [queries]
    elif stage < 3:
        out = state + mark
        scratch = [pltpu.VMEM(keys, BF16), pltpu.VMEM(values, BF16), queries]
    else:
        out = [shape((ATT_DIM, TOK), BF16)] * 4 + mark
        scratch = [pltpu.VMEM(keys, BF16), pltpu.VMEM(values, BF16), queries]
        scratch += [pltpu.VMEM((4, ATT_DIM, TOK), F32), queries]
    return pl.pallas_call(
        functools.partial(attend_kernel, stage),
        out_shape=out,
        in_specs=[SMEM] + vmem(len(operands)),
        out_specs=vmem(len(out)),
        scratch_shapes=scratch,
        compiler_params=params(24),
        cost_estimate=SMALL,
    )(info, *operands)


def unpack(info, mark, pieces):
    width = HEADS * ATT_DIM
    return pl.pallas_call(
        unpack_kernel,
        out_shape=shape((TOK, width), BF16),
        in_specs=[SMEM, ANY] + vmem(4),
        out_specs=vmem(1)[0],
        scratch_shapes=[pltpu.VMEM((width, TOK), BF16)],
        compiler_params=params(40),
    )(info, mark, *pieces)


def ssm_local(ssm_inputs, write_t, read_t, step_t, rate, gain):
    tokens, width = ssm_inputs.shape
    heads = step_t.shape[0]
    return pl.pallas_call(
        ssm_local_kernel,
        out_shape=[
            shape((tokens, width), F32),
            shape((HELD, width), F32),
            shape((SENT, width), BF16),
            shape((tokens, heads), F32),
        ],
        in_specs=vmem(6),
        out_specs=vmem(4),
        compiler_params=params(40),
        cost_estimate=SMALL,
    )(ssm_inputs, write_t, read_t, step_t, rate, gain)


def ssm_merge(level, info, got, total, before):
    held, sent = shape(total.shape, F32), shape(got.shape, BF16)
    return pl.pallas_call(
        functools.partial(ssm_merge_kernel, level),
        out_shape=[held, held, sent],
        in_specs=[SMEM] + vmem(3),
        out_specs=vmem(3),
        compiler_params=params(40),
        cost_estimate=SMALL,
    )(info, got, total, before)


def ssm_carry(state, mixed, cum, read_t, gate):
    tokens, width = mixed.shape
    return pl.pallas_call(
        ssm_carry_kernel,
        out_shape=[shape((tokens, width), F32), shape((1, tokens), F32)],
        in_specs=vmem(5),
        out_specs=vmem(2),
        compiler_params=params(40),
        cost_estimate=SMALL,
    )(state, mixed, cum, read_t, gate)


def on_device(
    query_rows,
    key_rows,
    value_rows,
    ssm_inputs,
    ssm_gate,
    write_vecs,
    read_vecs,
    step_raw,
    decay_log,
    skip_gain,
    norm_gain,
):
    me = lax.axis_index("ctx")
    y, x, core = me >> 3, (me >> 1) & 3, me & 1
    info = jnp.stack([y * 2 + (x >> 1), (x ^ (x >> 1)) & 1, core, me]).astype(jnp.int32)
    tie = lax.optimization_barrier

    q_own, kv_own, all_1, all_2, all_3 = pack(info, query_rows, key_rows, value_rows)
    here, near, from_core, near_core = [None] * 4, [None] * 4, [None] * 4, [None] * 4
    here[1], here[2] = head_swap(all_1, 1), head_swap(all_2, 2)
    near[0] = class_swap(kv_own)
    from_core[0] = core_swap(kv_own)

    from_core[0], ssm_inputs = tie((from_core[0], ssm_inputs))
    read_t = read_vecs.T
    mixed, total, sent, cum = ssm_local(
        ssm_inputs, write_vecs.T, read_t, step_raw.T, decay_log[None, :], skip_gain[None, :]
    )
    before = jnp.zeros_like(total)
    total, before, sent = ssm_merge(0, info, core_swap(sent), total, before)
    got = class_swap(sent)

    near[0], sent = tie((near[0], sent))
    near_core[0] = core_swap(near[0])

    here[1], here[2], near_core[0], all_3, got = tie((here[1], here[2], near_core[0], all_3, got))
    kv = [piece[ATT_DIM:] for piece in here[1:3]]
    near_both = class_swap(jnp.concatenate(kv, axis=0))
    here[3] = head_swap(all_3, 3)
    total, before, sent = ssm_merge(1, info, got, total, before)
    *kv, sent = tie((*kv, sent))
    from_core[1], from_core[2] = core_swap(kv[0]), core_swap(kv[1])
    from_core[1], from_core[2], sent = tie((from_core[1], from_core[2], sent))
    got = block_swap(sent, 4)
    *state, ks, vs, mark = attend(
        0, info, q_own, here[1], here[2], kv_own, *from_core[:3], near[0], near_core[0]
    )

    here[3], mark = tie((here[3], mark))
    kv = here[3][ATT_DIM:]
    from_core[3] = (core_swap(here[3][K_ROWS]), core_swap(here[3][V_ROWS]))
    queries = (q_own, here[1], here[2], here[3])
    *state, mark = attend(1, info, *queries, *from_core[3], mark, ks, vs, *state)

    near_both, got, mark = tie((near_both, got, mark))
    near_core_both = core_swap(near_both)
    kv, got = tie((kv, got))
    near[3] = class_swap(kv)
    total, before, sent = ssm_merge(2, info, got, total, before)
    sent, mark = tie((sent, mark))
    got = block_swap(sent, 8)
    *state, mark = attend(2, info, *queries, near_both, near_core_both, mark, *state)

    got, mark = tie((got, mark))
    total, before, sent = ssm_merge(3, info, got, total, before)
    gated, squares = ssm_carry(before, mixed, cum, read_t, ssm_gate)
    near[3], gated, squares, mark = tie((near[3], gated, squares, mark))
    near_core[3] = core_swap(near[3])
    squares = squares + step_swap(squares, 4)
    near_core[3], squares = tie((near_core[3], squares))
    *results, mark = attend(3, info, *queries, near[3], near_core[3], mark, *state)
    back = [results[0]] + [head_swap(results[r], r) for r in range(1, 4)]
    squares, mark = tie((squares, mark))
    for step in (1, 2):
        squares = squares + step_swap(squares, step)
    *back, squares = tie((*back, squares))
    factor = lax.rsqrt(squares.reshape(TOK) / SSM_WIDTH + 1e-05)
    mixer_out = (gated * factor[:, None] * norm_gain[None, :]).astype(BF16)
    return (unpack(info, mark, back), mixer_out)


def solution(mesh):
    placed = (
        P("ctx", "tp"),
        P("ctx", "tp"),
        P("ctx", "tp"),
        P("ctx", "tp"),
        P("ctx", "tp"),
        P("ctx", None),
        P("ctx", None),
        P("ctx", "tp"),
        P("tp"),
        P("tp"),
        P("tp"),
    )
    return jax.shard_map(
        on_device,
        mesh=mesh,
        in_specs=placed,
        out_specs=(P("ctx", "tp"), P("ctx", "tp")),
        check_vma=False,
    )
```
